32 devices in a mesh: section: 4 (over y, x), tm: 8 (over z, core).
Axes of the slice: x: 2, y: 2, z: 4, core: 2. Of those that a mesh axis runs over, the one named last changes fastest.
Arguments:
- signal: bfloat16 [4, 4096, 256], P(None, 'tm'), may hold values from -6 to 6
- skip_cot: bfloat16 [4, 4096, 256], P(None, 'tm'), may hold values from -6 to 6
- res_cot: bfloat16 [4, 4096, 256], P(None, 'tm'), may hold values from -6 to 6
- w_tap: bfloat16 [4, 256, 512], P('section'), may hold values from -0.25 to 0.25
- w_now: bfloat16 [4, 256, 512], P('section'), may hold values from -0.25 to 0.25
- w_res: bfloat16 [4, 256, 256], P('section'), may hold values from -0.375 to 0.375
- w_skip: bfloat16 [4, 256, 256], P('section'), may hold values from -0.375 to 0.375
Outputs:
- skip_total: bfloat16 [4, 4096, 256], P(None, 'tm')
- input_grads: bfloat16 [4, 4, 4096, 256], P('section', None, 'tm')
- grad_tap: float32 [4, 256, 512], P('section')
- grad_now: float32 [4, 256, 512], P('section')
- grad_res: float32 [4, 256, 256], P('section')
- grad_skip: float32 [4, 256, 256], P('section')
The draws below stay inside these ranges and needn't reach their ends.
All inputs are finite; a program needn't handle non-finite values.
Results may differ from the reference program's by a relative error of at most 0.01.
Values may be sent and summed in bfloat16 or wider, within the bound.
No kernel may reach another device: no remote copies, remote signals or barrier semaphores. Data moves between devices by JAX's collectives and lax.ppermute only.
A program may use at most 64 MiB of HBM per device.

```python
import math
import jax
import jax.numpy as jnp

C = 256
GATE = 512
SKIP = 256
B = 4
HALF = 256
LAYERS = 4
L = 4096
FIRST_DILATION = 2048


def levels(rng, extent, split, low, largest):
    gain, own = 1.0, jax.random.fold_in(rng, 6)
    for dim, shards_of in split:
        heights = jnp.exp(jax.random.uniform(jax.random.fold_in(own, dim), (shards_of,), jnp.float32, low / len(split), largest / len(split)))
        gain = gain * jnp.repeat(heights, extent[dim] // shards_of).reshape([-1 if axis == dim else 1 for axis in range(len(extent))])
    return gain


def gaussian(key, dims, spread, limit, shards=(), held_as=jnp.bfloat16):
    gain = levels(key, dims, shards, -0.22, 0.18) if shards else 1.0
    entries = jax.random.normal(key, dims, jnp.float32) * spread * gain
    return jnp.minimum(jnp.maximum(entries, -limit), limit).astype(held_as)


def setup_inputs(seed: int = 0) -> dict:
    key_of = jax.random.split(jax.random.key(seed), 8)
    signal = gaussian(key_of[0], (B, L, C), 1.0, 6.0, ((1, 8),))
    skip_cot = gaussian(key_of[1], (B, L, SKIP), 1.0, 6.0, ((1, 8),))
    res_cot = gaussian(key_of[2], (B, L, C), 1.0, 6.0, ((1, 8),))
    w_tap = gaussian(key_of[3], (LAYERS, C, GATE), (2 * C) ** -0.5, 0.25, ((0, 4),))
    w_now = gaussian(key_of[4], (LAYERS, C, GATE), (2 * C) ** -0.5, 0.25, ((0, 4),))
    w_res = gaussian(key_of[5], (LAYERS, HALF, C), HALF ** -0.5, 0.375, ((0, 4),))
    w_skip = gaussian(key_of[6], (LAYERS, HALF, SKIP), HALF ** -0.5, 0.375, ((0, 4),))
    return {"signal": signal, "skip_cot": skip_cot, "res_cot": res_cot, "w_tap": w_tap, "w_now": w_now, "w_res": w_res, "w_skip": w_skip}


def delayed_rows(values, dilation_offset):
    padded = jnp.pad(values, ((dilation_offset, 0), (0, 0)))
    return padded[:values.shape[0]]

def advanced_rows(values, dilation_offset):
    padded = jnp.pad(values, ((0, dilation_offset), (0, 0)))
    return padded[dilation_offset:]

def gate_parts(tapped, layer_in, tap_weight, now_weight):
    pre = jnp.dot(tapped, tap_weight, preferred_element_type=jnp.float32) + jnp.dot(layer_in, now_weight, preferred_element_type=jnp.float32)
    half_width = pre.shape[1] // 2
    return (jnp.tanh(pre[:, :half_width]), jax.nn.sigmoid(pre[:, half_width:]))

def reference(signal, skip_cot, res_cot, w_tap, w_now, w_res, w_skip):
    number, length, channels = signal.shape
    layers_total = w_tap.shape[0]
    streams = [signal[seq_index] for seq_index in range(number)]
    saved = []
    skip_running_sum = [jnp.zeros((length, w_skip.shape[2]), jnp.float32) for seq_index in range(number)]
    for layer_number in range(layers_total):
        dilation_offset = FIRST_DILATION * 2 ** layer_number
        saved.append(streams)
        new_streams = []
        for seq_index in range(number):
            layer_in = streams[seq_index]
            tapped = delayed_rows(layer_in, dilation_offset)
            tanh_part, sigmoid_part = gate_parts(tapped, layer_in, w_tap[layer_number], w_now[layer_number])
            gated = (tanh_part * sigmoid_part).astype(jnp.bfloat16)
            skip_running_sum[seq_index] = skip_running_sum[seq_index] + jnp.dot(gated, w_skip[layer_number], preferred_element_type=jnp.float32)
            new_streams.append((layer_in.astype(jnp.float32) + jnp.dot(gated, w_res[layer_number], preferred_element_type=jnp.float32)).astype(jnp.bfloat16))
        streams = new_streams
    skip_total = jnp.stack(skip_running_sum).astype(jnp.bfloat16)
    grad_scale = 1.0 / math.sqrt(number * length)
    grads_now = [res_cot[seq_index] for seq_index in range(number)]
    input_layers = [None] * layers_total
    tap_list = [None] * layers_total
    now_list = [None] * layers_total
    res_list = [None] * layers_total
    skip_list = [None] * layers_total
    for layer_number in reversed(range(layers_total)):
        dilation_offset = FIRST_DILATION * 2 ** layer_number
        grad_tap = jnp.zeros(w_tap.shape[1:], jnp.float32)
        grad_now = jnp.zeros(w_now.shape[1:], jnp.float32)
        grad_res = jnp.zeros(w_res.shape[1:], jnp.float32)
        grad_skip = jnp.zeros(w_skip.shape[1:], jnp.float32)
        new_grads = []
        for seq_index in range(number):
            layer_in = saved[layer_number][seq_index]
            grad_out = grads_now[seq_index]
            skip_grad = skip_cot[seq_index]
            tapped = delayed_rows(layer_in, dilation_offset)
            tanh_part, sigmoid_part = gate_parts(tapped, layer_in, w_tap[layer_number], w_now[layer_number])
            gated = (tanh_part * sigmoid_part).astype(jnp.bfloat16)
            grad_gated = jnp.dot(grad_out, w_res[layer_number].T, preferred_element_type=jnp.float32) + jnp.dot(skip_grad, w_skip[layer_number].T, preferred_element_type=jnp.float32)
            grad_pre = jnp.concatenate([grad_gated * sigmoid_part * (1.0 - tanh_part * tanh_part), grad_gated * tanh_part * sigmoid_part * (1.0 - sigmoid_part)], axis=1).astype(jnp.bfloat16)
            grad_tap = grad_tap + jnp.dot(tapped.T, grad_pre, preferred_element_type=jnp.float32)
            grad_now = grad_now + jnp.dot(layer_in.T, grad_pre, preferred_element_type=jnp.float32)
            grad_res = grad_res + jnp.dot(gated.T, grad_out, preferred_element_type=jnp.float32)
            grad_skip = grad_skip + jnp.dot(gated.T, skip_grad, preferred_element_type=jnp.float32)
            back_term = jnp.dot(grad_pre, w_tap[layer_number].T, preferred_element_type=jnp.float32).astype(jnp.bfloat16)
            grad_in = grad_out.astype(jnp.float32) + jnp.dot(grad_pre, w_now[layer_number].T, preferred_element_type=jnp.float32) + advanced_rows(back_term, dilation_offset).astype(jnp.float32)
            new_grads.append(grad_in.astype(jnp.bfloat16))
        grads_now = new_grads
        input_layers[layer_number] = jnp.stack(new_grads)
        tap_list[layer_number] = grad_tap * grad_scale
        now_list[layer_number] = grad_now * grad_scale
        res_list[layer_number] = grad_res * grad_scale
        skip_list[layer_number] = grad_skip * grad_scale
    return (skip_total, jnp.stack(input_layers), jnp.stack(tap_list), jnp.stack(now_list), jnp.stack(res_list), jnp.stack(skip_list))
```

```python
import functools
import math

import jax
import jax.numpy as jnp
from jax import lax
from jax.experimental import pallas as pl
from jax.experimental.pallas import tpu as pltpu
from jax.sharding import PartitionSpec as P

SPAN = 4


def passed_along(x, axis, by):
    size = lax.axis_size(axis)
    pairs = [(i, i + by) for i in range(size) if 0 <= i + by < size]
    return lax.ppermute(x, axis, pairs)


def flat_dot(left, right):
    result = jnp.dot(left.reshape(-1, left.shape[-1]), right, preferred_element_type=jnp.float32)
    return result.reshape(left.shape[:-1] + (right.shape[-1],))


def rows_spanning(left, right):
    return lax.dot_general(
        left.reshape(-1, left.shape[-1]),
        right.reshape(-1, right.shape[-1]),
        (((0,), (0,)), ((), ())),
        preferred_element_type=jnp.float32,
    )


def tap_rows(values, chosen, delayed):
    result = jnp.zeros_like(values)
    for layer_number, selected in chosen:
        if delayed:
            arrived = passed_along(values, "tm", SPAN << layer_number)
        else:
            arrived = passed_along(values, "tm", -(SPAN << layer_number))
        result = jnp.where(selected, arrived, result)
    return result


def gate_parts(tapped, layer_in, weights):
    pre = flat_dot(tapped, weights[0]) + flat_dot(layer_in, weights[1])
    half_width = pre.shape[-1] // 2
    return (jnp.tanh(pre[..., :half_width]), jax.nn.sigmoid(pre[..., half_width:]))


def layer_forward(layer_in, weights, chosen):
    tapped = tap_rows(layer_in, chosen, True)
    tanh_part, sigmoid_part = gate_parts(tapped, layer_in, weights)
    gated = (tanh_part * sigmoid_part).astype(jnp.bfloat16)
    stream_out = (layer_in.astype(jnp.float32) + flat_dot(gated, weights[2])).astype(jnp.bfloat16)
    return (tapped, stream_out, flat_dot(gated, weights[3]))


def layer_backward(layer_in, tapped, grad_out, skip_grad, weights, chosen):
    tanh_part, sigmoid_part = gate_parts(tapped, layer_in, weights)
    gated = (tanh_part * sigmoid_part).astype(jnp.bfloat16)
    grad_gated = flat_dot(grad_out, weights[2].T) + flat_dot(skip_grad, weights[3].T)
    grad_pre = jnp.concatenate(
        [
            grad_gated * sigmoid_part * (1.0 - tanh_part * tanh_part),
            grad_gated * tanh_part * sigmoid_part * (1.0 - sigmoid_part),
        ],
        axis=-1,
    ).astype(jnp.bfloat16)
    terms = (
        rows_spanning(tapped, grad_pre),
        rows_spanning(layer_in, grad_pre),
        rows_spanning(gated, grad_out),
        rows_spanning(gated, skip_grad),
    )
    back_term = flat_dot(grad_pre, weights[0].T).astype(jnp.bfloat16)
    arrived = tap_rows(back_term, chosen, False)
    grad_in = (
        grad_out.astype(jnp.float32)
        + flat_dot(grad_pre, weights[1].T)
        + arrived.astype(jnp.float32)
    )
    return (grad_in.astype(jnp.bfloat16), terms)


def keep_slot(holding_rows, micro_index, in_range, value):
    former = lax.dynamic_slice_in_dim(holding_rows, micro_index, 1, 0)
    return lax.dynamic_update_slice_in_dim(
        holding_rows, jnp.where(in_range, value, former), micro_index, 0
    )


def run_layers(signal, skip_cot, res_cot, w_tap, w_now, w_res, w_skip, section_index, sections):
    number, seq_rows, channels = signal.shape
    weights = (w_tap[0], w_now[0], w_res[0], w_skip[0])
    total_steps = number + sections - 1
    saved_in = jnp.zeros((number, seq_rows, channels), jnp.bfloat16)
    saved_tap = jnp.zeros((number, seq_rows, channels), jnp.bfloat16)
    skip_running_sum = jnp.zeros((number, seq_rows, w_skip.shape[2]), jnp.float32)
    received = jnp.zeros((1, seq_rows, channels), jnp.bfloat16)
    for moment in range(total_steps):
        chosen = [
            (layer_number, section_index == layer_number)
            for layer_number in range(sections)
            if 0 <= moment - layer_number < number
        ]
        position = moment - section_index
        in_range = (position >= 0) & (position < number)
        micro_index = jnp.clip(position, 0, number - 1)
        incoming = signal[min(moment, number - 1)][None]
        layer_in = jnp.where(section_index == 0, incoming, received)
        tapped, stream_out, skip_term = layer_forward(layer_in, weights, chosen)
        saved_in = keep_slot(saved_in, micro_index, in_range, layer_in)
        saved_tap = keep_slot(saved_tap, micro_index, in_range, tapped)
        skip_running_sum = keep_slot(skip_running_sum, micro_index, in_range, skip_term)
        if moment + 1 < total_steps:
            received = passed_along(stream_out, "section", 1)
    skip_total = lax.psum(skip_running_sum, "section").astype(jnp.bfloat16)
    partial_sums = [
        jnp.zeros(weights[0].shape, jnp.float32),
        jnp.zeros(weights[1].shape, jnp.float32),
        jnp.zeros(weights[2].shape, jnp.float32),
        jnp.zeros(weights[3].shape, jnp.float32),
    ]
    input_grads = jnp.zeros((number, seq_rows, channels), jnp.bfloat16)
    received = jnp.zeros((1, seq_rows, channels), jnp.bfloat16)
    for moment in range(total_steps):
        chosen = [
            (layer_number, section_index == layer_number)
            for layer_number in range(sections)
            if 0 <= moment - (sections - 1 - layer_number) < number
        ]
        position = moment - (sections - 1 - section_index)
        in_range = (position >= 0) & (position < number)
        micro_index = jnp.clip(position, 0, number - 1)
        top_grad = lax.dynamic_slice_in_dim(res_cot, micro_index, 1, 0)
        grad_out = jnp.where(section_index == sections - 1, top_grad, received)
        layer_in = lax.dynamic_slice_in_dim(saved_in, micro_index, 1, 0)
        tapped = lax.dynamic_slice_in_dim(saved_tap, micro_index, 1, 0)
        skip_grad = lax.dynamic_slice_in_dim(skip_cot, micro_index, 1, 0)
        grad_in, terms = layer_backward(layer_in, tapped, grad_out, skip_grad, weights, chosen)
        factor = in_range.astype(jnp.float32)
        partial_sums = [partial_sums[spot] + factor * terms[spot] for spot in range(4)]
        input_grads = keep_slot(input_grads, micro_index, in_range, grad_in)
        if moment + 1 < total_steps:
            received = passed_along(grad_in, "section", -1)
    return (skip_total, input_grads, tuple((part[None] for part in partial_sums)))


def pipelined_body(signal, skip_cot, res_cot, w_tap, w_now, w_res, w_skip):
    sections = lax.axis_size("section")
    shards = lax.axis_size("tm")
    section_index = lax.axis_index("section")
    number, seq_rows, channels = signal.shape
    skip_total, input_grads, partial_sums = run_layers(
        signal, skip_cot, res_cot, w_tap, w_now, w_res, w_skip, section_index, sections
    )
    summed = lax.psum((partial_sums[0], partial_sums[1], partial_sums[2], partial_sums[3]), "tm")
    grad_scale = 1.0 / math.sqrt(number * seq_rows * shards)
    return (
        skip_total,
        input_grads[None],
        summed[0] * grad_scale,
        summed[1] * grad_scale,
        summed[2] * grad_scale,
        summed[3] * grad_scale,
    )


def narrow_dot(left, right):
    return lax.dot_general(left, right, (((1,), (0,)), ((), ())), preferred_element_type=jnp.float32)


def rows_dot(left, right):
    return lax.dot_general(left, right, (((0,), (0,)), ((), ())), preferred_element_type=jnp.float32)


def stack_kernel(
    layers, section_ref, signal, tapped, skip_cot, res_cot, weights,
    skip_out, grad_out, back_out, sums,
    turned, h_all, gated_all, dz_all, g_all, tanh_all, sig_all,
):
    section = section_ref[0]
    seqs, seq_rows, channels = signal.shape
    half = channels
    now = slice(0, 2 * half)
    res = slice(2 * half, 2 * half + channels)
    skip = slice(2 * half + channels, 2 * half + 2 * channels)
    tap = slice(2 * half + 2 * channels, 4 * half + 2 * channels)
    first_slot = section

    @pl.when(pl.program_id(0) == 0)
    def _():
        sums[...] = jnp.zeros(sums.shape, jnp.float32)
        for k in range(layers):
            turned[k] = weights[jnp.bitwise_xor(k, section), :, : 4 * half].T
        turned[layers, : 2 * half] = weights[first_slot, :, tap].T

    places = [slice(i * seq_rows, (i + 1) * seq_rows) for i in range(seqs)]
    odd = jnp.bitwise_and(section, seqs - 1)
    tap_at = [jnp.bitwise_xor(i, odd) for i in range(seqs)]
    for i, rows in enumerate(places):
        h_all[0, rows] = signal[i]
        g_all[layers, rows] = res_cot[i]
    for k in range(layers):
        slot = jnp.bitwise_xor(k, section)
        for i, rows in enumerate(places):
            pre = narrow_dot(h_all[k, rows], weights[slot, :, now])
            if k == 0:
                pre = pre + narrow_dot(tapped[tap_at[i]], weights[first_slot, :, tap])
            tanh_part = jnp.tanh(pre[:, :half])
            sig_part = 0.5 * jnp.tanh(0.5 * pre[:, half:]) + 0.5
            tanh_all[k, rows] = tanh_part
            sig_all[k, rows] = sig_part
            gated_all[k, rows] = (tanh_part * sig_part).astype(jnp.bfloat16)
        if k + 1 < layers:
            for rows in places:
                stream = narrow_dot(gated_all[k, rows], weights[slot, :, res])
                h_all[k + 1, rows] = (h_all[k, rows].astype(jnp.float32) + stream).astype(jnp.bfloat16)
    for i, rows in enumerate(places):
        total = narrow_dot(gated_all[0, rows], weights[first_slot, :, skip])
        for k in range(1, layers):
            total = total + narrow_dot(gated_all[k, rows], weights[jnp.bitwise_xor(k, section), :, skip])
        skip_out[i] = total.astype(jnp.bfloat16)
    for k in reversed(range(layers)):
        for i, rows in enumerate(places):
            du = narrow_dot(g_all[k + 1, rows], turned[k, res]) + narrow_dot(skip_cot[i], turned[k, skip])
            tanh_part = tanh_all[k, rows]
            sig_part = sig_all[k, rows]
            scaled = du * sig_part
            dz_all[k, rows, :half] = (scaled * (1.0 - tanh_part * tanh_part)).astype(jnp.bfloat16)
            dz_all[k, rows, half:] = (scaled * (tanh_part * (1.0 - sig_part))).astype(jnp.bfloat16)
        for i, rows in enumerate(places):
            if k == 0:
                back_out[i] = narrow_dot(dz_all[0, rows], turned[layers, : 2 * half]).astype(jnp.bfloat16)
            below = narrow_dot(dz_all[k, rows], turned[k, now])
            g_all[k, rows] = (g_all[k + 1, rows].astype(jnp.float32) + below).astype(jnp.bfloat16)
    for i, rows in enumerate(places):
        grad_out[i] = g_all[section, rows]
        sums[:, : 2 * half] += rows_dot(tapped[tap_at[i]], dz_all[section, rows])
        sums[:, 2 * half : 4 * half] += rows_dot(h_all[section, rows], dz_all[section, rows])
        sums[:, 4 * half : 4 * half + channels] += rows_dot(gated_all[section, rows], g_all[section + 1, rows])
        sums[:, 4 * half + channels :] += rows_dot(gated_all[section, rows], skip_cot[i])


def layer_stack(section_index, signal, tapped, skip_cot, res_cot, weights):
    number, seq_rows, channels = signal.shape
    layers, _, width = weights.shape
    seqs = 2
    rows = seqs * seq_rows
    block = pl.BlockSpec((seqs, seq_rows, channels), lambda b, s: (b, 0, 0))
    tapped_block = pl.BlockSpec((seqs, seq_rows, channels), lambda b, s: (jnp.bitwise_xor(b, s[0] // seqs), 0, 0))
    whole = pl.BlockSpec(weights.shape, lambda b, s: (0, 0, 0))
    sums_shape = (channels, 6 * channels)
    stream = jax.ShapeDtypeStruct(signal.shape, jnp.bfloat16)
    return pl.pallas_call(
        functools.partial(stack_kernel, layers),
        grid_spec=pltpu.PrefetchScalarGridSpec(
            num_scalar_prefetch=1,
            grid=(number // seqs,),
            in_specs=[block, tapped_block, block, block, whole],
            out_specs=[block, block, block, pl.BlockSpec(sums_shape, lambda b, s: (0, 0))],
            scratch_shapes=[
                pltpu.VMEM((layers + 1, 4 * channels, channels), jnp.bfloat16),
                pltpu.VMEM((layers, rows, channels), jnp.bfloat16),
                pltpu.VMEM((layers, rows, channels), jnp.bfloat16),
                pltpu.VMEM((layers, rows, 2 * channels), jnp.bfloat16),
                pltpu.VMEM((layers + 1, rows, channels), jnp.bfloat16),
                pltpu.VMEM((layers, rows, channels), jnp.float32),
                pltpu.VMEM((layers, rows, channels), jnp.float32),
            ],
        ),
        out_shape=[stream, stream, stream, jax.ShapeDtypeStruct(sums_shape, jnp.float32)],
        compiler_params=pltpu.CompilerParams(vmem_limit_bytes=60 * 2**20),
        name="layer_stack",
    )(section_index.astype(jnp.int32).reshape(1), signal, tapped, skip_cot, res_cot, weights)


def swapped(x, axis, by):
    return lax.ppermute(x, axis, [(i, i ^ by) for i in range(lax.axis_size(axis))])


def gather_weights(w_tap, w_now, w_res, w_skip, sections, core):
    own = jnp.concatenate([w_now[0], w_res[0], w_skip[0], w_tap[0]], axis=1)
    half_rows = own.shape[0] // 2
    own_half = lax.dynamic_slice_in_dim(own, core * half_rows, half_rows, 0)
    mine = jnp.stack([swapped(own_half, "section", m) for m in range(1, sections)])
    other = swapped(mine, "tm", 1)
    low = jnp.where(core == 0, mine, other)
    high = jnp.where(core == 0, other, mine)
    return jnp.concatenate([own[None], jnp.concatenate([low, high], axis=1)])


def gather_tapped(signal, section_index, sections):
    part = lax.dynamic_index_in_dim(signal, section_index, 0, False)
    arrived = passed_along(part, "tm", SPAN)
    return jnp.stack([arrived] + [swapped(arrived, "section", m) for m in range(1, sections)])


def sum_over_shards(partial, core, place, places):
    rows, width = partial.shape
    halves = partial.reshape(2, rows // 2, width)
    sent = lax.dynamic_index_in_dim(halves, 1 - core, 0, False).astype(jnp.bfloat16)
    kept = lax.dynamic_index_in_dim(halves, core, 0, False)
    kept = kept + swapped(sent, "tm", 1).astype(jnp.float32)
    pieces = kept.reshape(places, rows // 2 // places, width)
    total = lax.dynamic_index_in_dim(pieces, place, 0, False)
    for m in range(1, places):
        sent = lax.dynamic_index_in_dim(pieces, place ^ m, 0, False).astype(jnp.bfloat16)
        total = total + swapped(sent, "tm", 2 * m).astype(jnp.float32)
    total = total.astype(jnp.bfloat16)
    by_distance = jnp.stack([total] + [swapped(total, "tm", 2 * m) for m in range(1, places)])
    half = jnp.concatenate([lax.dynamic_index_in_dim(by_distance, place ^ q, 0, False) for q in range(places)])
    other = swapped(half, "tm", 1)
    low = jnp.where(core == 0, half, other)
    high = jnp.where(core == 0, other, half)
    return jnp.concatenate([low, high]).astype(jnp.float32)


def stacked_body(signal, skip_cot, res_cot, w_tap, w_now, w_res, w_skip):
    sections = lax.axis_size("section")
    shards = lax.axis_size("tm")
    section_index = lax.axis_index("section")
    shard_index = lax.axis_index("tm")
    core = shard_index % 2
    place = shard_index // 2
    number, seq_rows, channels = signal.shape
    tapped = gather_tapped(signal, section_index, sections)
    weights = gather_weights(w_tap, w_now, w_res, w_skip, sections, core)
    skip_total, grads, back, sums = layer_stack(section_index, signal, tapped, skip_cot, res_cot, weights)
    arrived = jnp.stack(
        [
            lax.ppermute(back[j], ("section", "tm"), [(j * shards + t + SPAN, t) for t in range(shards - SPAN)])
            for j in range(number)
        ]
    )
    input_grads = (grads.astype(jnp.float32) + arrived.astype(jnp.float32)).astype(jnp.bfloat16)
    grad_scale = 1.0 / math.sqrt(number * seq_rows * shards)
    summed = sum_over_shards(sums, core, place, shards // 2) * grad_scale
    gate = 2 * channels
    grad_tap = jnp.where(section_index == 0, summed[:, :gate], 0.0)
    return (
        skip_total,
        input_grads[None],
        grad_tap[None],
        summed[None, :, gate : 2 * gate],
        summed[None, :, 2 * gate : 2 * gate + channels],
        summed[None, :, 2 * gate + channels :],
    )


def body(signal, skip_cot, res_cot, w_tap, w_now, w_res, w_skip):
    sections = lax.axis_size("section")
    shards = lax.axis_size("tm")
    number, seq_rows, channels = signal.shape
    one_live_tap = SPAN < shards <= 2 * SPAN
    square = w_res.shape[1:] == (channels, channels) and w_skip.shape[1:] == (channels, channels)
    if one_live_tap and square and number == sections and sections == 4 and shards == 8:
        return stacked_body(signal, skip_cot, res_cot, w_tap, w_now, w_res, w_skip)
    return pipelined_body(signal, skip_cot, res_cot, w_tap, w_now, w_res, w_skip)


def solution(mesh):
    in_specs = (
        P(None, "tm", None),
        P(None, "tm", None),
        P(None, "tm", None),
        P("section", None, None),
        P("section", None, None),
        P("section", None, None),
        P("section", None, None),
    )
    out_specs = (
        P(None, "tm", None),
        P("section", None, "tm", None),
        P("section", None, None),
        P("section", None, None),
        P("section", None, None),
        P("section", None, None),
    )
    return jax.shard_map(body, mesh=mesh, in_specs=in_specs, out_specs=out_specs, check_vma=False)
```

```python
import functools
import math

import jax
import jax.numpy as jnp
from jax import lax
from jax.experimental import pallas as pl
from jax.experimental.pallas import tpu as pltpu
from jax.sharding import PartitionSpec as P

SPAN = 4
FIRST_DILATION = 2048


def passed_along(x, axis, by):
    size = lax.axis_size(axis)
    pairs = [(i, i + by) for i in range(size) if 0 <= i + by < size]
    return lax.ppermute(x, axis, pairs)


def flat_dot(left, right):
    result = jnp.dot(left.reshape(-1, left.shape[-1]), right, preferred_element_type=jnp.float32)
    return result.reshape(left.shape[:-1] + (right.shape[-1],))


def rows_spanning(left, right):
    return lax.dot_general(
        left.reshape(-1, left.shape[-1]),
        right.reshape(-1, right.shape[-1]),
        (((0,), (0,)), ((), ())),
        preferred_element_type=jnp.float32,
    )


def tap_rows(values, chosen, delayed):
    result = jnp.zeros_like(values)
    for layer_number, selected in chosen:
        if delayed:
            arrived = passed_along(values, "tm", SPAN << layer_number)
        else:
            arrived = passed_along(values, "tm", -(SPAN << layer_number))
        result = jnp.where(selected, arrived, result)
    return result


def gate_parts(tapped, layer_in, weights):
    pre = flat_dot(tapped, weights[0]) + flat_dot(layer_in, weights[1])
    half_width = pre.shape[-1] // 2
    return (jnp.tanh(pre[..., :half_width]), jax.nn.sigmoid(pre[..., half_width:]))


def layer_forward(layer_in, weights, chosen):
    tapped = tap_rows(layer_in, chosen, True)
    tanh_part, sigmoid_part = gate_parts(tapped, layer_in, weights)
    gated = (tanh_part * sigmoid_part).astype(jnp.bfloat16)
    stream_out = (layer_in.astype(jnp.float32) + flat_dot(gated, weights[2])).astype(jnp.bfloat16)
    return (tapped, stream_out, flat_dot(gated, weights[3]))


def layer_backward(layer_in, tapped, grad_out, skip_grad, weights, chosen):
    tanh_part, sigmoid_part = gate_parts(tapped, layer_in, weights)
    gated = (tanh_part * sigmoid_part).astype(jnp.bfloat16)
    grad_gated = flat_dot(grad_out, weights[2].T) + flat_dot(skip_grad, weights[3].T)
    grad_pre = jnp.concatenate(
        [
            grad_gated * sigmoid_part * (1.0 - tanh_part * tanh_part),
            grad_gated * tanh_part * sigmoid_part * (1.0 - sigmoid_part),
        ],
        axis=-1,
    ).astype(jnp.bfloat16)
    terms = (
        rows_spanning(tapped, grad_pre),
        rows_spanning(layer_in, grad_pre),
        rows_spanning(gated, grad_out),
        rows_spanning(gated, skip_grad),
    )
    back_term = flat_dot(grad_pre, weights[0].T).astype(jnp.bfloat16)
    arrived = tap_rows(back_term, chosen, False)
    grad_in = (
        grad_out.astype(jnp.float32)
        + flat_dot(grad_pre, weights[1].T)
        + arrived.astype(jnp.float32)
    )
    return (grad_in.astype(jnp.bfloat16), terms)


def keep_slot(holding_rows, micro_index, in_range, value):
    former = lax.dynamic_slice_in_dim(holding_rows, micro_index, 1, 0)
    return lax.dynamic_update_slice_in_dim(
        holding_rows, jnp.where(in_range, value, former), micro_index, 0
    )


def run_layers(signal, skip_cot, res_cot, w_tap, w_now, w_res, w_skip, section_index, sections):
    number, seq_rows, channels = signal.shape
    weights = (w_tap[0], w_now[0], w_res[0], w_skip[0])
    total_steps = number + sections - 1
    saved_in = jnp.zeros((number, seq_rows, channels), jnp.bfloat16)
    saved_tap = jnp.zeros((number, seq_rows, channels), jnp.bfloat16)
    skip_running_sum = jnp.zeros((number, seq_rows, w_skip.shape[2]), jnp.float32)
    received = jnp.zeros((1, seq_rows, channels), jnp.bfloat16)
    for moment in range(total_steps):
        chosen = [
            (layer_number, section_index == layer_number)
            for layer_number in range(sections)
            if 0 <= moment - layer_number < number
        ]
        position = moment - section_index
        in_range = (position >= 0) & (position < number)
        micro_index = jnp.clip(position, 0, number - 1)
        incoming = signal[min(moment, number - 1)][None]
        layer_in = jnp.where(section_index == 0, incoming, received)
        tapped, stream_out, skip_term = layer_forward(layer_in, weights, chosen)
        saved_in = keep_slot(saved_in, micro_index, in_range, layer_in)
        saved_tap = keep_slot(saved_tap, micro_index, in_range, tapped)
        skip_running_sum = keep_slot(skip_running_sum, micro_index, in_range, skip_term)
        if moment + 1 < total_steps:
            received = passed_along(stream_out, "section", 1)
    skip_total = lax.psum(skip_running_sum, "section").astype(jnp.bfloat16)
    partial_sums = [
        jnp.zeros(weights[0].shape, jnp.float32),
        jnp.zeros(weights[1].shape, jnp.float32),
        jnp.zeros(weights[2].shape, jnp.float32),
        jnp.zeros(weights[3].shape, jnp.float32),
    ]
    input_grads = jnp.zeros((number, seq_rows, channels), jnp.bfloat16)
    received = jnp.zeros((1, seq_rows, channels), jnp.bfloat16)
    for moment in range(total_steps):
        chosen = [
            (layer_number, section_index == layer_number)
            for layer_number in range(sections)
            if 0 <= moment - (sections - 1 - layer_number) < number
        ]
        position = moment - (sections - 1 - section_index)
        in_range = (position >= 0) & (position < number)
        micro_index = jnp.clip(position, 0, number - 1)
        top_grad = lax.dynamic_slice_in_dim(res_cot, micro_index, 1, 0)
        grad_out = jnp.where(section_index == sections - 1, top_grad, received)
        layer_in = lax.dynamic_slice_in_dim(saved_in, micro_index, 1, 0)
        tapped = lax.dynamic_slice_in_dim(saved_tap, micro_index, 1, 0)
        skip_grad = lax.dynamic_slice_in_dim(skip_cot, micro_index, 1, 0)
        grad_in, terms = layer_backward(layer_in, tapped, grad_out, skip_grad, weights, chosen)
        factor = in_range.astype(jnp.float32)
        partial_sums = [partial_sums[spot] + factor * terms[spot] for spot in range(4)]
        input_grads = keep_slot(input_grads, micro_index, in_range, grad_in)
        if moment + 1 < total_steps:
            received = passed_along(grad_in, "section", -1)
    return (skip_total, input_grads, tuple((part[None] for part in partial_sums)))


def pipelined_body(signal, skip_cot, res_cot, w_tap, w_now, w_res, w_skip):
    sections = lax.axis_size("section")
    shards = lax.axis_size("tm")
    section_index = lax.axis_index("section")
    number, seq_rows, channels = signal.shape
    skip_total, input_grads, partial_sums = run_layers(
        signal, skip_cot, res_cot, w_tap, w_now, w_res, w_skip, section_index, sections
    )
    summed = lax.psum((partial_sums[0], partial_sums[1], partial_sums[2], partial_sums[3]), "tm")
    grad_scale = 1.0 / math.sqrt(number * seq_rows * shards)
    return (
        skip_total,
        input_grads[None],
        summed[0] * grad_scale,
        summed[1] * grad_scale,
        summed[2] * grad_scale,
        summed[3] * grad_scale,
    )


def narrow_dot(left, right):
    return lax.dot_general(left, right, (((1,), (0,)), ((), ())), preferred_element_type=jnp.float32)


def rows_dot(left, right):
    return lax.dot_general(left, right, (((0,), (0,)), ((), ())), preferred_element_type=jnp.float32)


def turned_dot(left, right):
    return lax.dot_general(left, right, (((1,), (1,)), ((), ())), preferred_element_type=jnp.float32)


def stack_kernel(layers, last, *refs):
    refs = list(refs)
    take = lambda count: [refs.pop(0) for _ in range(count)]
    signal, skip_cot, res_cot = take(3)
    taps = take(layers - 1 if last else 1)
    own = take(4)
    mine = take(layers - 1)
    other = take(layers - 1)
    if last:
        sums_in, _, _ = take(3)
        skip_out, grad_out, sent_out, kept_out = take(4)
    else:
        skip_out, grad_out, back_out, sums = take(4)
    weights, cot, tapped, h_all, gated_all, dz_all, g_all, tanh_all, sig_all, skip_total = take(10)
    weights_here, stream_here, tap_here, skip_gone, grad_gone = take(5)
    if last:
        sums, sums_here = take(2)
    section = lax.axis_index("section")
    core = lax.rem(lax.axis_index("tm"), 2)
    _, seqs, seq_rows, channels = h_all.shape
    half = channels
    now = slice(0, 2 * half)
    res = slice(2 * half, 2 * half + channels)
    skip = slice(2 * half + channels, 2 * half + 2 * channels)
    tap = slice(2 * half + 2 * channels, 4 * half + 2 * channels)
    low_rows = channels // 2
    these = [jnp.bitwise_xor(section, i + 1) if last else section for i in range(seqs)]

    def start_streams(source, target, there):
        for i in range(seqs):
            pltpu.make_async_copy(source.at[these[i]], target.at[i], there).start()

    def wait_streams(target, there):
        pltpu.make_async_copy(target, target, there).wait()

    start_streams(signal, h_all.at[0], stream_here.at[0])
    for ref, cols in zip(own, (now, res, skip, tap)):
        pltpu.make_async_copy(ref.at[0], weights.at[section, :, cols], weights_here.at[section]).start()
    for by in range(1, layers):
        slot = jnp.bitwise_xor(section, by)
        for ref, side in ((mine[by - 1], core), (other[by - 1], 1 - core)):
            rows = pl.ds(pl.multiple_of(side * low_rows, low_rows), low_rows)
            pltpu.make_async_copy(ref, weights.at[slot, rows], weights_here.at[slot]).start()
    for i, ref in enumerate(taps):
        pltpu.make_async_copy(ref, tapped.at[i], tap_here).start()
    start_streams(skip_cot, cot, stream_here.at[1])
    start_streams(res_cot, g_all.at[layers], stream_here.at[2])
    if last:
        sums_copy = pltpu.make_async_copy(sums_in, sums, sums_here)
        sums_copy.start()

    wait_streams(h_all.at[0], stream_here.at[0])
    for k in range(layers):
        pltpu.make_async_copy(weights.at[k], weights.at[k], weights_here.at[k]).wait()
        if k == 0:
            pltpu.make_async_copy(tapped, tapped, tap_here).wait()
        for i in range(seqs):
            pre = narrow_dot(h_all[k, i], weights[k, :, now])
            if k == 0:
                pre = pre + narrow_dot(tapped[i], weights[0, :, tap])
            tanh_part = jnp.tanh(pre[:, :half])
            sig_part = 0.5 * jnp.tanh(0.5 * pre[:, half:]) + 0.5
            tanh_all[k, i] = tanh_part
            sig_all[k, i] = sig_part
            gated_all[k, i] = (tanh_part * sig_part).astype(jnp.bfloat16)
        if k + 1 < layers:
            for i in range(seqs):
                stream = narrow_dot(gated_all[k, i], weights[k, :, res])
                h_all[k + 1, i] = (h_all[k, i].astype(jnp.float32) + stream).astype(jnp.bfloat16)
    wait_streams(cot, stream_here.at[1])
    wait_streams(g_all.at[layers], stream_here.at[2])
    for i in range(seqs):
        total = narrow_dot(gated_all[0, i], weights[0, :, skip])
        for k in range(1, layers):
            total = total + narrow_dot(gated_all[k, i], weights[k, :, skip])
        skip_total[i] = total.astype(jnp.bfloat16)
    for i in range(seqs):
        pltpu.make_async_copy(skip_total.at[i], skip_out.at[these[i]], skip_gone).start()
    for k in reversed(range(layers)):
        for i in range(seqs):
            du = turned_dot(g_all[k + 1, i], weights[k, :, res]) + turned_dot(cot[i], weights[k, :, skip])
            tanh_part = tanh_all[k, i]
            sig_part = sig_all[k, i]
            scaled = du * sig_part
            dz_all[k, i, :, :half] = (scaled * (1.0 - tanh_part * tanh_part)).astype(jnp.bfloat16)
            dz_all[k, i, :, half:] = (scaled * (tanh_part * (1.0 - sig_part))).astype(jnp.bfloat16)
        for i in range(seqs):
            below = turned_dot(dz_all[k, i], weights[k, :, now])
            g_all[k, i] = (g_all[k + 1, i].astype(jnp.float32) + below).astype(jnp.bfloat16)
    for i in range(seqs):
        pltpu.make_async_copy(g_all.at[section, i], grad_out.at[these[i]], grad_gone).start()
    if last:
        sums_copy.wait()
    else:
        back_out[...] = turned_dot(dz_all[0, 0], weights[0, :, tap]).astype(jnp.bfloat16)
    for i in range(seqs):
        products = (
            rows_dot(tapped[i], dz_all[section, i]),
            rows_dot(h_all[section, i], dz_all[section, i]),
            rows_dot(gated_all[section, i], g_all[section + 1, i]),
            rows_dot(gated_all[section, i], cot[i]),
        )
        spots = (slice(0, 2 * half), slice(2 * half, 4 * half), slice(4 * half, 4 * half + channels), slice(4 * half + channels, None))
        for spot, product in zip(spots, products):
            if i == 0 and not last:
                sums[:, spot] = product
            else:
                sums[:, spot] += product
    if last:
        kept_out[...] = sums[pl.ds(pl.multiple_of(core * low_rows, low_rows), low_rows)]
        sent_out[...] = sums[pl.ds(pl.multiple_of((1 - core) * low_rows, low_rows), low_rows)].astype(jnp.bfloat16)
    wait_streams(skip_total, skip_gone)
    wait_streams(cot, grad_gone)


def layer_stack(signal, skip_cot, res_cot, taps, own, mine, other, earlier=None):
    number, seq_rows, channels = signal.shape
    layers = len(mine) + 1
    seqs = len(taps)
    last = earlier is not None
    width = 6 * channels
    anywhere = pl.BlockSpec(memory_space=pl.ANY)
    far = pl.BlockSpec(memory_space=pltpu.HBM)
    near = pl.BlockSpec(memory_space=pltpu.VMEM)
    stream = jax.ShapeDtypeStruct(signal.shape, jnp.bfloat16)
    operands = [signal, skip_cot, res_cot, *taps, *own, *mine, *other]
    rows = lambda *shape: pltpu.VMEM((*shape, seqs, seq_rows, channels), jnp.bfloat16)
    scratch = [
        pltpu.VMEM((layers, channels, width), jnp.bfloat16),
        rows(),
        rows(),
        rows(layers),
        rows(layers),
        pltpu.VMEM((layers, seqs, seq_rows, 2 * channels), jnp.bfloat16),
        rows(layers + 1),
        pltpu.VMEM((layers, seqs, seq_rows, channels), jnp.float32),
        pltpu.VMEM((layers, seqs, seq_rows, channels), jnp.float32),
        rows(),
        pltpu.SemaphoreType.DMA((layers,)),
        pltpu.SemaphoreType.DMA((3,)),
        pltpu.SemaphoreType.DMA,
        pltpu.SemaphoreType.DMA,
        pltpu.SemaphoreType.DMA,
    ]
    in_specs = [far] * 3 + [anywhere] * (len(operands) - 3)
    aliases = {}
    if last:
        skip_total, grads, sums = earlier
        in_specs += [anywhere, far, far]
        aliases = {len(operands) + 1: 0, len(operands) + 2: 1}
        operands += [sums, skip_total, grads]
        shapes = [((channels // 2, width), jnp.bfloat16), ((channels // 2, width), jnp.float32)]
        scratch += [pltpu.VMEM((channels, width), jnp.float32), pltpu.SemaphoreType.DMA]
    else:
        shapes = [((seq_rows, channels), jnp.bfloat16), ((channels, width), jnp.float32)]
    flops = 2 * 22 * layers * seqs * seq_rows * channels * channels
    return pl.pallas_call(
        functools.partial(stack_kernel, layers, last),
        in_specs=in_specs,
        out_specs=[far, far, near, near],
        out_shape=[stream, stream] + [jax.ShapeDtypeStruct(*shape) for shape in shapes],
        scratch_shapes=scratch,
        input_output_aliases=aliases,
        compiler_params=pltpu.CompilerParams(vmem_limit_bytes=(48 if last else 24) * 2**20),
        cost_estimate=pl.CostEstimate(flops=flops, bytes_accessed=16 * seqs * seq_rows * channels, transcendentals=0),
        name="layer_stack",
    )(*operands)


def spread_kernel(places, kept, got, own_out, *outs):
    place = lax.axis_index("tm") // 2
    piece_rows = own_out.shape[0]
    for by in range(places):
        rows = pl.ds(pl.multiple_of(jnp.bitwise_xor(place, by) * piece_rows, piece_rows), piece_rows)
        total = kept[rows] + got[rows].astype(jnp.float32)
        if by == 0:
            own_out[...] = total
        else:
            outs[by - 1][...] = total.astype(jnp.bfloat16)


def final_kernel(places, scale, *refs):
    shard = lax.axis_index("tm")
    place, core = shard // 2, lax.rem(shard, 2)
    pieces, other, outs = refs[:places], refs[places], refs[places + 1 :]
    piece_rows = pieces[0].shape[0]
    live = jnp.where(lax.axis_index("section") == 0, scale, 0.0)
    for side, values in ((core, [ref[...] for ref in pieces]), (1 - core, [other[i] for i in range(places)])):
        for by, value in enumerate(values):
            at = (side * places + jnp.bitwise_xor(place, by)) * piece_rows
            rows = pl.ds(pl.multiple_of(at, piece_rows), piece_rows)
            value = value.astype(jnp.float32)
            column = 0
            for i, out in enumerate(outs):
                width = out.shape[2]
                out[0, rows, :] = value[:, column : column + width] * (live if i == 0 else scale)
                column += width


def local_call(kernel, name, operands, out_shape):
    near = pl.BlockSpec(memory_space=pltpu.VMEM)
    return pl.pallas_call(
        kernel,
        in_specs=[near] * len(operands),
        out_specs=[near] * len(out_shape),
        out_shape=out_shape,
        compiler_params=pltpu.CompilerParams(vmem_limit_bytes=12 * 2**20),
        name=name,
    )(*operands)


def swapped(x, axis, by):
    return lax.ppermute(x, axis, [(i, i ^ by) for i in range(lax.axis_size(axis))])


def sum_over_shards(sent, kept, places, scale):
    rows, width = kept.shape
    piece = (rows // places, width)
    got = swapped(sent, "tm", 1)
    narrow = jax.ShapeDtypeStruct(piece, jnp.bfloat16)
    own, *pieces = local_call(
        functools.partial(spread_kernel, places), "spread", [kept, got],
        [jax.ShapeDtypeStruct(piece, jnp.float32)] + [narrow] * (places - 1),
    )
    arrived = [swapped(value, "tm", 2 * (by + 1)) for by, value in enumerate(pieces)]
    total = sum([value.astype(jnp.float32) for value in arrived], own).astype(jnp.bfloat16)
    by_distance = [total] + [swapped(total, "tm", 2 * by) for by in range(1, places)]
    other = swapped(jnp.stack(by_distance), "tm", 1)
    channels = width // 6
    out_shape = [jax.ShapeDtypeStruct((1, 2 * rows, cols), jnp.float32) for cols in (2 * channels, 2 * channels, channels, channels)]
    return local_call(functools.partial(final_kernel, places, scale), "place_sums", by_distance + [other], out_shape)


def stacked_body(signal, skip_cot, res_cot, w_tap, w_now, w_res, w_skip):
    sections = lax.axis_size("section")
    shards = lax.axis_size("tm")
    section = lax.axis_index("section")
    core = lax.axis_index("tm") % 2
    number, seq_rows, channels = signal.shape
    span = FIRST_DILATION // seq_rows

    tap = passed_along(lax.dynamic_index_in_dim(signal, section, 0, False), "tm", span)
    packed = jnp.concatenate([w_now[0], w_res[0], w_skip[0], w_tap[0]], axis=1)
    half_rows = packed.shape[0] // 2
    own_half = lax.dynamic_slice_in_dim(packed, core * half_rows, half_rows, 0)
    mine = [swapped(own_half, "section", by) for by in range(1, sections)]
    tap, mine = lax.optimization_barrier((tap, mine))
    other = [swapped(piece, "tm", 1) for piece in mine]
    taps = [tap] + [swapped(tap, "section", by) for by in range(1, sections)]

    own = (w_now, w_res, w_skip, w_tap)
    streams = (signal, skip_cot, res_cot)
    skip_total, grads, back, sums = layer_stack(*streams, taps[:1], own, mine, other)
    back = passed_along(back, "tm", -span)
    skip_total, grads, sent, kept = layer_stack(*streams, taps[1:], own, mine, other, (skip_total, grads, sums))
    sent, back = lax.optimization_barrier((sent, back))
    arrived = [lax.ppermute(back, "section", [(by, 0)]) for by in range(1, sections)]
    first = jnp.where(section == 0, back, jnp.zeros_like(back))
    grad_scale = 1.0 / math.sqrt(number * seq_rows * shards)
    summed = sum_over_shards(sent, kept, shards // 2, grad_scale)
    back_total = jnp.stack([first] + arrived).astype(jnp.float32)
    input_grads = (grads.astype(jnp.float32) + back_total).astype(jnp.bfloat16)
    return (skip_total, input_grads[None], *summed)


def body(signal, skip_cot, res_cot, w_tap, w_now, w_res, w_skip):
    sections = lax.axis_size("section")
    shards = lax.axis_size("tm")
    number, seq_rows, channels = signal.shape
    span, beyond = divmod(FIRST_DILATION, seq_rows)
    one_live_tap = beyond == 0 and span < shards <= 2 * span
    square = w_res.shape[1:] == (channels, channels) and w_skip.shape[1:] == (channels, channels)
    pairs = sections == number == 4 and shards % 2 == 0 and shards & (shards - 1) == 0
    if one_live_tap and square and pairs:
        return stacked_body(signal, skip_cot, res_cot, w_tap, w_now, w_res, w_skip)
    return pipelined_body(signal, skip_cot, res_cot, w_tap, w_now, w_res, w_skip)


def solution(mesh):
    in_specs = (
        P(None, "tm", None),
        P(None, "tm", None),
        P(None, "tm", None),
        P("section", None, None),
        P("section", None, None),
        P("section", None, None),
        P("section", None, None),
    )
    out_specs = (
        P(None, "tm", None),
        P("section", None, "tm", None),
        P("section", None, None),
        P("section", None, None),
        P("section", None, None),
        P("section", None, None),
    )
    return jax.shard_map(body, mesh=mesh, in_specs=in_specs, out_specs=out_specs, check_vma=False)
```

```python
import functools
import math

import jax
import jax.numpy as jnp
from jax import lax
from jax.experimental import pallas as pl
from jax.experimental.pallas import tpu as pltpu
from jax.sharding import PartitionSpec as P

SPAN = 4
FIRST_DILATION = 2048


def passed_along(x, axis, by):
    size = lax.axis_size(axis)
    pairs = [(i, i + by) for i in range(size) if 0 <= i + by < size]
    return lax.ppermute(x, axis, pairs)


def flat_dot(left, right):
    result = jnp.dot(left.reshape(-1, left.shape[-1]), right, preferred_element_type=jnp.float32)
    return result.reshape(left.shape[:-1] + (right.shape[-1],))


def rows_spanning(left, right):
    return lax.dot_general(
        left.reshape(-1, left.shape[-1]),
        right.reshape(-1, right.shape[-1]),
        (((0,), (0,)), ((), ())),
        preferred_element_type=jnp.float32,
    )


def tap_rows(values, chosen, delayed):
    result = jnp.zeros_like(values)
    for layer_number, selected in chosen:
        if delayed:
            arrived = passed_along(values, "tm", SPAN << layer_number)
        else:
            arrived = passed_along(values, "tm", -(SPAN << layer_number))
        result = jnp.where(selected, arrived, result)
    return result


def gate_parts(tapped, layer_in, weights):
    pre = flat_dot(tapped, weights[0]) + flat_dot(layer_in, weights[1])
    half_width = pre.shape[-1] // 2
    return (jnp.tanh(pre[..., :half_width]), jax.nn.sigmoid(pre[..., half_width:]))


def layer_forward(layer_in, weights, chosen):
    tapped = tap_rows(layer_in, chosen, True)
    tanh_part, sigmoid_part = gate_parts(tapped, layer_in, weights)
    gated = (tanh_part * sigmoid_part).astype(jnp.bfloat16)
    stream_out = (layer_in.astype(jnp.float32) + flat_dot(gated, weights[2])).astype(jnp.bfloat16)
    return (tapped, stream_out, flat_dot(gated, weights[3]))


def layer_backward(layer_in, tapped, grad_out, skip_grad, weights, chosen):
    tanh_part, sigmoid_part = gate_parts(tapped, layer_in, weights)
    gated = (tanh_part * sigmoid_part).astype(jnp.bfloat16)
    grad_gated = flat_dot(grad_out, weights[2].T) + flat_dot(skip_grad, weights[3].T)
    grad_pre = jnp.concatenate(
        [
            grad_gated * sigmoid_part * (1.0 - tanh_part * tanh_part),
            grad_gated * tanh_part * sigmoid_part * (1.0 - sigmoid_part),
        ],
        axis=-1,
    ).astype(jnp.bfloat16)
    terms = (
        rows_spanning(tapped, grad_pre),
        rows_spanning(layer_in, grad_pre),
        rows_spanning(gated, grad_out),
        rows_spanning(gated, skip_grad),
    )
    back_term = flat_dot(grad_pre, weights[0].T).astype(jnp.bfloat16)
    arrived = tap_rows(back_term, chosen, False)
    grad_in = (
        grad_out.astype(jnp.float32)
        + flat_dot(grad_pre, weights[1].T)
        + arrived.astype(jnp.float32)
    )
    return (grad_in.astype(jnp.bfloat16), terms)


def keep_slot(holding_rows, micro_index, in_range, value):
    former = lax.dynamic_slice_in_dim(holding_rows, micro_index, 1, 0)
    return lax.dynamic_update_slice_in_dim(
        holding_rows, jnp.where(in_range, value, former), micro_index, 0
    )


def run_layers(signal, skip_cot, res_cot, w_tap, w_now, w_res, w_skip, section_index, sections):
    number, seq_rows, channels = signal.shape
    weights = (w_tap[0], w_now[0], w_res[0], w_skip[0])
    total_steps = number + sections - 1
    saved_in = jnp.zeros((number, seq_rows, channels), jnp.bfloat16)
    saved_tap = jnp.zeros((number, seq_rows, channels), jnp.bfloat16)
    skip_running_sum = jnp.zeros((number, seq_rows, w_skip.shape[2]), jnp.float32)
    received = jnp.zeros((1, seq_rows, channels), jnp.bfloat16)
    for moment in range(total_steps):
        chosen = [
            (layer_number, section_index == layer_number)
            for layer_number in range(sections)
            if 0 <= moment - layer_number < number
        ]
        position = moment - section_index
        in_range = (position >= 0) & (position < number)
        micro_index = jnp.clip(position, 0, number - 1)
        incoming = signal[min(moment, number - 1)][None]
        layer_in = jnp.where(section_index == 0, incoming, received)
        tapped, stream_out, skip_term = layer_forward(layer_in, weights, chosen)
        saved_in = keep_slot(saved_in, micro_index, in_range, layer_in)
        saved_tap = keep_slot(saved_tap, micro_index, in_range, tapped)
        skip_running_sum = keep_slot(skip_running_sum, micro_index, in_range, skip_term)
        if moment + 1 < total_steps:
            received = passed_along(stream_out, "section", 1)
    skip_total = lax.psum(skip_running_sum, "section").astype(jnp.bfloat16)
    partial_sums = [
        jnp.zeros(weights[0].shape, jnp.float32),
        jnp.zeros(weights[1].shape, jnp.float32),
        jnp.zeros(weights[2].shape, jnp.float32),
        jnp.zeros(weights[3].shape, jnp.float32),
    ]
    input_grads = jnp.zeros((number, seq_rows, channels), jnp.bfloat16)
    received = jnp.zeros((1, seq_rows, channels), jnp.bfloat16)
    for moment in range(total_steps):
        chosen = [
            (layer_number, section_index == layer_number)
            for layer_number in range(sections)
            if 0 <= moment - (sections - 1 - layer_number) < number
        ]
        position = moment - (sections - 1 - section_index)
        in_range = (position >= 0) & (position < number)
        micro_index = jnp.clip(position, 0, number - 1)
        top_grad = lax.dynamic_slice_in_dim(res_cot, micro_index, 1, 0)
        grad_out = jnp.where(section_index == sections - 1, top_grad, received)
        layer_in = lax.dynamic_slice_in_dim(saved_in, micro_index, 1, 0)
        tapped = lax.dynamic_slice_in_dim(saved_tap, micro_index, 1, 0)
        skip_grad = lax.dynamic_slice_in_dim(skip_cot, micro_index, 1, 0)
        grad_in, terms = layer_backward(layer_in, tapped, grad_out, skip_grad, weights, chosen)
        factor = in_range.astype(jnp.float32)
        partial_sums = [partial_sums[spot] + factor * terms[spot] for spot in range(4)]
        input_grads = keep_slot(input_grads, micro_index, in_range, grad_in)
        if moment + 1 < total_steps:
            received = passed_along(grad_in, "section", -1)
    return (skip_total, input_grads, tuple((part[None] for part in partial_sums)))


def pipelined_body(signal, skip_cot, res_cot, w_tap, w_now, w_res, w_skip):
    sections = lax.axis_size("section")
    shards = lax.axis_size("tm")
    section_index = lax.axis_index("section")
    number, seq_rows, channels = signal.shape
    skip_total, input_grads, partial_sums = run_layers(
        signal, skip_cot, res_cot, w_tap, w_now, w_res, w_skip, section_index, sections
    )
    summed = lax.psum((partial_sums[0], partial_sums[1], partial_sums[2], partial_sums[3]), "tm")
    grad_scale = 1.0 / math.sqrt(number * seq_rows * shards)
    return (
        skip_total,
        input_grads[None],
        summed[0] * grad_scale,
        summed[1] * grad_scale,
        summed[2] * grad_scale,
        summed[3] * grad_scale,
    )


def narrow_dot(left, right):
    return lax.dot_general(left, right, (((1,), (0,)), ((), ())), preferred_element_type=jnp.float32)


def rows_dot(left, right):
    return lax.dot_general(left, right, (((0,), (0,)), ((), ())), preferred_element_type=jnp.float32)


def turned_dot(left, right):
    return lax.dot_general(left, right, (((1,), (1,)), ((), ())), preferred_element_type=jnp.float32)


def stack_kernel(layers, last, *refs):
    refs = list(refs)
    take = lambda count: [refs.pop(0) for _ in range(count)]
    signal, cot, res_cot = take(3)
    taps = take(layers - 1 if last else 1)
    if last:
        weights, sums_in, _, _ = take(4)
        skip_out, grad_out, sent_out, kept_out = take(4)
    else:
        own = take(4)
        mine = take(layers - 1)
        other = take(layers - 1)
        skip_out, grad_out, back_out, sums, weights = take(5)
    tapped, h_all, gated_all, dz_all, g_all, tanh_all, sig_all, skip_total = take(8)
    stream_here, tap_here, skip_gone, grad_gone = take(4)
    if last:
        (sums,) = take(1)
    else:
        (weights_here,) = take(1)
    section = lax.axis_index("section")
    core = lax.rem(lax.axis_index("tm"), 2)
    _, seqs, seq_rows, channels = h_all.shape
    half = channels
    now = slice(0, 2 * half)
    res = slice(2 * half, 2 * half + channels)
    skip = slice(2 * half + channels, 2 * half + 2 * channels)
    tap = slice(2 * half + 2 * channels, 4 * half + 2 * channels)
    low_rows = channels // 2
    these = [jnp.bitwise_xor(section, i + 1) if last else section for i in range(seqs)]

    def wait_bytes(target, there):
        pltpu.make_async_copy(target, target, there).wait()

    if not last:
        for ref, cols in zip(own, (now, res, skip, tap)):
            pltpu.make_async_copy(ref.at[0], weights.at[section, :, cols], weights_here.at[section]).start()
        for by in range(1, layers):
            slot = jnp.bitwise_xor(section, by)
            for ref, side in ((mine[by - 1], core), (other[by - 1], 1 - core)):
                rows = pl.ds(pl.multiple_of(side * low_rows, low_rows), low_rows)
                pltpu.make_async_copy(ref, weights.at[slot, rows], weights_here.at[slot]).start()
    pltpu.make_async_copy(signal, h_all.at[0], stream_here.at[0]).start()
    for i, ref in enumerate(taps):
        pltpu.make_async_copy(ref, tapped.at[i], tap_here).start()
    pltpu.make_async_copy(res_cot, g_all.at[layers], stream_here.at[1]).start()

    wait_bytes(h_all.at[0], stream_here.at[0])
    for k in range(layers):
        if not last:
            wait_bytes(weights.at[k], weights_here.at[k])
        if k == 0:
            wait_bytes(tapped, tap_here)
        for i in range(seqs):
            pre = narrow_dot(h_all[k, i], weights[k, :, now])
            if k == 0:
                pre = pre + narrow_dot(tapped[i], weights[0, :, tap])
            tanh_part = jnp.tanh(pre[:, :half])
            sig_part = 0.5 * jnp.tanh(0.5 * pre[:, half:]) + 0.5
            tanh_all[k, i] = tanh_part
            sig_all[k, i] = sig_part
            gated_all[k, i] = (tanh_part * sig_part).astype(jnp.bfloat16)
        if k + 1 < layers:
            for i in range(seqs):
                stream = narrow_dot(gated_all[k, i], weights[k, :, res])
                h_all[k + 1, i] = (h_all[k, i].astype(jnp.float32) + stream).astype(jnp.bfloat16)
    wait_bytes(g_all.at[layers], stream_here.at[1])
    for i in range(seqs):
        total = narrow_dot(gated_all[0, i], weights[0, :, skip])
        for k in range(1, layers):
            total = total + narrow_dot(gated_all[k, i], weights[k, :, skip])
        skip_total[i] = total.astype(jnp.bfloat16)
    for i in range(seqs):
        pltpu.make_async_copy(skip_total.at[i], skip_out.at[these[i]], skip_gone).start()
    for k in reversed(range(layers)):
        for i in range(seqs):
            du = turned_dot(g_all[k + 1, i], weights[k, :, res]) + turned_dot(cot[i], weights[k, :, skip])
            tanh_part = tanh_all[k, i]
            sig_part = sig_all[k, i]
            scaled = du * sig_part
            dz_all[k, i, :, :half] = (scaled * (1.0 - tanh_part * tanh_part)).astype(jnp.bfloat16)
            dz_all[k, i, :, half:] = (scaled * (tanh_part * (1.0 - sig_part))).astype(jnp.bfloat16)
        for i in range(seqs):
            below = turned_dot(dz_all[k, i], weights[k, :, now])
            g_all[k, i] = (g_all[k + 1, i].astype(jnp.float32) + below).astype(jnp.bfloat16)
    for i in range(seqs):
        pltpu.make_async_copy(g_all.at[section, i], grad_out.at[these[i]], grad_gone).start()
    if not last:
        back_out[...] = turned_dot(dz_all[0, 0], weights[0, :, tap]).astype(jnp.bfloat16)
    for i in range(seqs):
        products = (
            rows_dot(tapped[i], dz_all[section, i]),
            rows_dot(h_all[section, i], dz_all[section, i]),
            rows_dot(gated_all[section, i], g_all[section + 1, i]),
            rows_dot(gated_all[section, i], cot[i]),
        )
        spots = (slice(0, 2 * half), slice(2 * half, 4 * half), slice(4 * half, 4 * half + channels), slice(4 * half + channels, None))
        for spot, product in zip(spots, products):
            if i == 0 and last:
                sums[:, spot] = sums_in[:, spot] + product
            elif i == 0:
                sums[:, spot] = product
            else:
                sums[:, spot] += product
    if last:
        kept_out[...] = sums[pl.ds(pl.multiple_of(core * low_rows, low_rows), low_rows)]
        sent_out[...] = sums[pl.ds(pl.multiple_of((1 - core) * low_rows, low_rows), low_rows)].astype(jnp.bfloat16)
    wait_bytes(skip_total, skip_gone)
    wait_bytes(skip_total, grad_gone)


def layer_stack(streams, taps, number, weights, earlier=None):
    seqs, seq_rows, channels = streams[0].shape
    layers = number
    last = earlier is not None
    width = 6 * channels
    anywhere = pl.BlockSpec(memory_space=pl.ANY)
    near = pl.BlockSpec(memory_space=pltpu.VMEM)
    stream = jax.ShapeDtypeStruct((number, seq_rows, channels), jnp.bfloat16)
    rows = lambda *shape: pltpu.VMEM((*shape, seqs, seq_rows, channels), jnp.bfloat16)
    scratch = [
        rows(),
        rows(layers),
        rows(layers),
        pltpu.VMEM((layers, seqs, seq_rows, 2 * channels), jnp.bfloat16),
        rows(layers + 1),
        pltpu.VMEM((layers, seqs, seq_rows, channels), jnp.float32),
        pltpu.VMEM((layers, seqs, seq_rows, channels), jnp.float32),
        rows(),
        pltpu.SemaphoreType.DMA((2,)),
        pltpu.SemaphoreType.DMA,
        pltpu.SemaphoreType.DMA,
        pltpu.SemaphoreType.DMA,
    ]
    operands = [*streams, *taps, *weights]
    in_specs = [near] * 3 + [anywhere] * len(taps) + [near if last else anywhere] * len(weights)
    aliases = {}
    if last:
        skip_total, grads, sums = earlier
        aliases = {len(operands) + 1: 0, len(operands) + 2: 1}
        operands += [sums, skip_total, grads]
        in_specs += [near, anywhere, anywhere]
        shapes = [((channels // 2, width), jnp.bfloat16), ((channels // 2, width), jnp.float32)]
        scratch += [pltpu.VMEM((channels, width), jnp.float32)]
    else:
        shapes = [((seq_rows, channels), jnp.bfloat16), ((channels, width), jnp.float32), ((layers, channels, width), jnp.bfloat16)]
        scratch += [pltpu.SemaphoreType.DMA((layers,))]
    flops = 2 * 22 * layers * seqs * seq_rows * channels * channels
    return pl.pallas_call(
        functools.partial(stack_kernel, layers, last),
        in_specs=in_specs,
        out_specs=[anywhere, anywhere] + [near] * len(shapes),
        out_shape=[stream, stream] + [jax.ShapeDtypeStruct(*shape) for shape in shapes],
        scratch_shapes=scratch,
        input_output_aliases=aliases,
        compiler_params=pltpu.CompilerParams(vmem_limit_bytes=(44 if last else 24) * 2**20),
        cost_estimate=pl.CostEstimate(flops=flops, bytes_accessed=16 * seqs * seq_rows * channels, transcendentals=0),
        name="layer_stack",
    )(*operands)


def order_kernel(*refs):
    count = (len(refs) - 1) // 3
    sources, owns, others, sems = refs[:count], refs[count : 2 * count], refs[2 * count : 3 * count], refs[-1]
    section = lax.axis_index("section")
    copies = []
    for i, source in enumerate(sources):
        for by in range(source.shape[0]):
            target = owns[i].at[0] if by == 0 else others[i].at[by - 1]
            copies.append(pltpu.make_async_copy(source.at[jnp.bitwise_xor(section, by)], target, sems.at[i, by]))
    for copy in copies:
        copy.start()
    for copy in copies:
        copy.wait()


def order_streams(*streams):
    number, seq_rows, channels = streams[0].shape
    count = len(streams)
    anywhere = pl.BlockSpec(memory_space=pl.ANY)
    near = pl.BlockSpec(memory_space=pltpu.VMEM)
    shape = lambda seqs: jax.ShapeDtypeStruct((seqs, seq_rows, channels), jnp.bfloat16)
    ordered = pl.pallas_call(
        order_kernel,
        in_specs=[anywhere] * count,
        out_specs=[near] * 2 * count,
        out_shape=[shape(1)] * count + [shape(number - 1)] * count,
        scratch_shapes=[pltpu.SemaphoreType.DMA((count, number))],
        compiler_params=pltpu.CompilerParams(vmem_limit_bytes=8 * 2**20),
        cost_estimate=pl.CostEstimate(flops=0, bytes_accessed=2**24, transcendentals=0),
        name="order_streams",
    )(*streams)
    return ordered[:count], ordered[count:]


def spread_kernel(places, kept, got, own_out, *outs):
    place = lax.axis_index("tm") // 2
    piece_rows = own_out.shape[0]
    for by in range(places):
        rows = pl.ds(pl.multiple_of(jnp.bitwise_xor(place, by) * piece_rows, piece_rows), piece_rows)
        total = kept[rows] + got[rows].astype(jnp.float32)
        if by == 0:
            own_out[...] = total
        else:
            outs[by - 1][...] = total.astype(jnp.bfloat16)


def final_kernel(places, scale, *refs):
    shard = lax.axis_index("tm")
    place, core = shard // 2, lax.rem(shard, 2)
    pieces, other, outs = refs[:places], refs[places], refs[places + 1 :]
    piece_rows = pieces[0].shape[0]
    live = jnp.where(lax.axis_index("section") == 0, scale, 0.0)
    for side, values in ((core, [ref[...] for ref in pieces]), (1 - core, [other[i] for i in range(places)])):
        for by, value in enumerate(values):
            at = (side * places + jnp.bitwise_xor(place, by)) * piece_rows
            rows = pl.ds(pl.multiple_of(at, piece_rows), piece_rows)
            value = value.astype(jnp.float32)
            column = 0
            for i, out in enumerate(outs):
                width = out.shape[2]
                out[0, rows, :] = value[:, column : column + width] * (live if i == 0 else scale)
                column += width


def local_call(kernel, name, operands, out_shape):
    near = pl.BlockSpec(memory_space=pltpu.VMEM)
    return pl.pallas_call(
        kernel,
        in_specs=[near] * len(operands),
        out_specs=[near] * len(out_shape),
        out_shape=out_shape,
        compiler_params=pltpu.CompilerParams(vmem_limit_bytes=12 * 2**20),
        name=name,
    )(*operands)


def swapped(x, axis, by):
    return lax.ppermute(x, axis, [(i, i ^ by) for i in range(lax.axis_size(axis))])


def between(x, shards, pairs, reached):
    return lax.ppermute(x, ("section", "tm"), [(i * shards + t, j * shards + t) for i, j in pairs for t in reached])


def sum_over_shards(sent, kept, places, scale, ready):
    rows, width = kept.shape
    piece = (rows // places, width)
    got = swapped(sent, "tm", 1)
    narrow = jax.ShapeDtypeStruct(piece, jnp.bfloat16)
    own, *pieces = local_call(
        functools.partial(spread_kernel, places), "spread", [kept, got],
        [jax.ShapeDtypeStruct(piece, jnp.float32)] + [narrow] * (places - 1),
    )
    arrived = [swapped(value, "tm", 2 * (by + 1)) for by, value in enumerate(pieces)]
    total = sum([value.astype(jnp.float32) for value in arrived], own).astype(jnp.bfloat16)
    total, ready = lax.optimization_barrier((total, ready))
    by_distance = [total] + [swapped(total, "tm", 2 * by) for by in range(1, places)]
    other = swapped(jnp.stack(by_distance), "tm", 1)
    channels = width // 6
    out_shape = [jax.ShapeDtypeStruct((1, 2 * rows, cols), jnp.float32) for cols in (2 * channels, 2 * channels, channels, channels)]
    return local_call(functools.partial(final_kernel, places, scale), "place_sums", by_distance + [other], out_shape), ready


def stacked_body(signal, skip_cot, res_cot, w_tap, w_now, w_res, w_skip):
    sections = lax.axis_size("section")
    shards = lax.axis_size("tm")
    section = lax.axis_index("section")
    core = lax.axis_index("tm") % 2
    number, seq_rows, channels = signal.shape
    span = FIRST_DILATION // seq_rows

    tap = passed_along(lax.dynamic_index_in_dim(signal, section, 0, False), "tm", span)
    packed = jnp.concatenate([w_now[0], w_res[0], w_skip[0], w_tap[0]], axis=1)
    half_rows = packed.shape[0] // 2
    own_half = lax.dynamic_slice_in_dim(packed, core * half_rows, half_rows, 0)
    mine = [swapped(own_half, "section", by) for by in range(1, sections)]
    own_streams, other_streams = order_streams(signal, skip_cot, res_cot)
    tap, mine, own_streams, other_streams = lax.optimization_barrier((tap, mine, own_streams, other_streams))
    other = [swapped(piece, "tm", 1) for piece in mine]
    taps = [tap] + [swapped(tap, "section", by) for by in range(1, sections)]

    pieces = [w_now, w_res, w_skip, w_tap, *mine, *other]
    skip_total, grads, back, sums, weights = layer_stack(own_streams, taps[:1], number, pieces)
    back = passed_along(back, "tm", -span)
    skip_total, grads, sent, kept = layer_stack(other_streams, taps[1:], number, [weights], (skip_total, grads, sums))
    sent, back = lax.optimization_barrier((sent, back))
    reached = range(shards - span)
    arrived = [between(back, shards, [(by, 0)], reached) for by in range(1, sections)]
    grad_scale = 1.0 / math.sqrt(number * seq_rows * shards)
    summed, arrived[::2] = sum_over_shards(sent, kept, shards // 2, grad_scale, arrived[::2])
    first = jnp.where(section == 0, back, jnp.zeros_like(back))
    back_total = jnp.stack([first] + arrived).astype(jnp.float32)
    input_grads = (grads.astype(jnp.float32) + back_total).astype(jnp.bfloat16)
    return (skip_total, input_grads[None], *summed)


def body(signal, skip_cot, res_cot, w_tap, w_now, w_res, w_skip):
    sections = lax.axis_size("section")
    shards = lax.axis_size("tm")
    number, seq_rows, channels = signal.shape
    span, beyond = divmod(FIRST_DILATION, seq_rows)
    one_live_tap = beyond == 0 and span < shards <= 2 * span
    square = w_res.shape[1:] == (channels, channels) and w_skip.shape[1:] == (channels, channels)
    pairs = sections == number == 4 and shards % 2 == 0 and shards & (shards - 1) == 0
    if one_live_tap and square and pairs:
        return stacked_body(signal, skip_cot, res_cot, w_tap, w_now, w_res, w_skip)
    return pipelined_body(signal, skip_cot, res_cot, w_tap, w_now, w_res, w_skip)


def solution(mesh):
    in_specs = (
        P(None, "tm", None),
        P(None, "tm", None),
        P(None, "tm", None),
        P("section", None, None),
        P("section", None, None),
        P("section", None, None),
        P("section", None, None),
    )
    out_specs = (
        P(None, "tm", None),
        P("section", None, "tm", None),
        P("section", None, None),
        P("section", None, None),
        P("section", None, None),
        P("section", None, None),
    )
    return jax.shard_map(body, mesh=mesh, in_specs=in_specs, out_specs=out_specs, check_vma=False)
```

```python
import functools
import math

import jax
import jax.numpy as jnp
from jax import lax
from jax.experimental import pallas as pl
from jax.experimental.pallas import tpu as pltpu
from jax.sharding import PartitionSpec as P

SPAN = 4
FIRST_DILATION = 2048


def passed_along(x, axis, by):
    size = lax.axis_size(axis)
    pairs = [(i, i + by) for i in range(size) if 0 <= i + by < size]
    return lax.ppermute(x, axis, pairs)


def flat_dot(left, right):
    result = jnp.dot(left.reshape(-1, left.shape[-1]), right, preferred_element_type=jnp.float32)
    return result.reshape(left.shape[:-1] + (right.shape[-1],))


def rows_spanning(left, right):
    return lax.dot_general(
        left.reshape(-1, left.shape[-1]),
        right.reshape(-1, right.shape[-1]),
        (((0,), (0,)), ((), ())),
        preferred_element_type=jnp.float32,
    )


def tap_rows(values, chosen, delayed):
    result = jnp.zeros_like(values)
    for layer_number, selected in chosen:
        if delayed:
            arrived = passed_along(values, "tm", SPAN << layer_number)
        else:
            arrived = passed_along(values, "tm", -(SPAN << layer_number))
        result = jnp.where(selected, arrived, result)
    return result


def gate_parts(tapped, layer_in, weights):
    pre = flat_dot(tapped, weights[0]) + flat_dot(layer_in, weights[1])
    half_width = pre.shape[-1] // 2
    return (jnp.tanh(pre[..., :half_width]), jax.nn.sigmoid(pre[..., half_width:]))


def layer_forward(layer_in, weights, chosen):
    tapped = tap_rows(layer_in, chosen, True)
    tanh_part, sigmoid_part = gate_parts(tapped, layer_in, weights)
    gated = (tanh_part * sigmoid_part).astype(jnp.bfloat16)
    stream_out = (layer_in.astype(jnp.float32) + flat_dot(gated, weights[2])).astype(jnp.bfloat16)
    return (tapped, stream_out, flat_dot(gated, weights[3]))


def layer_backward(layer_in, tapped, grad_out, skip_grad, weights, chosen):
    tanh_part, sigmoid_part = gate_parts(tapped, layer_in, weights)
    gated = (tanh_part * sigmoid_part).astype(jnp.bfloat16)
    grad_gated = flat_dot(grad_out, weights[2].T) + flat_dot(skip_grad, weights[3].T)
    grad_pre = jnp.concatenate(
        [
            grad_gated * sigmoid_part * (1.0 - tanh_part * tanh_part),
            grad_gated * tanh_part * sigmoid_part * (1.0 - sigmoid_part),
        ],
        axis=-1,
    ).astype(jnp.bfloat16)
    terms = (
        rows_spanning(tapped, grad_pre),
        rows_spanning(layer_in, grad_pre),
        rows_spanning(gated, grad_out),
        rows_spanning(gated, skip_grad),
    )
    back_term = flat_dot(grad_pre, weights[0].T).astype(jnp.bfloat16)
    arrived = tap_rows(back_term, chosen, False)
    grad_in = (
        grad_out.astype(jnp.float32)
        + flat_dot(grad_pre, weights[1].T)
        + arrived.astype(jnp.float32)
    )
    return (grad_in.astype(jnp.bfloat16), terms)


def keep_slot(holding_rows, micro_index, in_range, value):
    former = lax.dynamic_slice_in_dim(holding_rows, micro_index, 1, 0)
    return lax.dynamic_update_slice_in_dim(
        holding_rows, jnp.where(in_range, value, former), micro_index, 0
    )


def run_layers(signal, skip_cot, res_cot, w_tap, w_now, w_res, w_skip, section_index, sections):
    number, seq_rows, channels = signal.shape
    weights = (w_tap[0], w_now[0], w_res[0], w_skip[0])
    total_steps = number + sections - 1
    saved_in = jnp.zeros((number, seq_rows, channels), jnp.bfloat16)
    saved_tap = jnp.zeros((number, seq_rows, channels), jnp.bfloat16)
    skip_running_sum = jnp.zeros((number, seq_rows, w_skip.shape[2]), jnp.float32)
    received = jnp.zeros((1, seq_rows, channels), jnp.bfloat16)
    for moment in range(total_steps):
        chosen = [
            (layer_number, section_index == layer_number)
            for layer_number in range(sections)
            if 0 <= moment - layer_number < number
        ]
        position = moment - section_index
        in_range = (position >= 0) & (position < number)
        micro_index = jnp.clip(position, 0, number - 1)
        incoming = signal[min(moment, number - 1)][None]
        layer_in = jnp.where(section_index == 0, incoming, received)
        tapped, stream_out, skip_term = layer_forward(layer_in, weights, chosen)
        saved_in = keep_slot(saved_in, micro_index, in_range, layer_in)
        saved_tap = keep_slot(saved_tap, micro_index, in_range, tapped)
        skip_running_sum = keep_slot(skip_running_sum, micro_index, in_range, skip_term)
        if moment + 1 < total_steps:
            received = passed_along(stream_out, "section", 1)
    skip_total = lax.psum(skip_running_sum, "section").astype(jnp.bfloat16)
    partial_sums = [
        jnp.zeros(weights[0].shape, jnp.float32),
        jnp.zeros(weights[1].shape, jnp.float32),
        jnp.zeros(weights[2].shape, jnp.float32),
        jnp.zeros(weights[3].shape, jnp.float32),
    ]
    input_grads = jnp.zeros((number, seq_rows, channels), jnp.bfloat16)
    received = jnp.zeros((1, seq_rows, channels), jnp.bfloat16)
    for moment in range(total_steps):
        chosen = [
            (layer_number, section_index == layer_number)
            for layer_number in range(sections)
            if 0 <= moment - (sections - 1 - layer_number) < number
        ]
        position = moment - (sections - 1 - section_index)
        in_range = (position >= 0) & (position < number)
        micro_index = jnp.clip(position, 0, number - 1)
        top_grad = lax.dynamic_slice_in_dim(res_cot, micro_index, 1, 0)
        grad_out = jnp.where(section_index == sections - 1, top_grad, received)
        layer_in = lax.dynamic_slice_in_dim(saved_in, micro_index, 1, 0)
        tapped = lax.dynamic_slice_in_dim(saved_tap, micro_index, 1, 0)
        skip_grad = lax.dynamic_slice_in_dim(skip_cot, micro_index, 1, 0)
        grad_in, terms = layer_backward(layer_in, tapped, grad_out, skip_grad, weights, chosen)
        factor = in_range.astype(jnp.float32)
        partial_sums = [partial_sums[spot] + factor * terms[spot] for spot in range(4)]
        input_grads = keep_slot(input_grads, micro_index, in_range, grad_in)
        if moment + 1 < total_steps:
            received = passed_along(grad_in, "section", -1)
    return (skip_total, input_grads, tuple((part[None] for part in partial_sums)))


def pipelined_body(signal, skip_cot, res_cot, w_tap, w_now, w_res, w_skip):
    sections = lax.axis_size("section")
    shards = lax.axis_size("tm")
    section_index = lax.axis_index("section")
    number, seq_rows, channels = signal.shape
    skip_total, input_grads, partial_sums = run_layers(
        signal, skip_cot, res_cot, w_tap, w_now, w_res, w_skip, section_index, sections
    )
    summed = lax.psum((partial_sums[0], partial_sums[1], partial_sums[2], partial_sums[3]), "tm")
    grad_scale = 1.0 / math.sqrt(number * seq_rows * shards)
    return (
        skip_total,
        input_grads[None],
        summed[0] * grad_scale,
        summed[1] * grad_scale,
        summed[2] * grad_scale,
        summed[3] * grad_scale,
    )


def narrow_dot(left, right):
    return lax.dot_general(left, right, (((1,), (0,)), ((), ())), preferred_element_type=jnp.float32)


def rows_dot(left, right):
    return lax.dot_general(left, right, (((0,), (0,)), ((), ())), preferred_element_type=jnp.float32)


def turned_dot(left, right):
    return lax.dot_general(left, right, (((1,), (1,)), ((), ())), preferred_element_type=jnp.float32)


def stack_kernel(layers, last, *refs):
    refs = list(refs)
    take = lambda count: [refs.pop(0) for _ in range(count)]
    signal, cot, res_cot = take(3)
    taps = take(layers - 1 if last else 1)
    if last:
        weights, sums_in, _, _ = take(4)
        skip_out, grad_out, sent_out, kept_out = take(4)
    else:
        own = take(4)
        mine = take(layers - 1)
        other = take(layers - 1)
        skip_out, grad_out, back_out, sums, weights = take(5)
    tapped, h_all, gated_all, dz_all, g_all, tanh_all, sig_all, skip_total = take(8)
    stream_here, tap_here, skip_gone, grad_gone = take(4)
    if last:
        (sums,) = take(1)
    else:
        (weights_here,) = take(1)
    section = lax.axis_index("section")
    core = lax.rem(lax.axis_index("tm"), 2)
    _, seqs, seq_rows, channels = h_all.shape
    half = channels
    now = slice(0, 2 * half)
    res = slice(2 * half, 2 * half + channels)
    skip = slice(2 * half + channels, 2 * half + 2 * channels)
    tap = slice(2 * half + 2 * channels, 4 * half + 2 * channels)
    low_rows = channels // 2
    these = [jnp.bitwise_xor(section, i + 1) if last else section for i in range(seqs)]

    def wait_bytes(target, there):
        pltpu.make_async_copy(target, target, there).wait()

    if not last:
        for ref, cols in zip(own, (now, res, skip, tap)):
            pltpu.make_async_copy(ref.at[0], weights.at[section, :, cols], weights_here.at[section]).start()
        for by in range(1, layers):
            slot = jnp.bitwise_xor(section, by)
            for ref, side in ((mine[by - 1], core), (other[by - 1], 1 - core)):
                rows = pl.ds(pl.multiple_of(side * low_rows, low_rows), low_rows)
                pltpu.make_async_copy(ref, weights.at[slot, rows], weights_here.at[slot]).start()
    pltpu.make_async_copy(signal, h_all.at[0], stream_here.at[0]).start()
    for i, ref in enumerate(taps):
        pltpu.make_async_copy(ref, tapped.at[i], tap_here).start()
    pltpu.make_async_copy(res_cot, g_all.at[layers], stream_here.at[1]).start()

    wait_bytes(h_all.at[0], stream_here.at[0])
    for k in range(layers):
        if not last:
            wait_bytes(weights.at[k], weights_here.at[k])
        if k == 0:
            wait_bytes(tapped, tap_here)
        for i in range(seqs):
            pre = narrow_dot(h_all[k, i], weights[k, :, now])
            if k == 0:
                pre = pre + narrow_dot(tapped[i], weights[0, :, tap])
            tanh_part = jnp.tanh(pre[:, :half])
            sig_part = 0.5 * jnp.tanh(0.5 * pre[:, half:]) + 0.5
            tanh_all[k, i] = tanh_part
            sig_all[k, i] = sig_part
            gated_all[k, i] = (tanh_part * sig_part).astype(jnp.bfloat16)
        if k + 1 < layers:
            for i in range(seqs):
                stream = narrow_dot(gated_all[k, i], weights[k, :, res])
                h_all[k + 1, i] = (h_all[k, i].astype(jnp.float32) + stream).astype(jnp.bfloat16)
    wait_bytes(g_all.at[layers], stream_here.at[1])
    for i in range(seqs):
        total = narrow_dot(gated_all[0, i], weights[0, :, skip])
        for k in range(1, layers):
            total = total + narrow_dot(gated_all[k, i], weights[k, :, skip])
        skip_total[i] = total.astype(jnp.bfloat16)
    for i in range(seqs):
        pltpu.make_async_copy(skip_total.at[i], skip_out.at[these[i]], skip_gone).start()
    for k in reversed(range(layers)):
        for i in range(seqs):
            du = turned_dot(g_all[k + 1, i], weights[k, :, res]) + turned_dot(cot[i], weights[k, :, skip])
            tanh_part = tanh_all[k, i]
            sig_part = sig_all[k, i]
            scaled = du * sig_part
            dz_all[k, i, :, :half] = (scaled * (1.0 - tanh_part * tanh_part)).astype(jnp.bfloat16)
            dz_all[k, i, :, half:] = (scaled * (tanh_part * (1.0 - sig_part))).astype(jnp.bfloat16)
        for i in range(seqs):
            below = turned_dot(dz_all[k, i], weights[k, :, now])
            g_all[k, i] = (g_all[k + 1, i].astype(jnp.float32) + below).astype(jnp.bfloat16)
    for i in range(seqs):
        pltpu.make_async_copy(g_all.at[section, i], grad_out.at[these[i]], grad_gone).start()
    if not last:
        back_out[...] = turned_dot(dz_all[0, 0], weights[0, :, tap]).astype(jnp.bfloat16)
    for i in range(seqs):
        products = (
            rows_dot(tapped[i], dz_all[section, i]),
            rows_dot(h_all[section, i], dz_all[section, i]),
            rows_dot(gated_all[section, i], g_all[section + 1, i]),
            rows_dot(gated_all[section, i], cot[i]),
        )
        spots = (slice(0, 2 * half), slice(2 * half, 4 * half), slice(4 * half, 4 * half + channels), slice(4 * half + channels, None))
        for spot, product in zip(spots, products):
            if i == 0 and last:
                sums[:, spot] = sums_in[:, spot] + product
            elif i == 0:
                sums[:, spot] = product
            else:
                sums[:, spot] += product
    if last:
        kept_out[...] = sums[pl.ds(pl.multiple_of(core * low_rows, low_rows), low_rows)]
        sent_out[...] = sums[pl.ds(pl.multiple_of((1 - core) * low_rows, low_rows), low_rows)].astype(jnp.bfloat16)
    wait_bytes(skip_total, skip_gone)
    wait_bytes(skip_total, grad_gone)


def layer_stack(streams, taps, number, weights, earlier=None):
    seqs, seq_rows, channels = streams[0].shape
    layers = number
    last = earlier is not None
    width = 6 * channels
    anywhere = pl.BlockSpec(memory_space=pl.ANY)
    near = pl.BlockSpec(memory_space=pltpu.VMEM)
    stream = jax.ShapeDtypeStruct((number, seq_rows, channels), jnp.bfloat16)
    rows = lambda *shape: pltpu.VMEM((*shape, seqs, seq_rows, channels), jnp.bfloat16)
    scratch = [
        rows(),
        rows(layers),
        rows(layers),
        pltpu.VMEM((layers, seqs, seq_rows, 2 * channels), jnp.bfloat16),
        rows(layers + 1),
        pltpu.VMEM((layers, seqs, seq_rows, channels), jnp.float32),
        pltpu.VMEM((layers, seqs, seq_rows, channels), jnp.float32),
        rows(),
        pltpu.SemaphoreType.DMA((2,)),
        pltpu.SemaphoreType.DMA,
        pltpu.SemaphoreType.DMA,
        pltpu.SemaphoreType.DMA,
    ]
    operands = [*streams, *taps, *weights]
    in_specs = [near] * 3 + [anywhere] * len(taps) + [near if last else anywhere] * len(weights)
    aliases = {}
    if last:
        skip_total, grads, sums = earlier
        aliases = {len(operands) + 1: 0, len(operands) + 2: 1}
        operands += [sums, skip_total, grads]
        in_specs += [near, anywhere, anywhere]
        shapes = [((channels // 2, width), jnp.bfloat16), ((channels // 2, width), jnp.float32)]
        scratch += [pltpu.VMEM((channels, width), jnp.float32)]
    else:
        shapes = [((seq_rows, channels), jnp.bfloat16), ((channels, width), jnp.float32), ((layers, channels, width), jnp.bfloat16)]
        scratch += [pltpu.SemaphoreType.DMA((layers,))]
    flops = 2 * 22 * layers * seqs * seq_rows * channels * channels
    return pl.pallas_call(
        functools.partial(stack_kernel, layers, last),
        in_specs=in_specs,
        out_specs=[anywhere, anywhere] + [near] * len(shapes),
        out_shape=[stream, stream] + [jax.ShapeDtypeStruct(*shape) for shape in shapes],
        scratch_shapes=scratch,
        input_output_aliases=aliases,
        compiler_params=pltpu.CompilerParams(vmem_limit_bytes=(44 if last else 24) * 2**20),
        cost_estimate=pl.CostEstimate(flops=flops, bytes_accessed=16 * seqs * seq_rows * channels, transcendentals=0),
        name="layer_stack",
    )(*operands)


def order_kernel(*refs):
    count = (len(refs) - 1) // 3
    sources, owns, others, sems = refs[:count], refs[count : 2 * count], refs[2 * count : 3 * count], refs[-1]
    section = lax.axis_index("section")
    copies = []
    for i, source in enumerate(sources):
        for by in range(source.shape[0]):
            target = owns[i].at[0] if by == 0 else others[i].at[by - 1]
            copies.append(pltpu.make_async_copy(source.at[jnp.bitwise_xor(section, by)], target, sems.at[i, by]))
    for copy in copies:
        copy.start()
    for copy in copies:
        copy.wait()


def order_streams(*streams):
    number, seq_rows, channels = streams[0].shape
    count = len(streams)
    anywhere = pl.BlockSpec(memory_space=pl.ANY)
    near = pl.BlockSpec(memory_space=pltpu.VMEM)
    shape = lambda seqs: jax.ShapeDtypeStruct((seqs, seq_rows, channels), jnp.bfloat16)
    ordered = pl.pallas_call(
        order_kernel,
        in_specs=[anywhere] * count,
        out_specs=[near] * 2 * count,
        out_shape=[shape(1)] * count + [shape(number - 1)] * count,
        scratch_shapes=[pltpu.SemaphoreType.DMA((count, number))],
        compiler_params=pltpu.CompilerParams(vmem_limit_bytes=8 * 2**20),
        cost_estimate=pl.CostEstimate(flops=0, bytes_accessed=2**24, transcendentals=0),
        name="order_streams",
    )(*streams)
    return ordered[:count], ordered[count:]


def spread_kernel(places, kept, got, own_out, *outs):
    place = lax.axis_index("tm") // 2
    piece_rows = own_out.shape[0]
    for by in range(places):
        rows = pl.ds(pl.multiple_of(jnp.bitwise_xor(place, by) * piece_rows, piece_rows), piece_rows)
        total = kept[rows] + got[rows].astype(jnp.float32)
        if by == 0:
            own_out[...] = total
        else:
            outs[by - 1][...] = total.astype(jnp.bfloat16)


def final_kernel(places, scale, *refs):
    shard = lax.axis_index("tm")
    place, core = shard // 2, lax.rem(shard, 2)
    pieces, other, outs = refs[:places], refs[places], refs[places + 1 :]
    piece_rows = pieces[0].shape[0]
    live = jnp.where(lax.axis_index("section") == 0, scale, 0.0)
    for side, values in ((core, [ref[...] for ref in pieces]), (1 - core, [other[i] for i in range(places)])):
        for by, value in enumerate(values):
            at = (side * places + jnp.bitwise_xor(place, by)) * piece_rows
            rows = pl.ds(pl.multiple_of(at, piece_rows), piece_rows)
            value = value.astype(jnp.float32)
            column = 0
            for i, out in enumerate(outs):
                width = out.shape[2]
                out[0, rows, :] = value[:, column : column + width] * (live if i == 0 else scale)
                column += width


def add_kernel(grads, *refs):
    *backs, out = refs
    own = jnp.where(lax.axis_index("section") == 0, 1.0, 0.0)
    for i, back in enumerate(backs):
        term = back[...].astype(jnp.float32)
        out[i] = (grads[i].astype(jnp.float32) + (term * own if i == 0 else term)).astype(jnp.bfloat16)


def add_back(grads, backs):
    return local_call(add_kernel, "add_back", [grads, *backs], [grads], 2**24)[0]


def local_call(kernel, name, operands, out_shape, weight=0):
    near = pl.BlockSpec(memory_space=pltpu.VMEM)
    return pl.pallas_call(
        kernel,
        in_specs=[near] * len(operands),
        out_specs=[near] * len(out_shape),
        out_shape=[jax.ShapeDtypeStruct(value.shape, value.dtype) for value in out_shape],
        compiler_params=pltpu.CompilerParams(vmem_limit_bytes=12 * 2**20),
        cost_estimate=pl.CostEstimate(flops=0, bytes_accessed=weight, transcendentals=0) if weight else None,
        name=name,
    )(*operands)


def swapped(x, axis, by):
    return lax.ppermute(x, axis, [(i, i ^ by) for i in range(lax.axis_size(axis))])


def between(x, shards, pairs, reached):
    return lax.ppermute(x, ("section", "tm"), [(i * shards + t, j * shards + t) for i, j in pairs for t in reached])


def sum_over_shards(sent, kept, places, scale, beside):
    rows, width = kept.shape
    piece = (rows // places, width)
    got = swapped(sent, "tm", 1)
    narrow = jax.ShapeDtypeStruct(piece, jnp.bfloat16)
    own, *pieces = local_call(
        functools.partial(spread_kernel, places), "spread", [kept, got],
        [jax.ShapeDtypeStruct(piece, jnp.float32)] + [narrow] * (places - 1),
    )
    arrived = [swapped(value, "tm", 2 * (by + 1)) for by, value in enumerate(pieces)]
    total = sum([value.astype(jnp.float32) for value in arrived], own).astype(jnp.bfloat16)
    by_distance = [total] + [swapped(total, "tm", 2 * by) for by in range(1, places)]
    by_distance, beside = lax.optimization_barrier((by_distance, beside))
    other = swapped(jnp.stack(by_distance), "tm", 1)
    channels = width // 6
    out_shape = [jax.ShapeDtypeStruct((1, 2 * rows, cols), jnp.float32) for cols in (2 * channels, 2 * channels, channels, channels)]
    return local_call(functools.partial(final_kernel, places, scale), "place_sums", by_distance + [other], out_shape), beside


def stacked_body(signal, skip_cot, res_cot, w_tap, w_now, w_res, w_skip):
    sections = lax.axis_size("section")
    shards = lax.axis_size("tm")
    section = lax.axis_index("section")
    core = lax.axis_index("tm") % 2
    number, seq_rows, channels = signal.shape
    span = FIRST_DILATION // seq_rows

    tap = passed_along(lax.dynamic_index_in_dim(signal, section, 0, False), "tm", span)
    packed = jnp.concatenate([w_now[0], w_res[0], w_skip[0], w_tap[0]], axis=1)
    half_rows = packed.shape[0] // 2
    own_half = lax.dynamic_slice_in_dim(packed, core * half_rows, half_rows, 0)
    mine = [swapped(own_half, "section", by) for by in range(1, sections)]
    own_streams, other_streams = order_streams(signal, skip_cot, res_cot)
    tap, mine, own_streams, other_streams = lax.optimization_barrier((tap, mine, own_streams, other_streams))
    other = [swapped(piece, "tm", 1) for piece in mine]
    taps = [tap] + [swapped(tap, "section", by) for by in range(1, sections)]

    pieces = [w_now, w_res, w_skip, w_tap, *mine, *other]
    skip_total, grads, back, sums, weights = layer_stack(own_streams, taps[:1], number, pieces)
    back = passed_along(back, "tm", -span)
    skip_total, grads, sent, kept = layer_stack(other_streams, taps[1:], number, [weights], (skip_total, grads, sums))
    sent, back = lax.optimization_barrier((sent, back))
    reached = range(shards - span)
    arrived = [between(back, shards, [(by, 0)], reached) for by in range(1, sections)]
    grad_scale = 1.0 / math.sqrt(number * seq_rows * shards)
    input_grads = add_back(grads, [back, *arrived])
    summed, input_grads = sum_over_shards(sent, kept, shards // 2, grad_scale, input_grads)
    return (skip_total, input_grads[None], *summed)


def body(signal, skip_cot, res_cot, w_tap, w_now, w_res, w_skip):
    sections = lax.axis_size("section")
    shards = lax.axis_size("tm")
    number, seq_rows, channels = signal.shape
    span, beyond = divmod(FIRST_DILATION, seq_rows)
    one_live_tap = beyond == 0 and span < shards <= 2 * span
    square = w_res.shape[1:] == (channels, channels) and w_skip.shape[1:] == (channels, channels)
    pairs = sections == number == 4 and shards % 2 == 0 and shards & (shards - 1) == 0
    if one_live_tap and square and pairs:
        return stacked_body(signal, skip_cot, res_cot, w_tap, w_now, w_res, w_skip)
    return pipelined_body(signal, skip_cot, res_cot, w_tap, w_now, w_res, w_skip)


def solution(mesh):
    in_specs = (
        P(None, "tm", None),
        P(None, "tm", None),
        P(None, "tm", None),
        P("section", None, None),
        P("section", None, None),
        P("section", None, None),
        P("section", None, None),
    )
    out_specs = (
        P(None, "tm", None),
        P("section", None, "tm", None),
        P("section", None, None),
        P("section", None, None),
        P("section", None, None),
        P("section", None, None),
    )
    return jax.shard_map(body, mesh=mesh, in_specs=in_specs, out_specs=out_specs, check_vma=False)
```

```python
import functools
import math

import jax
import jax.numpy as jnp
from jax import lax
from jax.experimental import pallas as pl
from jax.experimental.pallas import tpu as pltpu
from jax.sharding import PartitionSpec as P

SPAN = 4
FIRST_DILATION = 2048


def passed_along(x, axis, by):
    size = lax.axis_size(axis)
    pairs = [(i, i + by) for i in range(size) if 0 <= i + by < size]
    return lax.ppermute(x, axis, pairs)


def flat_dot(left, right):
    result = jnp.dot(left.reshape(-1, left.shape[-1]), right, preferred_element_type=jnp.float32)
    return result.reshape(left.shape[:-1] + (right.shape[-1],))


def rows_spanning(left, right):
    return lax.dot_general(
        left.reshape(-1, left.shape[-1]),
        right.reshape(-1, right.shape[-1]),
        (((0,), (0,)), ((), ())),
        preferred_element_type=jnp.float32,
    )


def tap_rows(values, chosen, delayed):
    result = jnp.zeros_like(values)
    for layer_number, selected in chosen:
        if delayed:
            arrived = passed_along(values, "tm", SPAN << layer_number)
        else:
            arrived = passed_along(values, "tm", -(SPAN << layer_number))
        result = jnp.where(selected, arrived, result)
    return result


def gate_parts(tapped, layer_in, weights):
    pre = flat_dot(tapped, weights[0]) + flat_dot(layer_in, weights[1])
    half_width = pre.shape[-1] // 2
    return (jnp.tanh(pre[..., :half_width]), jax.nn.sigmoid(pre[..., half_width:]))


def layer_forward(layer_in, weights, chosen):
    tapped = tap_rows(layer_in, chosen, True)
    tanh_part, sigmoid_part = gate_parts(tapped, layer_in, weights)
    gated = (tanh_part * sigmoid_part).astype(jnp.bfloat16)
    stream_out = (layer_in.astype(jnp.float32) + flat_dot(gated, weights[2])).astype(jnp.bfloat16)
    return (tapped, stream_out, flat_dot(gated, weights[3]))


def layer_backward(layer_in, tapped, grad_out, skip_grad, weights, chosen):
    tanh_part, sigmoid_part = gate_parts(tapped, layer_in, weights)
    gated = (tanh_part * sigmoid_part).astype(jnp.bfloat16)
    grad_gated = flat_dot(grad_out, weights[2].T) + flat_dot(skip_grad, weights[3].T)
    grad_pre = jnp.concatenate(
        [
            grad_gated * sigmoid_part * (1.0 - tanh_part * tanh_part),
            grad_gated * tanh_part * sigmoid_part * (1.0 - sigmoid_part),
        ],
        axis=-1,
    ).astype(jnp.bfloat16)
    terms = (
        rows_spanning(tapped, grad_pre),
        rows_spanning(layer_in, grad_pre),
        rows_spanning(gated, grad_out),
        rows_spanning(gated, skip_grad),
    )
    back_term = flat_dot(grad_pre, weights[0].T).astype(jnp.bfloat16)
    arrived = tap_rows(back_term, chosen, False)
    grad_in = (
        grad_out.astype(jnp.float32)
        + flat_dot(grad_pre, weights[1].T)
        + arrived.astype(jnp.float32)
    )
    return (grad_in.astype(jnp.bfloat16), terms)


def keep_slot(holding_rows, micro_index, in_range, value):
    former = lax.dynamic_slice_in_dim(holding_rows, micro_index, 1, 0)
    return lax.dynamic_update_slice_in_dim(
        holding_rows, jnp.where(in_range, value, former), micro_index, 0
    )


def run_layers(signal, skip_cot, res_cot, w_tap, w_now, w_res, w_skip, section_index, sections):
    number, seq_rows, channels = signal.shape
    weights = (w_tap[0], w_now[0], w_res[0], w_skip[0])
    total_steps = number + sections - 1
    saved_in = jnp.zeros((number, seq_rows, channels), jnp.bfloat16)
    saved_tap = jnp.zeros((number, seq_rows, channels), jnp.bfloat16)
    skip_running_sum = jnp.zeros((number, seq_rows, w_skip.shape[2]), jnp.float32)
    received = jnp.zeros((1, seq_rows, channels), jnp.bfloat16)
    for moment in range(total_steps):
        chosen = [
            (layer_number, section_index == layer_number)
            for layer_number in range(sections)
            if 0 <= moment - layer_number < number
        ]
        position = moment - section_index
        in_range = (position >= 0) & (position < number)
        micro_index = jnp.clip(position, 0, number - 1)
        incoming = signal[min(moment, number - 1)][None]
        layer_in = jnp.where(section_index == 0, incoming, received)
        tapped, stream_out, skip_term = layer_forward(layer_in, weights, chosen)
        saved_in = keep_slot(saved_in, micro_index, in_range, layer_in)
        saved_tap = keep_slot(saved_tap, micro_index, in_range, tapped)
        skip_running_sum = keep_slot(skip_running_sum, micro_index, in_range, skip_term)
        if moment + 1 < total_steps:
            received = passed_along(stream_out, "section", 1)
    skip_total = lax.psum(skip_running_sum, "section").astype(jnp.bfloat16)
    partial_sums = [
        jnp.zeros(weights[0].shape, jnp.float32),
        jnp.zeros(weights[1].shape, jnp.float32),
        jnp.zeros(weights[2].shape, jnp.float32),
        jnp.zeros(weights[3].shape, jnp.float32),
    ]
    input_grads = jnp.zeros((number, seq_rows, channels), jnp.bfloat16)
    received = jnp.zeros((1, seq_rows, channels), jnp.bfloat16)
    for moment in range(total_steps):
        chosen = [
            (layer_number, section_index == layer_number)
            for layer_number in range(sections)
            if 0 <= moment - (sections - 1 - layer_number) < number
        ]
        position = moment - (sections - 1 - section_index)
        in_range = (position >= 0) & (position < number)
        micro_index = jnp.clip(position, 0, number - 1)
        top_grad = lax.dynamic_slice_in_dim(res_cot, micro_index, 1, 0)
        grad_out = jnp.where(section_index == sections - 1, top_grad, received)
        layer_in = lax.dynamic_slice_in_dim(saved_in, micro_index, 1, 0)
        tapped = lax.dynamic_slice_in_dim(saved_tap, micro_index, 1, 0)
        skip_grad = lax.dynamic_slice_in_dim(skip_cot, micro_index, 1, 0)
        grad_in, terms = layer_backward(layer_in, tapped, grad_out, skip_grad, weights, chosen)
        factor = in_range.astype(jnp.float32)
        partial_sums = [partial_sums[spot] + factor * terms[spot] for spot in range(4)]
        input_grads = keep_slot(input_grads, micro_index, in_range, grad_in)
        if moment + 1 < total_steps:
            received = passed_along(grad_in, "section", -1)
    return (skip_total, input_grads, tuple((part[None] for part in partial_sums)))


def pipelined_body(signal, skip_cot, res_cot, w_tap, w_now, w_res, w_skip):
    sections = lax.axis_size("section")
    shards = lax.axis_size("tm")
    section_index = lax.axis_index("section")
    number, seq_rows, channels = signal.shape
    skip_total, input_grads, partial_sums = run_layers(
        signal, skip_cot, res_cot, w_tap, w_now, w_res, w_skip, section_index, sections
    )
    summed = lax.psum((partial_sums[0], partial_sums[1], partial_sums[2], partial_sums[3]), "tm")
    grad_scale = 1.0 / math.sqrt(number * seq_rows * shards)
    return (
        skip_total,
        input_grads[None],
        summed[0] * grad_scale,
        summed[1] * grad_scale,
        summed[2] * grad_scale,
        summed[3] * grad_scale,
    )


def narrow_dot(left, right):
    return lax.dot_general(left, right, (((1,), (0,)), ((), ())), preferred_element_type=jnp.float32)


def rows_dot(left, right):
    return lax.dot_general(left, right, (((0,), (0,)), ((), ())), preferred_element_type=jnp.float32)


def turned_dot(left, right):
    return lax.dot_general(left, right, (((1,), (1,)), ((), ())), preferred_element_type=jnp.float32)


def skip_sum(gated, weights, columns):
    total = narrow_dot(gated[0], weights[0, :, columns])
    for k in range(1, len(gated)):
        total = total + narrow_dot(gated[k], weights[k, :, columns])
    return total.astype(jnp.bfloat16)


def finish_kernel(own_skip, gated_all, dz_all, g_all, weights, skip_out, base_out):
    section = lax.axis_index("section")
    layers, seqs, _, channels = gated_all.shape
    skip_out[section] = own_skip[...]
    above = jnp.maximum(section, 1)
    lowest = section == 0
    for i in range(seqs):
        at = jnp.bitwise_xor(section, i + 1)
        skip_out[at] = skip_sum([gated_all[k, i] for k in range(layers)], weights, slice(3 * channels, 4 * channels))
        below = turned_dot(dz_all[0, i], weights[0, :, : 2 * channels])
        base_out[i] = g_all[above, i].astype(jnp.float32) + jnp.where(lowest, below, 0.0)


def finish(own_skip, gated_all, dz_all, g_all, weights):
    layers, seqs, seq_rows, channels = gated_all.shape
    out_shape = [
        jax.ShapeDtypeStruct((layers, seq_rows, channels), jnp.bfloat16),
        jax.ShapeDtypeStruct((seqs, seq_rows, channels), jnp.float32),
    ]
    return local_call(finish_kernel, "finish", [own_skip, gated_all, dz_all, g_all, weights], out_shape)


def stack_kernel(layers, last, *refs):
    refs = list(refs)
    take = lambda count: [refs.pop(0) for _ in range(count)]
    signal, cot, res_cot = take(3)
    taps = take(layers - 1 if last else 1)
    if last:
        weights, sums_in, ahead_pre, ahead_du = take(4)
        gated_all, dz_all, g_all, *sent_outs, kept_out = take(6)
    else:
        own = take(4)
        mine = take(layers - 1)
        other = take(layers - 1)
        next_signal, next_cot = take(2)
        skip_out, grad_out, back_out, sums, weights, ahead_pre, ahead_du = take(7)
    early = layers - ahead_du.shape[0]
    tapped, h_all, tanh_all, sig_all = take(4)
    stream_here, tap_here = take(2)
    if last:
        (sums,) = take(1)
    else:
        gated_all, dz_all, g_all, weights_here = take(4)
    section = lax.axis_index("section")
    core = lax.rem(lax.axis_index("tm"), 2)
    _, seqs, seq_rows, channels = h_all.shape
    half = channels
    now = slice(0, 2 * half)
    res = slice(2 * half, 2 * half + channels)
    skip = slice(2 * half + channels, 2 * half + 2 * channels)
    tap = slice(2 * half + 2 * channels, 4 * half + 2 * channels)
    low_rows = channels // 2
    def wait_bytes(target, there):
        pltpu.make_async_copy(target, target, there).wait()

    if not last:
        for ref, cols in zip(own, (now, res, skip, tap)):
            pltpu.make_async_copy(ref.at[0], weights.at[section, :, cols], weights_here.at[section]).start()
        for by in range(1, layers):
            slot = jnp.bitwise_xor(section, by)
            for ref, side in ((mine[by - 1], core), (other[by - 1], 1 - core)):
                rows = pl.ds(pl.multiple_of(side * low_rows, low_rows), low_rows)
                pltpu.make_async_copy(ref, weights.at[slot, rows], weights_here.at[slot]).start()
    pltpu.make_async_copy(signal, h_all.at[0], stream_here.at[0]).start()
    for i, ref in enumerate(taps):
        pltpu.make_async_copy(ref, tapped.at[i], tap_here).start()
    pltpu.make_async_copy(res_cot, g_all.at[layers], stream_here.at[1]).start()

    wait_bytes(h_all.at[0], stream_here.at[0])
    for k in range(layers):
        if not last:
            wait_bytes(weights.at[k], weights_here.at[k])
        if k == 0:
            wait_bytes(tapped, tap_here)
        for i in range(seqs):
            if k == 0 and last:
                pre = ahead_pre[i] + narrow_dot(tapped[i], weights[0, :, tap])
            else:
                pre = narrow_dot(h_all[k, i], weights[k, :, now])
                if k == 0:
                    pre = pre + narrow_dot(tapped[i], weights[0, :, tap])
            tanh_part = jnp.tanh(pre[:, :half])
            sig_part = 0.5 * jnp.tanh(0.5 * pre[:, half:]) + 0.5
            tanh_all[k, i] = tanh_part
            sig_all[k, i] = sig_part
            gated_all[k, i] = (tanh_part * sig_part).astype(jnp.bfloat16)
        if k == 0 and not last:
            for i in range(layers - 1):
                ahead_pre[i] = narrow_dot(next_signal[i], weights[0, :, now])
        if k + 1 < layers:
            for i in range(seqs):
                stream = narrow_dot(gated_all[k, i], weights[k, :, res])
                h_all[k + 1, i] = (h_all[k, i].astype(jnp.float32) + stream).astype(jnp.bfloat16)
    wait_bytes(g_all.at[layers], stream_here.at[1])
    if not last:
        skip_out[...] = skip_sum([gated_all[k, 0] for k in range(layers)], weights, skip)
    for k in reversed(range(layers)):
        for i in range(seqs):
            du = turned_dot(g_all[k + 1, i], weights[k, :, res])
            if last and k >= early:
                du = du + ahead_du[k - early, i]
            else:
                du = du + turned_dot(cot[i], weights[k, :, skip])
            tanh_part = tanh_all[k, i]
            sig_part = sig_all[k, i]
            scaled = du * sig_part
            dz_all[k, i, :, :half] = (scaled * (1.0 - tanh_part * tanh_part)).astype(jnp.bfloat16)
            dz_all[k, i, :, half:] = (scaled * (tanh_part * (1.0 - sig_part))).astype(jnp.bfloat16)
        if k >= early and not last:
            for i in range(layers - 1):
                ahead_du[k - early, i] = turned_dot(next_cot[i], weights[k, :, skip])
        for i in range(seqs if k or not last else 0):
            below = turned_dot(dz_all[k, i], weights[k, :, now])
            g_all[k, i] = (g_all[k + 1, i].astype(jnp.float32) + below).astype(jnp.bfloat16)
    if not last:
        grad_out[...] = g_all[section, 0]
        back_out[...] = turned_dot(dz_all[0, 0], weights[0, :, tap]).astype(jnp.bfloat16)
    for i in range(seqs):
        products = (
            rows_dot(tapped[i], dz_all[section, i]),
            rows_dot(h_all[section, i], dz_all[section, i]),
            rows_dot(gated_all[section, i], g_all[section + 1, i]),
            rows_dot(gated_all[section, i], cot[i]),
        )
        spots = (slice(0, 2 * half), slice(2 * half, 4 * half), slice(4 * half, 4 * half + channels), slice(4 * half + channels, None))
        for spot, product in zip(spots, products):
            if i == 0 and last:
                sums[:, spot] = sums_in[:, spot] + product
            elif i == 0:
                sums[:, spot] = product
            else:
                sums[:, spot] += product
    if last:
        kept_out[...] = sums[pl.ds(pl.multiple_of(core * low_rows, low_rows), low_rows)]
        sent_rows = low_rows // len(sent_outs)
        for i, sent_out in enumerate(sent_outs):
            start = pl.multiple_of((1 - core) * low_rows + i * sent_rows, sent_rows)
            sent_out[...] = sums[pl.ds(start, sent_rows)].astype(jnp.bfloat16)


def layer_stack(streams, taps, number, weights, following=(), earlier=None):
    seqs, seq_rows, channels = streams[0].shape
    layers = number
    last = earlier is not None
    width = 6 * channels
    anywhere = pl.BlockSpec(memory_space=pl.ANY)
    near = pl.BlockSpec(memory_space=pltpu.VMEM)
    rows = lambda count, wide=1: ((count, seqs, seq_rows, wide * channels), jnp.bfloat16)
    kept = [rows(layers), rows(layers, 2), rows(layers + 1)]
    scratch = [
        pltpu.VMEM((seqs, seq_rows, channels), jnp.bfloat16),
        pltpu.VMEM(*rows(layers)),
        pltpu.VMEM((layers, seqs, seq_rows, channels), jnp.float32),
        pltpu.VMEM((layers, seqs, seq_rows, channels), jnp.float32),
        pltpu.SemaphoreType.DMA((2,)),
        pltpu.SemaphoreType.DMA,
    ]
    operands = [*streams, *taps, *weights]
    in_specs = [near] * 3 + [anywhere] * len(taps) + [near if last else anywhere] * len(weights)
    if last:
        operands += [*earlier]
        in_specs += [near] * len(earlier)
        shapes = kept + [((channels // 4, width), jnp.bfloat16)] * 2 + [((channels // 2, width), jnp.float32)]
        scratch += [pltpu.VMEM((channels, width), jnp.float32)]
    else:
        shapes = [((seq_rows, channels), jnp.bfloat16)] * 3
        shapes += [((channels, width), jnp.float32), ((layers, channels, width), jnp.bfloat16)]
        shapes += [((layers - 1, seq_rows, 2 * channels), jnp.float32)]
        shapes += [((2, layers - 1, seq_rows, channels), jnp.float32)]
        operands += [*following]
        in_specs += [near] * len(following)
        scratch += [pltpu.VMEM(*shape) for shape in kept] + [pltpu.SemaphoreType.DMA((layers,))]
    flops = 2 * 22 * layers * seqs * seq_rows * channels * channels
    return pl.pallas_call(
        functools.partial(stack_kernel, layers, last),
        in_specs=in_specs,
        out_specs=[near] * len(shapes),
        out_shape=[jax.ShapeDtypeStruct(*shape) for shape in shapes],
        scratch_shapes=scratch,
        compiler_params=pltpu.CompilerParams(vmem_limit_bytes=(24 if last else 20) * 2**20),
        cost_estimate=pl.CostEstimate(flops=flops, bytes_accessed=16 * seqs * seq_rows * channels, transcendentals=0),
        name="layer_stack",
    )(*operands)


def order_kernel(*refs):
    count = (len(refs) - 1) // 3
    sources, owns, others, sems = refs[:count], refs[count : 2 * count], refs[2 * count : 3 * count], refs[-1]
    section = lax.axis_index("section")
    copies = []
    for i, source in enumerate(sources):
        for by in range(source.shape[0]):
            target = owns[i].at[0] if by == 0 else others[i].at[by - 1]
            copies.append(pltpu.make_async_copy(source.at[jnp.bitwise_xor(section, by)], target, sems.at[i, by]))
    for copy in copies:
        copy.start()
    for copy in copies:
        copy.wait()


def order_streams(*streams):
    number, seq_rows, channels = streams[0].shape
    count = len(streams)
    anywhere = pl.BlockSpec(memory_space=pl.ANY)
    near = pl.BlockSpec(memory_space=pltpu.VMEM)
    shape = lambda seqs: jax.ShapeDtypeStruct((seqs, seq_rows, channels), jnp.bfloat16)
    ordered = pl.pallas_call(
        order_kernel,
        in_specs=[anywhere] * count,
        out_specs=[near] * 2 * count,
        out_shape=[shape(1)] * count + [shape(number - 1)] * count,
        scratch_shapes=[pltpu.SemaphoreType.DMA((count, number))],
        compiler_params=pltpu.CompilerParams(vmem_limit_bytes=8 * 2**20),
        cost_estimate=pl.CostEstimate(flops=0, bytes_accessed=2**24, transcendentals=0),
        name="order_streams",
    )(*streams)
    return ordered[:count], ordered[count:]


def spread_kernel(places, kept, got_low, got_high, own_out, *outs):
    place = lax.axis_index("tm") // 2
    piece_rows = own_out.shape[0]
    for by in range(places):
        rows = pl.ds(pl.multiple_of(jnp.bitwise_xor(place, by) * piece_rows, piece_rows), piece_rows)
        here = pl.ds(pl.multiple_of(lax.rem(jnp.bitwise_xor(place, by) * piece_rows, got_low.shape[0]), piece_rows), piece_rows)
        got = jnp.where(jnp.bitwise_xor(place, by) * piece_rows < got_low.shape[0], got_low[here], got_high[here])
        total = kept[rows] + got.astype(jnp.float32)
        if by == 0:
            own_out[...] = total
        else:
            outs[by - 1][...] = total.astype(jnp.bfloat16)


def final_kernel(places, scale, *refs):
    shard = lax.axis_index("tm")
    place, core = shard // 2, lax.rem(shard, 2)
    pieces, other, outs = refs[:places], refs[places], refs[places + 1 :]
    piece_rows = pieces[0].shape[0]
    live = jnp.where(lax.axis_index("section") == 0, scale, 0.0)
    for side, values in ((core, [ref[...] for ref in pieces]), (1 - core, [other[i] for i in range(places)])):
        for by, value in enumerate(values):
            at = (side * places + jnp.bitwise_xor(place, by)) * piece_rows
            rows = pl.ds(pl.multiple_of(at, piece_rows), piece_rows)
            value = value.astype(jnp.float32)
            column = 0
            for i, out in enumerate(outs):
                width = out.shape[2]
                out[0, rows, :] = value[:, column : column + width] * (live if i == 0 else scale)
                column += width


def add_kernel(own_base, base, *refs):
    *backs, out = refs
    section = lax.axis_index("section")
    own = jnp.where(section == 0, 1.0, 0.0)
    for i, back in enumerate(backs):
        term = back[...].astype(jnp.float32)
        total = base[i - 1] + term if i else own_base[...].astype(jnp.float32) + term * own
        out[0, jnp.bitwise_xor(section, i)] = total.astype(jnp.bfloat16)


def add_back(own_base, base, backs):
    shape = (1, len(backs), *own_base.shape)
    return local_call(add_kernel, "add_back", [own_base, base, *backs], [jax.ShapeDtypeStruct(shape, jnp.bfloat16)], 2**24)[0]


def local_call(kernel, name, operands, out_shape, weight=0):
    near = pl.BlockSpec(memory_space=pltpu.VMEM)
    return pl.pallas_call(
        kernel,
        in_specs=[near] * len(operands),
        out_specs=[near] * len(out_shape),
        out_shape=[jax.ShapeDtypeStruct(value.shape, value.dtype) for value in out_shape],
        compiler_params=pltpu.CompilerParams(vmem_limit_bytes=12 * 2**20),
        cost_estimate=pl.CostEstimate(flops=0, bytes_accessed=weight, transcendentals=0) if weight else None,
        name=name,
    )(*operands)


def swapped(x, axis, by):
    return lax.ppermute(x, axis, [(i, i ^ by) for i in range(lax.axis_size(axis))])


def between(x, shards, pairs, reached):
    return lax.ppermute(x, ("section", "tm"), [(i * shards + t, j * shards + t) for i, j in pairs for t in reached])


def spread(got, kept, places):
    rows, width = kept.shape
    piece = (rows // places, width)
    narrow = jax.ShapeDtypeStruct(piece, jnp.bfloat16)
    own, *pieces = local_call(
        functools.partial(spread_kernel, places), "spread", [kept, *got],
        [jax.ShapeDtypeStruct(piece, jnp.float32)] + [narrow] * (places - 1),
    )
    return own, pieces


def sum_over_chips(own, pieces, scale, beside):
    rows, width = own.shape
    places = len(pieces) + 1
    arrived = [swapped(value, "tm", 2 * (by + 1)) for by, value in enumerate(pieces)]
    total = sum([value.astype(jnp.float32) for value in arrived], own).astype(jnp.bfloat16)
    by_distance = [total] + [swapped(total, "tm", 2 * by) for by in range(1, places)]
    by_distance, beside = lax.optimization_barrier((by_distance, beside))
    other = swapped(jnp.stack(by_distance), "tm", 1)
    channels = width // 6
    out_shape = [jax.ShapeDtypeStruct((1, 2 * places * rows, cols), jnp.float32) for cols in (2 * channels, 2 * channels, channels, channels)]
    return local_call(functools.partial(final_kernel, places, scale), "place_sums", by_distance + [other], out_shape), beside


def stacked_body(signal, skip_cot, res_cot, w_tap, w_now, w_res, w_skip):
    sections = lax.axis_size("section")
    shards = lax.axis_size("tm")
    section = lax.axis_index("section")
    core = lax.axis_index("tm") % 2
    number, seq_rows, channels = signal.shape
    span = FIRST_DILATION // seq_rows

    tap = passed_along(lax.dynamic_index_in_dim(signal, section, 0, False), "tm", span)
    packed = jnp.concatenate([w_now[0], w_res[0], w_skip[0], w_tap[0]], axis=1)
    half_rows = packed.shape[0] // 2
    own_half = lax.dynamic_slice_in_dim(packed, core * half_rows, half_rows, 0)
    mine = [swapped(own_half, "section", by) for by in range(1, sections)]
    own_streams, other_streams = order_streams(signal, skip_cot, res_cot)
    tap, mine, own_streams, other_streams = lax.optimization_barrier((tap, mine, own_streams, other_streams))
    other = [swapped(piece, "tm", 1) for piece in mine]
    taps = [tap] + [swapped(tap, "section", by) for by in range(1, sections)]

    pieces = [w_now, w_res, w_skip, w_tap, *mine, *other]
    following = other_streams[:2]
    own_skip, own_base, back, sums, weights, *ahead = layer_stack(own_streams, taps[:1], number, pieces, following)
    back = passed_along(back, "tm", -span)
    gated, dz, g, *sent, kept = layer_stack(other_streams, taps[1:], number, [weights], earlier=(sums, *ahead))
    got = [swapped(value, "tm", 1) for value in sent]
    own_piece, pieces = spread(got, kept, shards // 2)
    pieces, back = lax.optimization_barrier((pieces, back))
    reached = range(shards - span)
    arrived = [between(back, shards, [(by, 0)], reached) for by in range(1, sections)]
    grad_scale = 1.0 / math.sqrt(number * seq_rows * shards)
    skip_total, base = finish(own_skip, gated, dz, g, weights)
    input_grads = add_back(own_base, base, [back, *arrived])
    summed, input_grads = sum_over_chips(own_piece, pieces, grad_scale, input_grads)
    return (skip_total, input_grads, *summed)


def body(signal, skip_cot, res_cot, w_tap, w_now, w_res, w_skip):
    sections = lax.axis_size("section")
    shards = lax.axis_size("tm")
    number, seq_rows, channels = signal.shape
    span, beyond = divmod(FIRST_DILATION, seq_rows)
    one_live_tap = beyond == 0 and span < shards <= 2 * span
    square = w_res.shape[1:] == (channels, channels) and w_skip.shape[1:] == (channels, channels)
    pairs = sections == number == 4 and shards % 2 == 0 and shards & (shards - 1) == 0
    if one_live_tap and square and pairs:
        return stacked_body(signal, skip_cot, res_cot, w_tap, w_now, w_res, w_skip)
    return pipelined_body(signal, skip_cot, res_cot, w_tap, w_now, w_res, w_skip)


def solution(mesh):
    in_specs = (
        P(None, "tm", None),
        P(None, "tm", None),
        P(None, "tm", None),
        P("section", None, None),
        P("section", None, None),
        P("section", None, None),
        P("section", None, None),
    )
    out_specs = (
        P(None, "tm", None),
        P("section", None, "tm", None),
        P("section", None, None),
        P("section", None, None),
        P("section", None, None),
        P("section", None, None),
    )
    return jax.shard_map(body, mesh=mesh, in_specs=in_specs, out_specs=out_specs, check_vma=False)
```

```python
import functools
import math

import jax
import jax.numpy as jnp
from jax import lax
from jax.experimental import pallas as pl
from jax.experimental.pallas import tpu as pltpu
from jax.sharding import PartitionSpec as P

SPAN = 4
FIRST_DILATION = 2048


def passed_along(x, axis, by):
    size = lax.axis_size(axis)
    pairs = [(i, i + by) for i in range(size) if 0 <= i + by < size]
    return lax.ppermute(x, axis, pairs)


def flat_dot(left, right):
    result = jnp.dot(left.reshape(-1, left.shape[-1]), right, preferred_element_type=jnp.float32)
    return result.reshape(left.shape[:-1] + (right.shape[-1],))


def rows_spanning(left, right):
    return lax.dot_general(
        left.reshape(-1, left.shape[-1]),
        right.reshape(-1, right.shape[-1]),
        (((0,), (0,)), ((), ())),
        preferred_element_type=jnp.float32,
    )


def tap_rows(values, chosen, delayed):
    result = jnp.zeros_like(values)
    for layer_number, selected in chosen:
        if delayed:
            arrived = passed_along(values, "tm", SPAN << layer_number)
        else:
            arrived = passed_along(values, "tm", -(SPAN << layer_number))
        result = jnp.where(selected, arrived, result)
    return result


def gate_parts(tapped, layer_in, weights):
    pre = flat_dot(tapped, weights[0]) + flat_dot(layer_in, weights[1])
    half_width = pre.shape[-1] // 2
    return (jnp.tanh(pre[..., :half_width]), jax.nn.sigmoid(pre[..., half_width:]))


def layer_forward(layer_in, weights, chosen):
    tapped = tap_rows(layer_in, chosen, True)
    tanh_part, sigmoid_part = gate_parts(tapped, layer_in, weights)
    gated = (tanh_part * sigmoid_part).astype(jnp.bfloat16)
    stream_out = (layer_in.astype(jnp.float32) + flat_dot(gated, weights[2])).astype(jnp.bfloat16)
    return (tapped, stream_out, flat_dot(gated, weights[3]))


def layer_backward(layer_in, tapped, grad_out, skip_grad, weights, chosen):
    tanh_part, sigmoid_part = gate_parts(tapped, layer_in, weights)
    gated = (tanh_part * sigmoid_part).astype(jnp.bfloat16)
    grad_gated = flat_dot(grad_out, weights[2].T) + flat_dot(skip_grad, weights[3].T)
    grad_pre = jnp.concatenate(
        [
            grad_gated * sigmoid_part * (1.0 - tanh_part * tanh_part),
            grad_gated * tanh_part * sigmoid_part * (1.0 - sigmoid_part),
        ],
        axis=-1,
    ).astype(jnp.bfloat16)
    terms = (
        rows_spanning(tapped, grad_pre),
        rows_spanning(layer_in, grad_pre),
        rows_spanning(gated, grad_out),
        rows_spanning(gated, skip_grad),
    )
    back_term = flat_dot(grad_pre, weights[0].T).astype(jnp.bfloat16)
    arrived = tap_rows(back_term, chosen, False)
    grad_in = (
        grad_out.astype(jnp.float32)
        + flat_dot(grad_pre, weights[1].T)
        + arrived.astype(jnp.float32)
    )
    return (grad_in.astype(jnp.bfloat16), terms)


def keep_slot(holding_rows, micro_index, in_range, value):
    former = lax.dynamic_slice_in_dim(holding_rows, micro_index, 1, 0)
    return lax.dynamic_update_slice_in_dim(
        holding_rows, jnp.where(in_range, value, former), micro_index, 0
    )


def run_layers(signal, skip_cot, res_cot, w_tap, w_now, w_res, w_skip, section_index, sections):
    number, seq_rows, channels = signal.shape
    weights = (w_tap[0], w_now[0], w_res[0], w_skip[0])
    total_steps = number + sections - 1
    saved_in = jnp.zeros((number, seq_rows, channels), jnp.bfloat16)
    saved_tap = jnp.zeros((number, seq_rows, channels), jnp.bfloat16)
    skip_running_sum = jnp.zeros((number, seq_rows, w_skip.shape[2]), jnp.float32)
    received = jnp.zeros((1, seq_rows, channels), jnp.bfloat16)
    for moment in range(total_steps):
        chosen = [
            (layer_number, section_index == layer_number)
            for layer_number in range(sections)
            if 0 <= moment - layer_number < number
        ]
        position = moment - section_index
        in_range = (position >= 0) & (position < number)
        micro_index = jnp.clip(position, 0, number - 1)
        incoming = signal[min(moment, number - 1)][None]
        layer_in = jnp.where(section_index == 0, incoming, received)
        tapped, stream_out, skip_term = layer_forward(layer_in, weights, chosen)
        saved_in = keep_slot(saved_in, micro_index, in_range, layer_in)
        saved_tap = keep_slot(saved_tap, micro_index, in_range, tapped)
        skip_running_sum = keep_slot(skip_running_sum, micro_index, in_range, skip_term)
        if moment + 1 < total_steps:
            received = passed_along(stream_out, "section", 1)
    skip_total = lax.psum(skip_running_sum, "section").astype(jnp.bfloat16)
    partial_sums = [
        jnp.zeros(weights[0].shape, jnp.float32),
        jnp.zeros(weights[1].shape, jnp.float32),
        jnp.zeros(weights[2].shape, jnp.float32),
        jnp.zeros(weights[3].shape, jnp.float32),
    ]
    input_grads = jnp.zeros((number, seq_rows, channels), jnp.bfloat16)
    received = jnp.zeros((1, seq_rows, channels), jnp.bfloat16)
    for moment in range(total_steps):
        chosen = [
            (layer_number, section_index == layer_number)
            for layer_number in range(sections)
            if 0 <= moment - (sections - 1 - layer_number) < number
        ]
        position = moment - (sections - 1 - section_index)
        in_range = (position >= 0) & (position < number)
        micro_index = jnp.clip(position, 0, number - 1)
        top_grad = lax.dynamic_slice_in_dim(res_cot, micro_index, 1, 0)
        grad_out = jnp.where(section_index == sections - 1, top_grad, received)
        layer_in = lax.dynamic_slice_in_dim(saved_in, micro_index, 1, 0)
        tapped = lax.dynamic_slice_in_dim(saved_tap, micro_index, 1, 0)
        skip_grad = lax.dynamic_slice_in_dim(skip_cot, micro_index, 1, 0)
        grad_in, terms = layer_backward(layer_in, tapped, grad_out, skip_grad, weights, chosen)
        factor = in_range.astype(jnp.float32)
        partial_sums = [partial_sums[spot] + factor * terms[spot] for spot in range(4)]
        input_grads = keep_slot(input_grads, micro_index, in_range, grad_in)
        if moment + 1 < total_steps:
            received = passed_along(grad_in, "section", -1)
    return (skip_total, input_grads, tuple((part[None] for part in partial_sums)))


def pipelined_body(signal, skip_cot, res_cot, w_tap, w_now, w_res, w_skip):
    sections = lax.axis_size("section")
    shards = lax.axis_size("tm")
    section_index = lax.axis_index("section")
    number, seq_rows, channels = signal.shape
    skip_total, input_grads, partial_sums = run_layers(
        signal, skip_cot, res_cot, w_tap, w_now, w_res, w_skip, section_index, sections
    )
    summed = lax.psum((partial_sums[0], partial_sums[1], partial_sums[2], partial_sums[3]), "tm")
    grad_scale = 1.0 / math.sqrt(number * seq_rows * shards)
    return (
        skip_total,
        input_grads[None],
        summed[0] * grad_scale,
        summed[1] * grad_scale,
        summed[2] * grad_scale,
        summed[3] * grad_scale,
    )


def narrow_dot(left, right):
    return lax.dot_general(left, right, (((1,), (0,)), ((), ())), preferred_element_type=jnp.float32)


def rows_dot(left, right):
    return lax.dot_general(left, right, (((0,), (0,)), ((), ())), preferred_element_type=jnp.float32)


def turned_dot(left, right):
    return lax.dot_general(left, right, (((1,), (1,)), ((), ())), preferred_element_type=jnp.float32)


def skip_sum(gated, weights, columns):
    total = narrow_dot(gated[0], weights[0, :, columns])
    for k in range(1, len(gated)):
        total = total + narrow_dot(gated[k], weights[k, :, columns])
    return total.astype(jnp.bfloat16)


def finish_kernel(own_skip, gated_all, dz_all, g_all, weights, skip_out, base_out):
    section = lax.axis_index("section")
    layers, seqs, _, channels = gated_all.shape
    skip_out[section] = own_skip[...]
    above = jnp.maximum(section, 1)
    lowest = section == 0
    for i in range(seqs):
        at = jnp.bitwise_xor(section, i + 1)
        skip_out[at] = skip_sum([gated_all[k, i] for k in range(layers)], weights, slice(3 * channels, 4 * channels))
        below = turned_dot(dz_all[0, i], weights[0, :, : 2 * channels])
        base_out[i] = g_all[above, i].astype(jnp.float32) + jnp.where(lowest, below, 0.0)


def finish(own_skip, gated_all, dz_all, g_all, weights):
    layers, seqs, seq_rows, channels = gated_all.shape
    out_shape = [
        jax.ShapeDtypeStruct((layers, seq_rows, channels), jnp.bfloat16),
        jax.ShapeDtypeStruct((seqs, seq_rows, channels), jnp.float32),
    ]
    return local_call(finish_kernel, "finish", [own_skip, gated_all, dz_all, g_all, weights], out_shape)


def stack_kernel(layers, last, *refs):
    refs = list(refs)
    take = lambda count: [refs.pop(0) for _ in range(count)]
    signal, cot, res_cot = take(3)
    taps = take(layers - 1 if last else 1)
    if last:
        weights, sums_in, ahead_pre, ahead_du = take(4)
        gated_all, dz_all, g_all, *sent_outs, kept_out = take(6)
    else:
        own = take(4)
        mine = take(layers - 1)
        other = take(layers - 1)
        next_signal, next_cot, next_res = take(3)
        skip_out, grad_out, back_out, sums, weights, ahead_pre, ahead_du = take(7)
    early = layers - ahead_du.shape[0]
    tapped, h_all, tanh_all, sig_all = take(4)
    stream_here, tap_here = take(2)
    if last:
        (sums,) = take(1)
    else:
        gated_all, dz_all, g_all, weights_here = take(4)
    section = lax.axis_index("section")
    core = lax.rem(lax.axis_index("tm"), 2)
    _, seqs, seq_rows, channels = h_all.shape
    half = channels
    now = slice(0, 2 * half)
    res = slice(2 * half, 2 * half + channels)
    skip = slice(2 * half + channels, 2 * half + 2 * channels)
    tap = slice(2 * half + 2 * channels, 4 * half + 2 * channels)
    low_rows = channels // 2
    def wait_bytes(target, there):
        pltpu.make_async_copy(target, target, there).wait()

    if not last:
        for ref, cols in zip(own, (now, res, skip, tap)):
            pltpu.make_async_copy(ref.at[0], weights.at[section, :, cols], weights_here.at[section]).start()
        for by in range(1, layers):
            slot = jnp.bitwise_xor(section, by)
            for ref, side in ((mine[by - 1], core), (other[by - 1], 1 - core)):
                rows = pl.ds(pl.multiple_of(side * low_rows, low_rows), low_rows)
                pltpu.make_async_copy(ref, weights.at[slot, rows], weights_here.at[slot]).start()
    pltpu.make_async_copy(signal, h_all.at[0], stream_here.at[0]).start()
    for i, ref in enumerate(taps):
        pltpu.make_async_copy(ref, tapped.at[i], tap_here).start()
    pltpu.make_async_copy(res_cot, g_all.at[layers], stream_here.at[1]).start()

    wait_bytes(h_all.at[0], stream_here.at[0])
    for k in range(layers):
        if not last:
            wait_bytes(weights.at[k], weights_here.at[k])
        if k == 0:
            wait_bytes(tapped, tap_here)
        for i in range(seqs):
            if k == 0 and last:
                pre = ahead_pre[i] + narrow_dot(tapped[i], weights[0, :, tap])
            else:
                pre = narrow_dot(h_all[k, i], weights[k, :, now])
                if k == 0:
                    pre = pre + narrow_dot(tapped[i], weights[0, :, tap])
            tanh_part = jnp.tanh(pre[:, :half])
            sig_part = 0.5 * jnp.tanh(0.5 * pre[:, half:]) + 0.5
            tanh_all[k, i] = tanh_part
            sig_all[k, i] = sig_part
            gated_all[k, i] = (tanh_part * sig_part).astype(jnp.bfloat16)
        if k == 0 and not last:
            for i in range(layers - 1):
                ahead_pre[i] = narrow_dot(next_signal[i], weights[0, :, now])
        if k + 1 < layers:
            for i in range(seqs):
                stream = narrow_dot(gated_all[k, i], weights[k, :, res])
                h_all[k + 1, i] = (h_all[k, i].astype(jnp.float32) + stream).astype(jnp.bfloat16)
    wait_bytes(g_all.at[layers], stream_here.at[1])
    if not last:
        skip_out[...] = skip_sum([gated_all[k, 0] for k in range(layers)], weights, skip)
    for k in reversed(range(layers)):
        for i in range(seqs):
            if last and k == layers - 1:
                du = ahead_du[k - early, i]
            else:
                du = turned_dot(g_all[k + 1, i], weights[k, :, res])
                if last and k >= early:
                    du = du + ahead_du[k - early, i]
                else:
                    du = du + turned_dot(cot[i], weights[k, :, skip])
            tanh_part = tanh_all[k, i]
            sig_part = sig_all[k, i]
            scaled = du * sig_part
            dz_all[k, i, :, :half] = (scaled * (1.0 - tanh_part * tanh_part)).astype(jnp.bfloat16)
            dz_all[k, i, :, half:] = (scaled * (tanh_part * (1.0 - sig_part))).astype(jnp.bfloat16)
        if k >= early and not last:
            for i in range(layers - 1):
                du = turned_dot(next_cot[i], weights[k, :, skip])
                if k == layers - 1:
                    du = du + turned_dot(next_res[i], weights[k, :, res])
                ahead_du[k - early, i] = du
        for i in range(seqs if k or not last else 0):
            below = turned_dot(dz_all[k, i], weights[k, :, now])
            g_all[k, i] = (g_all[k + 1, i].astype(jnp.float32) + below).astype(jnp.bfloat16)
    if not last:
        grad_out[...] = g_all[section, 0]
        back_out[...] = turned_dot(dz_all[0, 0], weights[0, :, tap]).astype(jnp.bfloat16)
    for i in range(seqs):
        products = (
            rows_dot(tapped[i], dz_all[section, i]),
            rows_dot(h_all[section, i], dz_all[section, i]),
            rows_dot(gated_all[section, i], g_all[section + 1, i]),
            rows_dot(gated_all[section, i], cot[i]),
        )
        spots = (slice(0, 2 * half), slice(2 * half, 4 * half), slice(4 * half, 4 * half + channels), slice(4 * half + channels, None))
        for spot, product in zip(spots, products):
            if i == 0 and last:
                sums[:, spot] = sums_in[:, spot] + product
            elif i == 0:
                sums[:, spot] = product
            else:
                sums[:, spot] += product
    if last:
        kept_out[...] = sums[pl.ds(pl.multiple_of(core * low_rows, low_rows), low_rows)]
        sent_rows = low_rows // len(sent_outs)
        for i, sent_out in enumerate(sent_outs):
            start = pl.multiple_of((1 - core) * low_rows + i * sent_rows, sent_rows)
            sent_out[...] = sums[pl.ds(start, sent_rows)].astype(jnp.bfloat16)


def layer_stack(streams, taps, number, weights, following=(), earlier=None):
    seqs, seq_rows, channels = streams[0].shape
    layers = number
    last = earlier is not None
    width = 6 * channels
    anywhere = pl.BlockSpec(memory_space=pl.ANY)
    near = pl.BlockSpec(memory_space=pltpu.VMEM)
    rows = lambda count, wide=1: ((count, seqs, seq_rows, wide * channels), jnp.bfloat16)
    kept = [rows(layers), rows(layers, 2), rows(layers + 1)]
    scratch = [
        pltpu.VMEM((seqs, seq_rows, channels), jnp.bfloat16),
        pltpu.VMEM(*rows(layers)),
        pltpu.VMEM((layers, seqs, seq_rows, channels), jnp.float32),
        pltpu.VMEM((layers, seqs, seq_rows, channels), jnp.float32),
        pltpu.SemaphoreType.DMA((2,)),
        pltpu.SemaphoreType.DMA,
    ]
    operands = [*streams, *taps, *weights]
    in_specs = [near] * 3 + [anywhere] * len(taps) + [near if last else anywhere] * len(weights)
    if last:
        operands += [*earlier]
        in_specs += [near] * len(earlier)
        shapes = kept + [((channels // 4, width), jnp.bfloat16)] * 2 + [((channels // 2, width), jnp.float32)]
        scratch += [pltpu.VMEM((channels, width), jnp.float32)]
    else:
        shapes = [((seq_rows, channels), jnp.bfloat16)] * 3
        shapes += [((channels, width), jnp.float32), ((layers, channels, width), jnp.bfloat16)]
        shapes += [((layers - 1, seq_rows, 2 * channels), jnp.float32)]
        shapes += [((2, layers - 1, seq_rows, channels), jnp.float32)]
        operands += [*following]
        in_specs += [near] * len(following)
        scratch += [pltpu.VMEM(*shape) for shape in kept] + [pltpu.SemaphoreType.DMA((layers,))]
    flops = 2 * 22 * layers * seqs * seq_rows * channels * channels
    return pl.pallas_call(
        functools.partial(stack_kernel, layers, last),
        in_specs=in_specs,
        out_specs=[near] * len(shapes),
        out_shape=[jax.ShapeDtypeStruct(*shape) for shape in shapes],
        scratch_shapes=scratch,
        compiler_params=pltpu.CompilerParams(vmem_limit_bytes=(24 if last else 20) * 2**20),
        cost_estimate=pl.CostEstimate(flops=flops, bytes_accessed=16 * seqs * seq_rows * channels, transcendentals=0),
        name="layer_stack",
    )(*operands)


def order_kernel(*refs):
    count = (len(refs) - 1) // 3
    sources, owns, others, sems = refs[:count], refs[count : 2 * count], refs[2 * count : 3 * count], refs[-1]
    section = lax.axis_index("section")
    copies = []
    for i, source in enumerate(sources):
        for by in range(source.shape[0]):
            target = owns[i].at[0] if by == 0 else others[i].at[by - 1]
            copies.append(pltpu.make_async_copy(source.at[jnp.bitwise_xor(section, by)], target, sems.at[i, by]))
    for copy in copies:
        copy.start()
    for copy in copies:
        copy.wait()


def order_streams(*streams):
    number, seq_rows, channels = streams[0].shape
    count = len(streams)
    anywhere = pl.BlockSpec(memory_space=pl.ANY)
    near = pl.BlockSpec(memory_space=pltpu.VMEM)
    shape = lambda seqs: jax.ShapeDtypeStruct((seqs, seq_rows, channels), jnp.bfloat16)
    ordered = pl.pallas_call(
        order_kernel,
        in_specs=[anywhere] * count,
        out_specs=[near] * 2 * count,
        out_shape=[shape(1)] * count + [shape(number - 1)] * count,
        scratch_shapes=[pltpu.SemaphoreType.DMA((count, number))],
        compiler_params=pltpu.CompilerParams(vmem_limit_bytes=8 * 2**20),
        cost_estimate=pl.CostEstimate(flops=0, bytes_accessed=2**24, transcendentals=0),
        name="order_streams",
    )(*streams)
    return ordered[:count], ordered[count:]


def spread_kernel(places, kept, got_low, got_high, own_out, *outs):
    place = lax.axis_index("tm") // 2
    piece_rows = own_out.shape[0]
    for by in range(places):
        rows = pl.ds(pl.multiple_of(jnp.bitwise_xor(place, by) * piece_rows, piece_rows), piece_rows)
        here = pl.ds(pl.multiple_of(lax.rem(jnp.bitwise_xor(place, by) * piece_rows, got_low.shape[0]), piece_rows), piece_rows)
        got = jnp.where(jnp.bitwise_xor(place, by) * piece_rows < got_low.shape[0], got_low[here], got_high[here])
        total = kept[rows] + got.astype(jnp.float32)
        if by == 0:
            own_out[...] = total
        else:
            outs[by - 1][...] = total.astype(jnp.bfloat16)


def final_kernel(places, scale, *refs):
    shard = lax.axis_index("tm")
    place, core = shard // 2, lax.rem(shard, 2)
    pieces, other, outs = refs[:places], refs[places], refs[places + 1 :]
    piece_rows = pieces[0].shape[0]
    live = jnp.where(lax.axis_index("section") == 0, scale, 0.0)
    for side, values in ((core, [ref[...] for ref in pieces]), (1 - core, [other[i] for i in range(places)])):
        for by, value in enumerate(values):
            at = (side * places + jnp.bitwise_xor(place, by)) * piece_rows
            rows = pl.ds(pl.multiple_of(at, piece_rows), piece_rows)
            value = value.astype(jnp.float32)
            column = 0
            for i, out in enumerate(outs):
                width = out.shape[2]
                out[0, rows, :] = value[:, column : column + width] * (live if i == 0 else scale)
                column += width


def add_kernel(own_base, base, *refs):
    *backs, out = refs
    section = lax.axis_index("section")
    own = jnp.where(section == 0, 1.0, 0.0)
    for i, back in enumerate(backs):
        term = back[...].astype(jnp.float32)
        total = base[i - 1] + term if i else own_base[...].astype(jnp.float32) + term * own
        out[0, jnp.bitwise_xor(section, i)] = total.astype(jnp.bfloat16)


def add_back(own_base, base, backs):
    shape = (1, len(backs), *own_base.shape)
    return local_call(add_kernel, "add_back", [own_base, base, *backs], [jax.ShapeDtypeStruct(shape, jnp.bfloat16)], 2**24)[0]


def local_call(kernel, name, operands, out_shape, weight=0):
    near = pl.BlockSpec(memory_space=pltpu.VMEM)
    return pl.pallas_call(
        kernel,
        in_specs=[near] * len(operands),
        out_specs=[near] * len(out_shape),
        out_shape=[jax.ShapeDtypeStruct(value.shape, value.dtype) for value in out_shape],
        compiler_params=pltpu.CompilerParams(vmem_limit_bytes=12 * 2**20),
        cost_estimate=pl.CostEstimate(flops=0, bytes_accessed=weight, transcendentals=0) if weight else None,
        name=name,
    )(*operands)


def swapped(x, axis, by):
    return lax.ppermute(x, axis, [(i, i ^ by) for i in range(lax.axis_size(axis))])


def between(x, shards, pairs, reached):
    return lax.ppermute(x, ("section", "tm"), [(i * shards + t, j * shards + t) for i, j in pairs for t in reached])


def spread(got, kept, places):
    rows, width = kept.shape
    piece = (rows // places, width)
    narrow = jax.ShapeDtypeStruct(piece, jnp.bfloat16)
    own, *pieces = local_call(
        functools.partial(spread_kernel, places), "spread", [kept, *got],
        [jax.ShapeDtypeStruct(piece, jnp.float32)] + [narrow] * (places - 1),
    )
    return own, pieces


def sum_over_chips(own, pieces, scale, beside):
    rows, width = own.shape
    places = len(pieces) + 1
    arrived = [swapped(value, "tm", 2 * (by + 1)) for by, value in reversed(list(enumerate(pieces)))]
    total = sum([value.astype(jnp.float32) for value in arrived], own).astype(jnp.bfloat16)
    by_distance = [total] + [swapped(total, "tm", 2 * by) for by in range(1, places)]
    by_distance, beside = lax.optimization_barrier((by_distance, beside))
    other = swapped(jnp.stack(by_distance), "tm", 1)
    channels = width // 6
    out_shape = [jax.ShapeDtypeStruct((1, 2 * places * rows, cols), jnp.float32) for cols in (2 * channels, 2 * channels, channels, channels)]
    return local_call(functools.partial(final_kernel, places, scale), "place_sums", by_distance + [other], out_shape), beside


def stacked_body(signal, skip_cot, res_cot, w_tap, w_now, w_res, w_skip):
    sections = lax.axis_size("section")
    shards = lax.axis_size("tm")
    section = lax.axis_index("section")
    core = lax.axis_index("tm") % 2
    number, seq_rows, channels = signal.shape
    span = FIRST_DILATION // seq_rows

    tap = passed_along(lax.dynamic_index_in_dim(signal, section, 0, False), "tm", span)
    packed = jnp.concatenate([w_now[0], w_res[0], w_skip[0], w_tap[0]], axis=1)
    half_rows = packed.shape[0] // 2
    own_half = lax.dynamic_slice_in_dim(packed, core * half_rows, half_rows, 0)
    mine = [swapped(own_half, "section", by) for by in range(1, sections)]
    own_streams, other_streams = order_streams(signal, skip_cot, res_cot)
    tap, mine, own_streams, other_streams = lax.optimization_barrier((tap, mine, own_streams, other_streams))
    other = [swapped(piece, "tm", 1) for piece in mine]
    taps = [tap] + [swapped(tap, "section", by) for by in range(1, sections)]

    pieces = [w_now, w_res, w_skip, w_tap, *mine, *other]
    own_skip, own_base, back, sums, weights, *ahead = layer_stack(own_streams, taps[:1], number, pieces, other_streams)
    back = passed_along(back, "tm", -span)
    gated, dz, g, *sent, kept = layer_stack(other_streams, taps[1:], number, [weights], earlier=(sums, *ahead))
    got = [swapped(value, "tm", 1) for value in sent]
    own_piece, pieces = spread(got, kept, shards // 2)
    pieces, back = lax.optimization_barrier((pieces, back))
    reached = range(shards - span)
    arrived = [between(back, shards, [(by, 0)], reached) for by in range(1, sections)]
    grad_scale = 1.0 / math.sqrt(number * seq_rows * shards)
    skip_total, base = finish(own_skip, gated, dz, g, weights)
    input_grads = add_back(own_base, base, [back, *arrived])
    summed, input_grads = sum_over_chips(own_piece, pieces, grad_scale, input_grads)
    return (skip_total, input_grads, *summed)


def body(signal, skip_cot, res_cot, w_tap, w_now, w_res, w_skip):
    sections = lax.axis_size("section")
    shards = lax.axis_size("tm")
    number, seq_rows, channels = signal.shape
    span, beyond = divmod(FIRST_DILATION, seq_rows)
    one_live_tap = beyond == 0 and span < shards <= 2 * span
    square = w_res.shape[1:] == (channels, channels) and w_skip.shape[1:] == (channels, channels)
    pairs = sections == number == 4 and shards % 2 == 0 and shards & (shards - 1) == 0
    if one_live_tap and square and pairs:
        return stacked_body(signal, skip_cot, res_cot, w_tap, w_now, w_res, w_skip)
    return pipelined_body(signal, skip_cot, res_cot, w_tap, w_now, w_res, w_skip)


def solution(mesh):
    in_specs = (
        P(None, "tm", None),
        P(None, "tm", None),
        P(None, "tm", None),
        P("section", None, None),
        P("section", None, None),
        P("section", None, None),
        P("section", None, None),
    )
    out_specs = (
        P(None, "tm", None),
        P("section", None, "tm", None),
        P("section", None, None),
        P("section", None, None),
        P("section", None, None),
        P("section", None, None),
    )
    return jax.shard_map(body, mesh=mesh, in_specs=in_specs, out_specs=out_specs, check_vma=False)
```

```python
import functools
import math

import jax
import jax.numpy as jnp
from jax import lax
from jax.experimental import pallas as pl
from jax.experimental.pallas import tpu as pltpu
from jax.sharding import PartitionSpec as P

SPAN = 4
FIRST_DILATION = 2048


def passed_along(x, axis, by):
    size = lax.axis_size(axis)
    pairs = [(i, i + by) for i in range(size) if 0 <= i + by < size]
    return lax.ppermute(x, axis, pairs)


def flat_dot(left, right):
    result = jnp.dot(left.reshape(-1, left.shape[-1]), right, preferred_element_type=jnp.float32)
    return result.reshape(left.shape[:-1] + (right.shape[-1],))


def rows_spanning(left, right):
    return lax.dot_general(
        left.reshape(-1, left.shape[-1]),
        right.reshape(-1, right.shape[-1]),
        (((0,), (0,)), ((), ())),
        preferred_element_type=jnp.float32,
    )


def tap_rows(values, chosen, delayed):
    result = jnp.zeros_like(values)
    for layer_number, selected in chosen:
        if delayed:
            arrived = passed_along(values, "tm", SPAN << layer_number)
        else:
            arrived = passed_along(values, "tm", -(SPAN << layer_number))
        result = jnp.where(selected, arrived, result)
    return result


def gate_parts(tapped, layer_in, weights):
    pre = flat_dot(tapped, weights[0]) + flat_dot(layer_in, weights[1])
    half_width = pre.shape[-1] // 2
    return (jnp.tanh(pre[..., :half_width]), jax.nn.sigmoid(pre[..., half_width:]))


def layer_forward(layer_in, weights, chosen):
    tapped = tap_rows(layer_in, chosen, True)
    tanh_part, sigmoid_part = gate_parts(tapped, layer_in, weights)
    gated = (tanh_part * sigmoid_part).astype(jnp.bfloat16)
    stream_out = (layer_in.astype(jnp.float32) + flat_dot(gated, weights[2])).astype(jnp.bfloat16)
    return (tapped, stream_out, flat_dot(gated, weights[3]))


def layer_backward(layer_in, tapped, grad_out, skip_grad, weights, chosen):
    tanh_part, sigmoid_part = gate_parts(tapped, layer_in, weights)
    gated = (tanh_part * sigmoid_part).astype(jnp.bfloat16)
    grad_gated = flat_dot(grad_out, weights[2].T) + flat_dot(skip_grad, weights[3].T)
    grad_pre = jnp.concatenate(
        [
            grad_gated * sigmoid_part * (1.0 - tanh_part * tanh_part),
            grad_gated * tanh_part * sigmoid_part * (1.0 - sigmoid_part),
        ],
        axis=-1,
    ).astype(jnp.bfloat16)
    terms = (
        rows_spanning(tapped, grad_pre),
        rows_spanning(layer_in, grad_pre),
        rows_spanning(gated, grad_out),
        rows_spanning(gated, skip_grad),
    )
    back_term = flat_dot(grad_pre, weights[0].T).astype(jnp.bfloat16)
    arrived = tap_rows(back_term, chosen, False)
    grad_in = (
        grad_out.astype(jnp.float32)
        + flat_dot(grad_pre, weights[1].T)
        + arrived.astype(jnp.float32)
    )
    return (grad_in.astype(jnp.bfloat16), terms)


def keep_slot(holding_rows, micro_index, in_range, value):
    former = lax.dynamic_slice_in_dim(holding_rows, micro_index, 1, 0)
    return lax.dynamic_update_slice_in_dim(
        holding_rows, jnp.where(in_range, value, former), micro_index, 0
    )


def run_layers(signal, skip_cot, res_cot, w_tap, w_now, w_res, w_skip, section_index, sections):
    number, seq_rows, channels = signal.shape
    weights = (w_tap[0], w_now[0], w_res[0], w_skip[0])
    total_steps = number + sections - 1
    saved_in = jnp.zeros((number, seq_rows, channels), jnp.bfloat16)
    saved_tap = jnp.zeros((number, seq_rows, channels), jnp.bfloat16)
    skip_running_sum = jnp.zeros((number, seq_rows, w_skip.shape[2]), jnp.float32)
    received = jnp.zeros((1, seq_rows, channels), jnp.bfloat16)
    for moment in range(total_steps):
        chosen = [
            (layer_number, section_index == layer_number)
            for layer_number in range(sections)
            if 0 <= moment - layer_number < number
        ]
        position = moment - section_index
        in_range = (position >= 0) & (position < number)
        micro_index = jnp.clip(position, 0, number - 1)
        incoming = signal[min(moment, number - 1)][None]
        layer_in = jnp.where(section_index == 0, incoming, received)
        tapped, stream_out, skip_term = layer_forward(layer_in, weights, chosen)
        saved_in = keep_slot(saved_in, micro_index, in_range, layer_in)
        saved_tap = keep_slot(saved_tap, micro_index, in_range, tapped)
        skip_running_sum = keep_slot(skip_running_sum, micro_index, in_range, skip_term)
        if moment + 1 < total_steps:
            received = passed_along(stream_out, "section", 1)
    skip_total = lax.psum(skip_running_sum, "section").astype(jnp.bfloat16)
    partial_sums = [
        jnp.zeros(weights[0].shape, jnp.float32),
        jnp.zeros(weights[1].shape, jnp.float32),
        jnp.zeros(weights[2].shape, jnp.float32),
        jnp.zeros(weights[3].shape, jnp.float32),
    ]
    input_grads = jnp.zeros((number, seq_rows, channels), jnp.bfloat16)
    received = jnp.zeros((1, seq_rows, channels), jnp.bfloat16)
    for moment in range(total_steps):
        chosen = [
            (layer_number, section_index == layer_number)
            for layer_number in range(sections)
            if 0 <= moment - (sections - 1 - layer_number) < number
        ]
        position = moment - (sections - 1 - section_index)
        in_range = (position >= 0) & (position < number)
        micro_index = jnp.clip(position, 0, number - 1)
        top_grad = lax.dynamic_slice_in_dim(res_cot, micro_index, 1, 0)
        grad_out = jnp.where(section_index == sections - 1, top_grad, received)
        layer_in = lax.dynamic_slice_in_dim(saved_in, micro_index, 1, 0)
        tapped = lax.dynamic_slice_in_dim(saved_tap, micro_index, 1, 0)
        skip_grad = lax.dynamic_slice_in_dim(skip_cot, micro_index, 1, 0)
        grad_in, terms = layer_backward(layer_in, tapped, grad_out, skip_grad, weights, chosen)
        factor = in_range.astype(jnp.float32)
        partial_sums = [partial_sums[spot] + factor * terms[spot] for spot in range(4)]
        input_grads = keep_slot(input_grads, micro_index, in_range, grad_in)
        if moment + 1 < total_steps:
            received = passed_along(grad_in, "section", -1)
    return (skip_total, input_grads, tuple((part[None] for part in partial_sums)))


def pipelined_body(signal, skip_cot, res_cot, w_tap, w_now, w_res, w_skip):
    sections = lax.axis_size("section")
    shards = lax.axis_size("tm")
    section_index = lax.axis_index("section")
    number, seq_rows, channels = signal.shape
    skip_total, input_grads, partial_sums = run_layers(
        signal, skip_cot, res_cot, w_tap, w_now, w_res, w_skip, section_index, sections
    )
    summed = lax.psum((partial_sums[0], partial_sums[1], partial_sums[2], partial_sums[3]), "tm")
    grad_scale = 1.0 / math.sqrt(number * seq_rows * shards)
    return (
        skip_total,
        input_grads[None],
        summed[0] * grad_scale,
        summed[1] * grad_scale,
        summed[2] * grad_scale,
        summed[3] * grad_scale,
    )


def narrow_dot(left, right):
    return lax.dot_general(left, right, (((1,), (0,)), ((), ())), preferred_element_type=jnp.float32)


def rows_dot(left, right):
    return lax.dot_general(left, right, (((0,), (0,)), ((), ())), preferred_element_type=jnp.float32)


def turned_dot(left, right):
    return lax.dot_general(left, right, (((1,), (1,)), ((), ())), preferred_element_type=jnp.float32)


def skip_sum(gated, weights, columns):
    total = narrow_dot(gated[0], weights[0, :, columns])
    for k in range(1, len(gated)):
        total = total + narrow_dot(gated[k], weights[k, :, columns])
    return total.astype(jnp.bfloat16)


def finish_kernel(own_skip, gated_all, dz_all, g_all, weights, skip_out, base_out):
    section = lax.axis_index("section")
    layers, seqs, _, channels = gated_all.shape
    skip_out[section] = own_skip[...]
    above = jnp.maximum(section, 1)
    lowest = section == 0
    for i in range(seqs):
        at = jnp.bitwise_xor(section, i + 1)
        skip_out[at] = skip_sum([gated_all[k, i] for k in range(layers)], weights, slice(3 * channels, 4 * channels))
        below = turned_dot(dz_all[0, i], weights[0, :, : 2 * channels])
        base_out[i] = g_all[above, i].astype(jnp.float32) + jnp.where(lowest, below, 0.0)


def finish(own_skip, gated_all, dz_all, g_all, weights):
    layers, seqs, seq_rows, channels = gated_all.shape
    out_shape = [
        jax.ShapeDtypeStruct((layers, seq_rows, channels), jnp.bfloat16),
        jax.ShapeDtypeStruct((seqs, seq_rows, channels), jnp.float32),
    ]
    return local_call(finish_kernel, "finish", [own_skip, gated_all, dz_all, g_all, weights], out_shape)


def add_products(section, sums, sums_in, tapped, h_all, gated_all, dz_all, g_all, cot):
    channels = tapped.shape[-1]
    for i in range(tapped.shape[0]):
        products = (
            rows_dot(tapped[i], dz_all[section, i]),
            rows_dot(h_all[section, i], dz_all[section, i]),
            rows_dot(gated_all[section, i], g_all[section + 1, i]),
            rows_dot(gated_all[section, i], cot[i]),
        )
        column = 0
        for product in products:
            spot = slice(column, column + product.shape[1])
            column += product.shape[1]
            if i:
                sums[:, spot] += product
            else:
                sums[:, spot] = sums_in[:, spot] + product if sums_in is not None else product


def ahead_kernel(tapped, cot, h_all, gated_all, dz_all, g_all, weights, next_signal, next_cot, next_res, sums, ahead_pre, ahead_du):
    layers, _, _, channels = gated_all.shape
    half = channels
    early = layers - ahead_du.shape[0]
    section = lax.axis_index("section")
    add_products(section, sums, None, tapped, h_all, gated_all, dz_all, g_all, cot)
    for i in range(layers - 1):
        ahead_pre[i] = narrow_dot(next_signal[i], weights[0, :, : 2 * half])
        for k in range(early, layers):
            du = turned_dot(next_cot[i], weights[k, :, 3 * half : 4 * half])
            if k == layers - 1:
                du = du + turned_dot(next_res[i], weights[k, :, 2 * half : 3 * half])
            ahead_du[k - early, i] = du


def ahead(tap, cot, kept, weights, following):
    layers, channels, width = weights.shape
    _, seq_rows, _ = cot.shape
    shapes = [(channels, width), (layers - 1, seq_rows, 2 * channels), (4, layers - 1, seq_rows, channels)]
    out_shape = [jax.ShapeDtypeStruct(shape, jnp.float32) for shape in shapes]
    return local_call(ahead_kernel, "ahead", [tap[None], cot, *kept, weights, *following], out_shape)


def stack_kernel(layers, last, *refs):
    refs = list(refs)
    take = lambda count: [refs.pop(0) for _ in range(count)]
    signal, cot, res_cot = take(3)
    taps = take(layers - 1 if last else 1)
    if last:
        weights, sums_in, ahead_pre, ahead_du = take(4)
        gated_all, dz_all, g_all, *sent_outs, kept_out = take(6)
    else:
        own = take(4)
        mine = take(layers - 1)
        other = take(layers - 1)
        skip_out, grad_out, back_out, weights, h_all, gated_all, dz_all, g_all = take(8)
    early = layers - ahead_du.shape[0] if last else layers
    if last:
        (h_all,) = take(1)
    tapped, tanh_all, sig_all = take(3)
    stream_here, tap_here = take(2)
    if last:
        (sums,) = take(1)
    else:
        (weights_here,) = take(1)
    section = lax.axis_index("section")
    core = lax.rem(lax.axis_index("tm"), 2)
    _, seqs, seq_rows, channels = h_all.shape
    half = channels
    now = slice(0, 2 * half)
    res = slice(2 * half, 2 * half + channels)
    skip = slice(2 * half + channels, 2 * half + 2 * channels)
    tap = slice(2 * half + 2 * channels, 4 * half + 2 * channels)
    low_rows = channels // 2
    def wait_bytes(target, there):
        pltpu.make_async_copy(target, target, there).wait()

    if not last:
        for ref, cols in zip(own, (now, res, skip, tap)):
            pltpu.make_async_copy(ref.at[0], weights.at[section, :, cols], weights_here.at[section]).start()
        for by in range(1, layers):
            slot = jnp.bitwise_xor(section, by)
            for ref, side in ((mine[by - 1], core), (other[by - 1], 1 - core)):
                rows = pl.ds(pl.multiple_of(side * low_rows, low_rows), low_rows)
                pltpu.make_async_copy(ref, weights.at[slot, rows], weights_here.at[slot]).start()
    pltpu.make_async_copy(signal, h_all.at[0], stream_here.at[0]).start()
    for i, ref in enumerate(taps):
        pltpu.make_async_copy(ref, tapped.at[i], tap_here).start()
    pltpu.make_async_copy(res_cot, g_all.at[layers], stream_here.at[1]).start()

    layer_in = lambda k, i: h_all[k, i] if k else signal[i]
    grad_out_of = lambda k, i: g_all[k + 1, i] if k + 1 < layers else res_cot[i]
    for k in range(layers):
        if not last:
            wait_bytes(weights.at[k], weights_here.at[k])
        for i in range(seqs):
            if k == 0 and last:
                pre = ahead_pre[i] + narrow_dot(taps[i][...], weights[0, :, tap])
            else:
                pre = narrow_dot(layer_in(k, i), weights[k, :, now])
                if k == 0:
                    pre = pre + narrow_dot(taps[i][...], weights[0, :, tap])
            tanh_part = jnp.tanh(pre[:, :half])
            sig_part = 0.5 * jnp.tanh(0.5 * pre[:, half:]) + 0.5
            tanh_all[k, i] = tanh_part
            sig_all[k, i] = sig_part
            gated_all[k, i] = (tanh_part * sig_part).astype(jnp.bfloat16)
        if k + 1 < layers:
            for i in range(seqs):
                stream = narrow_dot(gated_all[k, i], weights[k, :, res])
                h_all[k + 1, i] = (layer_in(k, i).astype(jnp.float32) + stream).astype(jnp.bfloat16)
    if not last:
        skip_out[...] = skip_sum([gated_all[k, 0] for k in range(layers)], weights, skip)
    for k in reversed(range(layers)):
        for i in range(seqs):
            if last and k == layers - 1:
                du = ahead_du[k - early, i]
            else:
                du = turned_dot(grad_out_of(k, i), weights[k, :, res])
                if last and k >= early:
                    du = du + ahead_du[k - early, i]
                else:
                    du = du + turned_dot(cot[i], weights[k, :, skip])
            tanh_part = tanh_all[k, i]
            sig_part = sig_all[k, i]
            scaled = du * sig_part
            dz_all[k, i, :, :half] = (scaled * (1.0 - tanh_part * tanh_part)).astype(jnp.bfloat16)
            dz_all[k, i, :, half:] = (scaled * (tanh_part * (1.0 - sig_part))).astype(jnp.bfloat16)
        for i in range(seqs if k or not last else 0):
            below = turned_dot(dz_all[k, i], weights[k, :, now])
            g_all[k, i] = (grad_out_of(k, i).astype(jnp.float32) + below).astype(jnp.bfloat16)
    wait_bytes(h_all.at[0], stream_here.at[0])
    wait_bytes(tapped, tap_here)
    wait_bytes(g_all.at[layers], stream_here.at[1])
    if not last:
        grad_out[...] = g_all[section, 0]
        back_out[...] = turned_dot(dz_all[0, 0], weights[0, :, tap]).astype(jnp.bfloat16)
    if last:
        add_products(section, sums, sums_in, tapped, h_all, gated_all, dz_all, g_all, cot)
    if last:
        kept_out[...] = sums[pl.ds(pl.multiple_of(core * low_rows, low_rows), low_rows)]
        sent_rows = low_rows // len(sent_outs)
        for i, sent_out in enumerate(sent_outs):
            start = pl.multiple_of((1 - core) * low_rows + i * sent_rows, sent_rows)
            sent_out[...] = sums[pl.ds(start, sent_rows)].astype(jnp.bfloat16)


def layer_stack(streams, taps, number, weights, earlier=None):
    seqs, seq_rows, channels = streams[0].shape
    layers = number
    last = earlier is not None
    width = 6 * channels
    anywhere = pl.BlockSpec(memory_space=pl.ANY)
    near = pl.BlockSpec(memory_space=pltpu.VMEM)
    rows = lambda count, wide=1: ((count, seqs, seq_rows, wide * channels), jnp.bfloat16)
    kept = [rows(layers), rows(layers, 2), rows(layers + 1)]
    scratch = [pltpu.VMEM(*rows(layers))] if last else []
    scratch += [
        pltpu.VMEM((seqs, seq_rows, channels), jnp.bfloat16),
        pltpu.VMEM((layers, seqs, seq_rows, channels), jnp.float32),
        pltpu.VMEM((layers, seqs, seq_rows, channels), jnp.float32),
        pltpu.SemaphoreType.DMA((2,)),
        pltpu.SemaphoreType.DMA,
    ]
    operands = [*streams, *taps, *weights]
    in_specs = [near] * (3 + len(taps)) + [near if last else anywhere] * len(weights)
    if last:
        operands += [*earlier]
        in_specs += [near] * len(earlier)
        shapes = kept + [((channels // 4, width), jnp.bfloat16)] * 2 + [((channels // 2, width), jnp.float32)]
        scratch += [pltpu.VMEM((channels, width), jnp.float32)]
    else:
        shapes = [((seq_rows, channels), jnp.bfloat16)] * 3 + [((layers, channels, width), jnp.bfloat16), rows(layers)] + kept
        scratch += [pltpu.SemaphoreType.DMA((layers,))]
    flops = 2 * 22 * layers * seqs * seq_rows * channels * channels
    return pl.pallas_call(
        functools.partial(stack_kernel, layers, last),
        in_specs=in_specs,
        out_specs=[near] * len(shapes),
        out_shape=[jax.ShapeDtypeStruct(*shape) for shape in shapes],
        scratch_shapes=scratch,
        compiler_params=pltpu.CompilerParams(vmem_limit_bytes=(21 if last else 18) * 2**20),
        cost_estimate=pl.CostEstimate(flops=flops, bytes_accessed=16 * seqs * seq_rows * channels, transcendentals=0),
        name="layer_stack",
    )(*operands)


def order_kernel(*refs):
    count = (len(refs) - 1) // 3
    sources, owns, others, sems = refs[:count], refs[count : 2 * count], refs[2 * count : 3 * count], refs[-1]
    section = lax.axis_index("section")
    copies = []
    for i, source in enumerate(sources):
        for by in range(source.shape[0]):
            target = owns[i].at[0] if by == 0 else others[i].at[by - 1]
            copies.append(pltpu.make_async_copy(source.at[jnp.bitwise_xor(section, by)], target, sems.at[i, by]))
    for copy in copies:
        copy.start()
    for copy in copies:
        copy.wait()


def order_streams(*streams):
    number, seq_rows, channels = streams[0].shape
    count = len(streams)
    anywhere = pl.BlockSpec(memory_space=pl.ANY)
    near = pl.BlockSpec(memory_space=pltpu.VMEM)
    shape = lambda seqs: jax.ShapeDtypeStruct((seqs, seq_rows, channels), jnp.bfloat16)
    ordered = pl.pallas_call(
        order_kernel,
        in_specs=[anywhere] * count,
        out_specs=[near] * 2 * count,
        out_shape=[shape(1)] * count + [shape(number - 1)] * count,
        scratch_shapes=[pltpu.SemaphoreType.DMA((count, number))],
        compiler_params=pltpu.CompilerParams(vmem_limit_bytes=8 * 2**20),
        cost_estimate=pl.CostEstimate(flops=0, bytes_accessed=2**24, transcendentals=0),
        name="order_streams",
    )(*streams)
    return ordered[:count], ordered[count:]


def spread_kernel(places, kept, got_low, got_high, own_out, *outs):
    place = lax.axis_index("tm") // 2
    piece_rows = own_out.shape[0]
    for by in range(places):
        rows = pl.ds(pl.multiple_of(jnp.bitwise_xor(place, by) * piece_rows, piece_rows), piece_rows)
        here = pl.ds(pl.multiple_of(lax.rem(jnp.bitwise_xor(place, by) * piece_rows, got_low.shape[0]), piece_rows), piece_rows)
        got = jnp.where(jnp.bitwise_xor(place, by) * piece_rows < got_low.shape[0], got_low[here], got_high[here])
        total = kept[rows] + got.astype(jnp.float32)
        if by == 0:
            own_out[...] = total
        else:
            outs[by - 1][...] = total.astype(jnp.bfloat16)


def final_kernel(places, scale, *refs):
    shard = lax.axis_index("tm")
    place, core = shard // 2, lax.rem(shard, 2)
    pieces, other, outs = refs[:places], refs[places], refs[places + 1 :]
    piece_rows = pieces[0].shape[0]
    live = jnp.where(lax.axis_index("section") == 0, scale, 0.0)
    for side, values in ((core, [ref[...] for ref in pieces]), (1 - core, [other[i] for i in range(places)])):
        for by, value in enumerate(values):
            at = (side * places + jnp.bitwise_xor(place, by)) * piece_rows
            rows = pl.ds(pl.multiple_of(at, piece_rows), piece_rows)
            value = value.astype(jnp.float32)
            column = 0
            for i, out in enumerate(outs):
                width = out.shape[2]
                out[0, rows, :] = value[:, column : column + width] * (live if i == 0 else scale)
                column += width


def add_kernel(own_base, base, *refs):
    *backs, out = refs
    section = lax.axis_index("section")
    own = jnp.where(section == 0, 1.0, 0.0)
    for i, back in enumerate(backs):
        term = back[...].astype(jnp.float32)
        total = base[i - 1] + term if i else own_base[...].astype(jnp.float32) + term * own
        out[0, jnp.bitwise_xor(section, i)] = total.astype(jnp.bfloat16)


def add_back(own_base, base, backs):
    shape = (1, len(backs), *own_base.shape)
    return local_call(add_kernel, "add_back", [own_base, base, *backs], [jax.ShapeDtypeStruct(shape, jnp.bfloat16)], 2**24)[0]


def local_call(kernel, name, operands, out_shape, weight=0):
    near = pl.BlockSpec(memory_space=pltpu.VMEM)
    return pl.pallas_call(
        kernel,
        in_specs=[near] * len(operands),
        out_specs=[near] * len(out_shape),
        out_shape=[jax.ShapeDtypeStruct(value.shape, value.dtype) for value in out_shape],
        compiler_params=pltpu.CompilerParams(vmem_limit_bytes=12 * 2**20),
        cost_estimate=pl.CostEstimate(flops=0, bytes_accessed=weight, transcendentals=0) if weight else None,
        name=name,
    )(*operands)


def swapped(x, axis, by):
    return lax.ppermute(x, axis, [(i, i ^ by) for i in range(lax.axis_size(axis))])


def between(x, shards, pairs, reached):
    return lax.ppermute(x, ("section", "tm"), [(i * shards + t, j * shards + t) for i, j in pairs for t in reached])


def spread(got, kept, places):
    rows, width = kept.shape
    piece = (rows // places, width)
    narrow = jax.ShapeDtypeStruct(piece, jnp.bfloat16)
    own, *pieces = local_call(
        functools.partial(spread_kernel, places), "spread", [kept, *got],
        [jax.ShapeDtypeStruct(piece, jnp.float32)] + [narrow] * (places - 1),
    )
    return own, pieces


def sum_over_chips(own, pieces, scale, beside):
    rows, width = own.shape
    places = len(pieces) + 1
    arrived = [swapped(value, "tm", 2 * (by + 1)) for by, value in reversed(list(enumerate(pieces)))]
    total = sum([value.astype(jnp.float32) for value in arrived], own).astype(jnp.bfloat16)
    by_distance = [total] + [swapped(total, "tm", 2 * by) for by in range(1, places)]
    by_distance, beside = lax.optimization_barrier((by_distance, beside))
    other = swapped(jnp.stack(by_distance), "tm", 1)
    channels = width // 6
    out_shape = [jax.ShapeDtypeStruct((1, 2 * places * rows, cols), jnp.float32) for cols in (2 * channels, 2 * channels, channels, channels)]
    return local_call(functools.partial(final_kernel, places, scale), "place_sums", by_distance + [other], out_shape), beside


def stacked_body(signal, skip_cot, res_cot, w_tap, w_now, w_res, w_skip):
    sections = lax.axis_size("section")
    shards = lax.axis_size("tm")
    section = lax.axis_index("section")
    core = lax.axis_index("tm") % 2
    number, seq_rows, channels = signal.shape
    span = FIRST_DILATION // seq_rows

    tap = passed_along(lax.dynamic_index_in_dim(signal, section, 0, False), "tm", span)
    packed = jnp.concatenate([w_now[0], w_res[0], w_skip[0], w_tap[0]], axis=1)
    half_rows = packed.shape[0] // 2
    own_half = lax.dynamic_slice_in_dim(packed, core * half_rows, half_rows, 0)
    mine = [swapped(own_half, "section", by) for by in range(1, sections)]
    own_streams, other_streams = order_streams(signal, skip_cot, res_cot)
    tap, mine, own_streams, other_streams = lax.optimization_barrier((tap, mine, own_streams, other_streams))
    other = [swapped(piece, "tm", 1) for piece in mine]
    taps = [tap] + [swapped(tap, "section", by) for by in range(1, sections)]

    pieces = [w_now, w_res, w_skip, w_tap, *mine, *other]
    own_skip, own_base, back, weights, *kept_own = layer_stack(own_streams, taps[:1], number, pieces)
    ahead_terms = ahead(taps[0], own_streams[1], kept_own, weights, other_streams)
    back = passed_along(back, "tm", -span)
    gated, dz, g, *sent, kept = layer_stack(other_streams, taps[1:], number, [weights], earlier=ahead_terms)
    got = [swapped(value, "tm", 1) for value in sent]
    own_piece, pieces = spread(got, kept, shards // 2)
    pieces, back = lax.optimization_barrier((pieces, back))
    reached = range(shards - span)
    arrived = [between(back, shards, [(by, 0)], reached) for by in range(1, sections)]
    grad_scale = 1.0 / math.sqrt(number * seq_rows * shards)
    skip_total, base = finish(own_skip, gated, dz, g, weights)
    input_grads = add_back(own_base, base, [back, *arrived])
    summed, input_grads = sum_over_chips(own_piece, pieces, grad_scale, input_grads)
    return (skip_total, input_grads, *summed)


def body(signal, skip_cot, res_cot, w_tap, w_now, w_res, w_skip):
    sections = lax.axis_size("section")
    shards = lax.axis_size("tm")
    number, seq_rows, channels = signal.shape
    span, beyond = divmod(FIRST_DILATION, seq_rows)
    one_live_tap = beyond == 0 and span < shards <= 2 * span
    square = w_res.shape[1:] == (channels, channels) and w_skip.shape[1:] == (channels, channels)
    pairs = sections == number == 4 and shards % 2 == 0 and shards & (shards - 1) == 0
    if one_live_tap and square and pairs:
        return stacked_body(signal, skip_cot, res_cot, w_tap, w_now, w_res, w_skip)
    return pipelined_body(signal, skip_cot, res_cot, w_tap, w_now, w_res, w_skip)


def solution(mesh):
    in_specs = (
        P(None, "tm", None),
        P(None, "tm", None),
        P(None, "tm", None),
        P("section", None, None),
        P("section", None, None),
        P("section", None, None),
        P("section", None, None),
    )
    out_specs = (
        P(None, "tm", None),
        P("section", None, "tm", None),
        P("section", None, None),
        P("section", None, None),
        P("section", None, None),
        P("section", None, None),
    )
    return jax.shard_map(body, mesh=mesh, in_specs=in_specs, out_specs=out_specs, check_vma=False)
```

```python
import functools
import math

import jax
import jax.numpy as jnp
from jax import lax
from jax.experimental import pallas as pl
from jax.experimental.pallas import tpu as pltpu
from jax.sharding import PartitionSpec as P

SPAN = 4
FIRST_DILATION = 2048


def passed_along(x, axis, by):
    size = lax.axis_size(axis)
    pairs = [(i, i + by) for i in range(size) if 0 <= i + by < size]
    return lax.ppermute(x, axis, pairs)


def flat_dot(left, right):
    result = jnp.dot(left.reshape(-1, left.shape[-1]), right, preferred_element_type=jnp.float32)
    return result.reshape(left.shape[:-1] + (right.shape[-1],))


def rows_spanning(left, right):
    return lax.dot_general(
        left.reshape(-1, left.shape[-1]),
        right.reshape(-1, right.shape[-1]),
        (((0,), (0,)), ((), ())),
        preferred_element_type=jnp.float32,
    )


def tap_rows(values, chosen, delayed):
    result = jnp.zeros_like(values)
    for layer_number, selected in chosen:
        if delayed:
            arrived = passed_along(values, "tm", SPAN << layer_number)
        else:
            arrived = passed_along(values, "tm", -(SPAN << layer_number))
        result = jnp.where(selected, arrived, result)
    return result


def gate_parts(tapped, layer_in, weights):
    pre = flat_dot(tapped, weights[0]) + flat_dot(layer_in, weights[1])
    half_width = pre.shape[-1] // 2
    return (jnp.tanh(pre[..., :half_width]), jax.nn.sigmoid(pre[..., half_width:]))


def layer_forward(layer_in, weights, chosen):
    tapped = tap_rows(layer_in, chosen, True)
    tanh_part, sigmoid_part = gate_parts(tapped, layer_in, weights)
    gated = (tanh_part * sigmoid_part).astype(jnp.bfloat16)
    stream_out = (layer_in.astype(jnp.float32) + flat_dot(gated, weights[2])).astype(jnp.bfloat16)
    return (tapped, stream_out, flat_dot(gated, weights[3]))


def layer_backward(layer_in, tapped, grad_out, skip_grad, weights, chosen):
    tanh_part, sigmoid_part = gate_parts(tapped, layer_in, weights)
    gated = (tanh_part * sigmoid_part).astype(jnp.bfloat16)
    grad_gated = flat_dot(grad_out, weights[2].T) + flat_dot(skip_grad, weights[3].T)
    grad_pre = jnp.concatenate(
        [
            grad_gated * sigmoid_part * (1.0 - tanh_part * tanh_part),
            grad_gated * tanh_part * sigmoid_part * (1.0 - sigmoid_part),
        ],
        axis=-1,
    ).astype(jnp.bfloat16)
    terms = (
        rows_spanning(tapped, grad_pre),
        rows_spanning(layer_in, grad_pre),
        rows_spanning(gated, grad_out),
        rows_spanning(gated, skip_grad),
    )
    back_term = flat_dot(grad_pre, weights[0].T).astype(jnp.bfloat16)
    arrived = tap_rows(back_term, chosen, False)
    grad_in = (
        grad_out.astype(jnp.float32)
        + flat_dot(grad_pre, weights[1].T)
        + arrived.astype(jnp.float32)
    )
    return (grad_in.astype(jnp.bfloat16), terms)


def keep_slot(holding_rows, micro_index, in_range, value):
    former = lax.dynamic_slice_in_dim(holding_rows, micro_index, 1, 0)
    return lax.dynamic_update_slice_in_dim(
        holding_rows, jnp.where(in_range, value, former), micro_index, 0
    )


def run_layers(signal, skip_cot, res_cot, w_tap, w_now, w_res, w_skip, section_index, sections):
    number, seq_rows, channels = signal.shape
    weights = (w_tap[0], w_now[0], w_res[0], w_skip[0])
    total_steps = number + sections - 1
    saved_in = jnp.zeros((number, seq_rows, channels), jnp.bfloat16)
    saved_tap = jnp.zeros((number, seq_rows, channels), jnp.bfloat16)
    skip_running_sum = jnp.zeros((number, seq_rows, w_skip.shape[2]), jnp.float32)
    received = jnp.zeros((1, seq_rows, channels), jnp.bfloat16)
    for moment in range(total_steps):
        chosen = [
            (layer_number, section_index == layer_number)
            for layer_number in range(sections)
            if 0 <= moment - layer_number < number
        ]
        position = moment - section_index
        in_range = (position >= 0) & (position < number)
        micro_index = jnp.clip(position, 0, number - 1)
        incoming = signal[min(moment, number - 1)][None]
        layer_in = jnp.where(section_index == 0, incoming, received)
        tapped, stream_out, skip_term = layer_forward(layer_in, weights, chosen)
        saved_in = keep_slot(saved_in, micro_index, in_range, layer_in)
        saved_tap = keep_slot(saved_tap, micro_index, in_range, tapped)
        skip_running_sum = keep_slot(skip_running_sum, micro_index, in_range, skip_term)
        if moment + 1 < total_steps:
            received = passed_along(stream_out, "section", 1)
    skip_total = lax.psum(skip_running_sum, "section").astype(jnp.bfloat16)
    partial_sums = [
        jnp.zeros(weights[0].shape, jnp.float32),
        jnp.zeros(weights[1].shape, jnp.float32),
        jnp.zeros(weights[2].shape, jnp.float32),
        jnp.zeros(weights[3].shape, jnp.float32),
    ]
    input_grads = jnp.zeros((number, seq_rows, channels), jnp.bfloat16)
    received = jnp.zeros((1, seq_rows, channels), jnp.bfloat16)
    for moment in range(total_steps):
        chosen = [
            (layer_number, section_index == layer_number)
            for layer_number in range(sections)
            if 0 <= moment - (sections - 1 - layer_number) < number
        ]
        position = moment - (sections - 1 - section_index)
        in_range = (position >= 0) & (position < number)
        micro_index = jnp.clip(position, 0, number - 1)
        top_grad = lax.dynamic_slice_in_dim(res_cot, micro_index, 1, 0)
        grad_out = jnp.where(section_index == sections - 1, top_grad, received)
        layer_in = lax.dynamic_slice_in_dim(saved_in, micro_index, 1, 0)
        tapped = lax.dynamic_slice_in_dim(saved_tap, micro_index, 1, 0)
        skip_grad = lax.dynamic_slice_in_dim(skip_cot, micro_index, 1, 0)
        grad_in, terms = layer_backward(layer_in, tapped, grad_out, skip_grad, weights, chosen)
        factor = in_range.astype(jnp.float32)
        partial_sums = [partial_sums[spot] + factor * terms[spot] for spot in range(4)]
        input_grads = keep_slot(input_grads, micro_index, in_range, grad_in)
        if moment + 1 < total_steps:
            received = passed_along(grad_in, "section", -1)
    return (skip_total, input_grads, tuple((part[None] for part in partial_sums)))


def pipelined_body(signal, skip_cot, res_cot, w_tap, w_now, w_res, w_skip):
    sections = lax.axis_size("section")
    shards = lax.axis_size("tm")
    section_index = lax.axis_index("section")
    number, seq_rows, channels = signal.shape
    skip_total, input_grads, partial_sums = run_layers(
        signal, skip_cot, res_cot, w_tap, w_now, w_res, w_skip, section_index, sections
    )
    summed = lax.psum((partial_sums[0], partial_sums[1], partial_sums[2], partial_sums[3]), "tm")
    grad_scale = 1.0 / math.sqrt(number * seq_rows * shards)
    return (
        skip_total,
        input_grads[None],
        summed[0] * grad_scale,
        summed[1] * grad_scale,
        summed[2] * grad_scale,
        summed[3] * grad_scale,
    )


def narrow_dot(left, right):
    return lax.dot_general(left, right, (((1,), (0,)), ((), ())), preferred_element_type=jnp.float32)


def rows_dot(left, right):
    return lax.dot_general(left, right, (((0,), (0,)), ((), ())), preferred_element_type=jnp.float32)


def turned_dot(left, right):
    return lax.dot_general(left, right, (((1,), (1,)), ((), ())), preferred_element_type=jnp.float32)


def skip_sum(gated, weights, columns):
    total = narrow_dot(gated[0], weights[0, :, columns])
    for k in range(1, len(gated)):
        total = total + narrow_dot(gated[k], weights[k, :, columns])
    return total.astype(jnp.bfloat16)


def finish_kernel(own_skip, gated_all, dz_all, g_all, weights, skip_out, base_out):
    section = lax.axis_index("section")
    layers, seqs, _, channels = gated_all.shape
    skip_out[section] = own_skip[...]
    above = jnp.maximum(section, 1)
    lowest = section == 0
    for i in range(seqs):
        at = jnp.bitwise_xor(section, i + 1)
        skip_out[at] = skip_sum([gated_all[k, i] for k in range(layers)], weights, slice(3 * channels, 4 * channels))
        below = turned_dot(dz_all[0, i], weights[0, :, : 2 * channels])
        base_out[i] = g_all[above, i].astype(jnp.float32) + jnp.where(lowest, below, 0.0)


def finish(own_skip, gated_all, dz_all, g_all, weights):
    layers, seqs, seq_rows, channels = gated_all.shape
    out_shape = [
        jax.ShapeDtypeStruct((layers, seq_rows, channels), jnp.bfloat16),
        jax.ShapeDtypeStruct((seqs, seq_rows, channels), jnp.float32),
    ]
    return local_call(finish_kernel, "finish", [own_skip, gated_all, dz_all, g_all, weights], out_shape)


def tap_factor(seq_rows):
    return jnp.where(lax.axis_index("tm") >= FIRST_DILATION // seq_rows, 1.0, 0.0)


def add_products(section, sums, sums_in, tapped, h_all, gated_all, dz_all, g_all, cot):
    channels = tapped.shape[-1]
    for i in range(tapped.shape[0]):
        products = (
            rows_dot(tapped[i], dz_all[section, i]) * tap_factor(tapped.shape[1]),
            rows_dot(h_all[section, i], dz_all[section, i]),
            rows_dot(gated_all[section, i], g_all[section + 1, i]),
            rows_dot(gated_all[section, i], cot[i]),
        )
        column = 0
        for product in products:
            spot = slice(column, column + product.shape[1])
            column += product.shape[1]
            if i:
                sums[:, spot] += product
            else:
                sums[:, spot] = sums_in[:, spot] + product if sums_in is not None else product


def ahead_kernel(tapped, cot, h_all, gated_all, dz_all, g_all, weights, next_signal, next_cot, next_res, sums, ahead_pre, ahead_du):
    layers, _, _, channels = gated_all.shape
    half = channels
    early = layers - ahead_du.shape[0]
    section = lax.axis_index("section")
    add_products(section, sums, None, tapped, h_all, gated_all, dz_all, g_all, cot)
    for i in range(layers - 1):
        ahead_pre[i] = narrow_dot(next_signal[i], weights[0, :, : 2 * half])
        for k in range(early, layers):
            du = turned_dot(next_cot[i], weights[k, :, 3 * half : 4 * half])
            if k == layers - 1:
                du = du + turned_dot(next_res[i], weights[k, :, 2 * half : 3 * half])
            ahead_du[k - early, i] = du


def ahead(tap, cot, kept, weights, following):
    layers, channels, width = weights.shape
    _, seq_rows, _ = cot.shape
    shapes = [(channels, width), (layers - 1, seq_rows, 2 * channels), (4, layers - 1, seq_rows, channels)]
    out_shape = [jax.ShapeDtypeStruct(shape, jnp.float32) for shape in shapes]
    return local_call(ahead_kernel, "ahead", [tap[None], cot, *kept, weights, *following], out_shape)


def stack_kernel(layers, last, *refs):
    refs = list(refs)
    take = lambda count: [refs.pop(0) for _ in range(count)]
    signal, cot, res_cot = take(3)
    taps = take(layers - 1 if last else 1)
    if last:
        weights, sums_in, ahead_pre, ahead_du = take(4)
        gated_all, dz_all, g_all, *sent_outs, kept_out = take(6)
    else:
        own = take(4)
        mine = take(layers - 1)
        other = take(layers - 1)
        skip_out, grad_out, back_out, weights, h_all, gated_all, dz_all, g_all = take(8)
    early = layers - ahead_du.shape[0] if last else layers
    if last:
        (h_all,) = take(1)
    tapped, tanh_all, sig_all = take(3)
    stream_here, tap_here = take(2)
    if last:
        (sums,) = take(1)
    else:
        (weights_here,) = take(1)
    section = lax.axis_index("section")
    core = lax.rem(lax.axis_index("tm"), 2)
    _, seqs, seq_rows, channels = h_all.shape
    half = channels
    now = slice(0, 2 * half)
    res = slice(2 * half, 2 * half + channels)
    skip = slice(2 * half + channels, 2 * half + 2 * channels)
    tap = slice(2 * half + 2 * channels, 4 * half + 2 * channels)
    low_rows = channels // 2
    def wait_bytes(target, there):
        pltpu.make_async_copy(target, target, there).wait()

    if not last:
        for ref, cols in zip(own, (now, res, skip, tap)):
            pltpu.make_async_copy(ref.at[0], weights.at[section, :, cols], weights_here.at[section]).start()
        for by in range(1, layers):
            slot = jnp.bitwise_xor(section, by)
            for ref, side in ((mine[by - 1], core), (other[by - 1], 1 - core)):
                rows = pl.ds(pl.multiple_of(side * low_rows, low_rows), low_rows)
                pltpu.make_async_copy(ref, weights.at[slot, rows], weights_here.at[slot]).start()
    pltpu.make_async_copy(signal, h_all.at[0], stream_here.at[0]).start()
    for i, ref in enumerate(taps):
        pltpu.make_async_copy(ref, tapped.at[i], tap_here).start()
    pltpu.make_async_copy(res_cot, g_all.at[layers], stream_here.at[1]).start()

    layer_in = lambda k, i: h_all[k, i] if k else signal[i]
    grad_out_of = lambda k, i: g_all[k + 1, i] if k + 1 < layers else res_cot[i]
    for k in range(layers):
        if not last:
            wait_bytes(weights.at[k], weights_here.at[k])
            if k == 0:
                weights[0, :, tap] = weights[0, :, tap] * tap_factor(seq_rows).astype(jnp.bfloat16)
        for i in range(seqs):
            if k == 0 and last:
                pre = ahead_pre[i] + narrow_dot(taps[i][...], weights[0, :, tap])
            else:
                pre = narrow_dot(layer_in(k, i), weights[k, :, now])
                if k == 0:
                    pre = pre + narrow_dot(taps[i][...], weights[0, :, tap])
            tanh_part = jnp.tanh(pre[:, :half])
            sig_part = 0.5 * jnp.tanh(0.5 * pre[:, half:]) + 0.5
            tanh_all[k, i] = tanh_part
            sig_all[k, i] = sig_part
            gated_all[k, i] = (tanh_part * sig_part).astype(jnp.bfloat16)
        if k + 1 < layers:
            for i in range(seqs):
                stream = narrow_dot(gated_all[k, i], weights[k, :, res])
                h_all[k + 1, i] = (layer_in(k, i).astype(jnp.float32) + stream).astype(jnp.bfloat16)
    if not last:
        skip_out[...] = skip_sum([gated_all[k, 0] for k in range(layers)], weights, skip)
    for k in reversed(range(layers)):
        for i in range(seqs):
            if last and k == layers - 1:
                du = ahead_du[k - early, i]
            else:
                du = turned_dot(grad_out_of(k, i), weights[k, :, res])
                if last and k >= early:
                    du = du + ahead_du[k - early, i]
                else:
                    du = du + turned_dot(cot[i], weights[k, :, skip])
            tanh_part = tanh_all[k, i]
            sig_part = sig_all[k, i]
            scaled = du * sig_part
            dz_all[k, i, :, :half] = (scaled * (1.0 - tanh_part * tanh_part)).astype(jnp.bfloat16)
            dz_all[k, i, :, half:] = (scaled * (tanh_part * (1.0 - sig_part))).astype(jnp.bfloat16)
        for i in range(seqs if k or not last else 0):
            below = turned_dot(dz_all[k, i], weights[k, :, now])
            g_all[k, i] = (grad_out_of(k, i).astype(jnp.float32) + below).astype(jnp.bfloat16)
    wait_bytes(h_all.at[0], stream_here.at[0])
    wait_bytes(tapped, tap_here)
    wait_bytes(g_all.at[layers], stream_here.at[1])
    if not last:
        grad_out[...] = g_all[section, 0]
        back_out[...] = turned_dot(dz_all[0, 0], weights[0, :, tap]).astype(jnp.bfloat16)
    if last:
        add_products(section, sums, sums_in, tapped, h_all, gated_all, dz_all, g_all, cot)
    if last:
        kept_out[...] = sums[pl.ds(pl.multiple_of(core * low_rows, low_rows), low_rows)]
        sent_rows = low_rows // len(sent_outs)
        for i, sent_out in enumerate(sent_outs):
            start = pl.multiple_of((1 - core) * low_rows + i * sent_rows, sent_rows)
            sent_out[...] = sums[pl.ds(start, sent_rows)].astype(jnp.bfloat16)


def layer_stack(streams, taps, number, weights, earlier=None):
    seqs, seq_rows, channels = streams[0].shape
    layers = number
    last = earlier is not None
    width = 6 * channels
    anywhere = pl.BlockSpec(memory_space=pl.ANY)
    near = pl.BlockSpec(memory_space=pltpu.VMEM)
    rows = lambda count, wide=1: ((count, seqs, seq_rows, wide * channels), jnp.bfloat16)
    kept = [rows(layers), rows(layers, 2), rows(layers + 1)]
    scratch = [pltpu.VMEM(*rows(layers))] if last else []
    scratch += [
        pltpu.VMEM((seqs, seq_rows, channels), jnp.bfloat16),
        pltpu.VMEM((layers, seqs, seq_rows, channels), jnp.float32),
        pltpu.VMEM((layers, seqs, seq_rows, channels), jnp.float32),
        pltpu.SemaphoreType.DMA((2,)),
        pltpu.SemaphoreType.DMA,
    ]
    operands = [*streams, *taps, *weights]
    in_specs = [near] * (3 + len(taps)) + [near if last else anywhere] * len(weights)
    if last:
        operands += [*earlier]
        in_specs += [near] * len(earlier)
        shapes = kept + [((channels // 4, width), jnp.bfloat16)] * 2 + [((channels // 2, width), jnp.float32)]
        scratch += [pltpu.VMEM((channels, width), jnp.float32)]
    else:
        shapes = [((seq_rows, channels), jnp.bfloat16)] * 3 + [((layers, channels, width), jnp.bfloat16), rows(layers)] + kept
        scratch += [pltpu.SemaphoreType.DMA((layers,))]
    flops = 2 * 22 * layers * seqs * seq_rows * channels * channels
    return pl.pallas_call(
        functools.partial(stack_kernel, layers, last),
        in_specs=in_specs,
        out_specs=[near] * len(shapes),
        out_shape=[jax.ShapeDtypeStruct(*shape) for shape in shapes],
        scratch_shapes=scratch,
        compiler_params=pltpu.CompilerParams(vmem_limit_bytes=(21 if last else 18) * 2**20),
        cost_estimate=pl.CostEstimate(flops=flops, bytes_accessed=16 * seqs * seq_rows * channels, transcendentals=0),
        name="layer_stack",
    )(*operands)


def order_kernel(*refs):
    count = (len(refs) - 1) // 3
    sources, owns, others, sems = refs[:count], refs[count : 2 * count], refs[2 * count : 3 * count], refs[-1]
    section = lax.axis_index("section")
    copies = []
    for i, source in enumerate(sources):
        for by in range(source.shape[0]):
            target = owns[i].at[0] if by == 0 else others[i].at[by - 1]
            copies.append(pltpu.make_async_copy(source.at[jnp.bitwise_xor(section, by)], target, sems.at[i, by]))
    for copy in copies:
        copy.start()
    for copy in copies:
        copy.wait()


def order_streams(*streams):
    number, seq_rows, channels = streams[0].shape
    count = len(streams)
    anywhere = pl.BlockSpec(memory_space=pl.ANY)
    near = pl.BlockSpec(memory_space=pltpu.VMEM)
    shape = lambda seqs: jax.ShapeDtypeStruct((seqs, seq_rows, channels), jnp.bfloat16)
    ordered = pl.pallas_call(
        order_kernel,
        in_specs=[anywhere] * count,
        out_specs=[near] * 2 * count,
        out_shape=[shape(1)] * count + [shape(number - 1)] * count,
        scratch_shapes=[pltpu.SemaphoreType.DMA((count, number))],
        compiler_params=pltpu.CompilerParams(vmem_limit_bytes=8 * 2**20),
        cost_estimate=pl.CostEstimate(flops=0, bytes_accessed=2**24, transcendentals=0),
        name="order_streams",
    )(*streams)
    return ordered[:count], ordered[count:]


def spread_kernel(places, kept, got_low, got_high, own_out, *outs):
    place = lax.axis_index("tm") // 2
    piece_rows = own_out.shape[0]
    for by in range(places):
        rows = pl.ds(pl.multiple_of(jnp.bitwise_xor(place, by) * piece_rows, piece_rows), piece_rows)
        here = pl.ds(pl.multiple_of(lax.rem(jnp.bitwise_xor(place, by) * piece_rows, got_low.shape[0]), piece_rows), piece_rows)
        got = jnp.where(jnp.bitwise_xor(place, by) * piece_rows < got_low.shape[0], got_low[here], got_high[here])
        total = kept[rows] + got.astype(jnp.float32)
        if by == 0:
            own_out[...] = total
        else:
            outs[by - 1][...] = total.astype(jnp.bfloat16)


def final_kernel(places, scale, *refs):
    shard = lax.axis_index("tm")
    place, core = shard // 2, lax.rem(shard, 2)
    pieces, other, outs = refs[:places], refs[places], refs[places + 1 :]
    piece_rows = pieces[0].shape[0]
    live = jnp.where(lax.axis_index("section") == 0, scale, 0.0)
    for side, values in ((core, [ref[...] for ref in pieces]), (1 - core, [other[i] for i in range(places)])):
        for by, value in enumerate(values):
            at = (side * places + jnp.bitwise_xor(place, by)) * piece_rows
            rows = pl.ds(pl.multiple_of(at, piece_rows), piece_rows)
            value = value.astype(jnp.float32)
            column = 0
            for i, out in enumerate(outs):
                width = out.shape[2]
                out[0, rows, :] = value[:, column : column + width] * (live if i == 0 else scale)
                column += width


def add_kernel(reach, own_base, base, *refs):
    *backs, out = refs
    section = lax.axis_index("section")
    own = jnp.where((section == 0) & (lax.axis_index("tm") < reach), 1.0, 0.0)
    for i, back in enumerate(backs):
        term = back[...].astype(jnp.float32)
        total = base[i - 1] + term if i else own_base[...].astype(jnp.float32) + term * own
        out[0, jnp.bitwise_xor(section, i)] = total.astype(jnp.bfloat16)


def add_back(own_base, base, backs, reach):
    shape = (1, len(backs), *own_base.shape)
    kernel = functools.partial(add_kernel, reach)
    return local_call(kernel, "add_back", [own_base, base, *backs], [jax.ShapeDtypeStruct(shape, jnp.bfloat16)], 2**24)[0]


def local_call(kernel, name, operands, out_shape, weight=0):
    near = pl.BlockSpec(memory_space=pltpu.VMEM)
    return pl.pallas_call(
        kernel,
        in_specs=[near] * len(operands),
        out_specs=[near] * len(out_shape),
        out_shape=[jax.ShapeDtypeStruct(value.shape, value.dtype) for value in out_shape],
        compiler_params=pltpu.CompilerParams(vmem_limit_bytes=12 * 2**20),
        cost_estimate=pl.CostEstimate(flops=0, bytes_accessed=weight, transcendentals=0) if weight else None,
        name=name,
    )(*operands)


def swapped(x, axis, by):
    return lax.ppermute(x, axis, [(i, i ^ by) for i in range(lax.axis_size(axis))])


def rotated(x, by):
    size = lax.axis_size("tm")
    return lax.ppermute(x, "tm", [(i, (i + by) % size) for i in range(size)])


def between(x, shards, pairs, reached):
    return lax.ppermute(x, ("section", "tm"), [(i * shards + t, j * shards + t) for i, j in pairs for t in reached])


def spread(got, kept, places):
    rows, width = kept.shape
    piece = (rows // places, width)
    narrow = jax.ShapeDtypeStruct(piece, jnp.bfloat16)
    own, *pieces = local_call(
        functools.partial(spread_kernel, places), "spread", [kept, *got],
        [jax.ShapeDtypeStruct(piece, jnp.float32)] + [narrow] * (places - 1),
    )
    return own, pieces


def sum_over_chips(own, pieces, scale, beside):
    rows, width = own.shape
    places = len(pieces) + 1
    arrived = [swapped(value, "tm", 2 * (by + 1)) for by, value in reversed(list(enumerate(pieces)))]
    total = sum([value.astype(jnp.float32) for value in arrived], own).astype(jnp.bfloat16)
    by_distance = [total] + [swapped(total, "tm", 2 * by) for by in range(1, places)]
    by_distance, beside = lax.optimization_barrier((by_distance, beside))
    other = swapped(jnp.stack(by_distance), "tm", 1)
    channels = width // 6
    out_shape = [jax.ShapeDtypeStruct((1, 2 * places * rows, cols), jnp.float32) for cols in (2 * channels, 2 * channels, channels, channels)]
    return local_call(functools.partial(final_kernel, places, scale), "place_sums", by_distance + [other], out_shape), beside


def stacked_body(signal, skip_cot, res_cot, w_tap, w_now, w_res, w_skip):
    sections = lax.axis_size("section")
    shards = lax.axis_size("tm")
    section = lax.axis_index("section")
    core = lax.axis_index("tm") % 2
    number, seq_rows, channels = signal.shape
    span = FIRST_DILATION // seq_rows

    tap = rotated(lax.dynamic_index_in_dim(signal, section, 0, False), span)
    packed = jnp.concatenate([w_now[0], w_res[0], w_skip[0], w_tap[0]], axis=1)
    half_rows = packed.shape[0] // 2
    own_half = lax.dynamic_slice_in_dim(packed, core * half_rows, half_rows, 0)
    mine = [swapped(own_half, "section", by) for by in range(1, sections)]
    own_streams, other_streams = order_streams(signal, skip_cot, res_cot)
    tap, mine, own_streams, other_streams = lax.optimization_barrier((tap, mine, own_streams, other_streams))
    other = [swapped(piece, "tm", 1) for piece in mine]
    taps = [tap] + [swapped(tap, "section", by) for by in range(1, sections)]

    pieces = [w_now, w_res, w_skip, w_tap, *mine, *other]
    own_skip, own_base, back, weights, *kept_own = layer_stack(own_streams, taps[:1], number, pieces)
    ahead_terms = ahead(taps[0], own_streams[1], kept_own, weights, other_streams)
    back = rotated(back, -span)
    gated, dz, g, *sent, kept = layer_stack(other_streams, taps[1:], number, [weights], earlier=ahead_terms)
    got = [swapped(value, "tm", 1) for value in sent]
    own_piece, pieces = spread(got, kept, shards // 2)
    pieces, back = lax.optimization_barrier((pieces, back))
    reached = range(shards - span)
    arrived = [between(back, shards, [(by, 0)], reached) for by in range(1, sections)]
    grad_scale = 1.0 / math.sqrt(number * seq_rows * shards)
    skip_total, base = finish(own_skip, gated, dz, g, weights)
    input_grads = add_back(own_base, base, [back, *arrived], shards - span)
    summed, input_grads = sum_over_chips(own_piece, pieces, grad_scale, input_grads)
    return (skip_total, input_grads, *summed)


def body(signal, skip_cot, res_cot, w_tap, w_now, w_res, w_skip):
    sections = lax.axis_size("section")
    shards = lax.axis_size("tm")
    number, seq_rows, channels = signal.shape
    span, beyond = divmod(FIRST_DILATION, seq_rows)
    one_live_tap = beyond == 0 and span < shards <= 2 * span
    square = w_res.shape[1:] == (channels, channels) and w_skip.shape[1:] == (channels, channels)
    pairs = sections == number == 4 and shards % 2 == 0 and shards & (shards - 1) == 0
    if one_live_tap and square and pairs:
        return stacked_body(signal, skip_cot, res_cot, w_tap, w_now, w_res, w_skip)
    return pipelined_body(signal, skip_cot, res_cot, w_tap, w_now, w_res, w_skip)


def solution(mesh):
    in_specs = (
        P(None, "tm", None),
        P(None, "tm", None),
        P(None, "tm", None),
        P("section", None, None),
        P("section", None, None),
        P("section", None, None),
        P("section", None, None),
    )
    out_specs = (
        P(None, "tm", None),
        P("section", None, "tm", None),
        P("section", None, None),
        P("section", None, None),
        P("section", None, None),
        P("section", None, None),
    )
    return jax.shard_map(body, mesh=mesh, in_specs=in_specs, out_specs=out_specs, check_vma=False)
```

```python
import functools
import math

import jax
import jax.numpy as jnp
from jax import lax
from jax.experimental import pallas as pl
from jax.experimental.pallas import tpu as pltpu
from jax.sharding import PartitionSpec as P

SPAN = 4
FIRST_DILATION = 2048


def passed_along(x, axis, by):
    size = lax.axis_size(axis)
    pairs = [(i, i + by) for i in range(size) if 0 <= i + by < size]
    return lax.ppermute(x, axis, pairs)


def flat_dot(left, right):
    result = jnp.dot(left.reshape(-1, left.shape[-1]), right, preferred_element_type=jnp.float32)
    return result.reshape(left.shape[:-1] + (right.shape[-1],))


def rows_spanning(left, right):
    return lax.dot_general(
        left.reshape(-1, left.shape[-1]),
        right.reshape(-1, right.shape[-1]),
        (((0,), (0,)), ((), ())),
        preferred_element_type=jnp.float32,
    )


def tap_rows(values, chosen, delayed):
    result = jnp.zeros_like(values)
    for layer_number, selected in chosen:
        if delayed:
            arrived = passed_along(values, "tm", SPAN << layer_number)
        else:
            arrived = passed_along(values, "tm", -(SPAN << layer_number))
        result = jnp.where(selected, arrived, result)
    return result


def gate_parts(tapped, layer_in, weights):
    pre = flat_dot(tapped, weights[0]) + flat_dot(layer_in, weights[1])
    half_width = pre.shape[-1] // 2
    return (jnp.tanh(pre[..., :half_width]), jax.nn.sigmoid(pre[..., half_width:]))


def layer_forward(layer_in, weights, chosen):
    tapped = tap_rows(layer_in, chosen, True)
    tanh_part, sigmoid_part = gate_parts(tapped, layer_in, weights)
    gated = (tanh_part * sigmoid_part).astype(jnp.bfloat16)
    stream_out = (layer_in.astype(jnp.float32) + flat_dot(gated, weights[2])).astype(jnp.bfloat16)
    return (tapped, stream_out, flat_dot(gated, weights[3]))


def layer_backward(layer_in, tapped, grad_out, skip_grad, weights, chosen):
    tanh_part, sigmoid_part = gate_parts(tapped, layer_in, weights)
    gated = (tanh_part * sigmoid_part).astype(jnp.bfloat16)
    grad_gated = flat_dot(grad_out, weights[2].T) + flat_dot(skip_grad, weights[3].T)
    grad_pre = jnp.concatenate(
        [
            grad_gated * sigmoid_part * (1.0 - tanh_part * tanh_part),
            grad_gated * tanh_part * sigmoid_part * (1.0 - sigmoid_part),
        ],
        axis=-1,
    ).astype(jnp.bfloat16)
    terms = (
        rows_spanning(tapped, grad_pre),
        rows_spanning(layer_in, grad_pre),
        rows_spanning(gated, grad_out),
        rows_spanning(gated, skip_grad),
    )
    back_term = flat_dot(grad_pre, weights[0].T).astype(jnp.bfloat16)
    arrived = tap_rows(back_term, chosen, False)
    grad_in = (
        grad_out.astype(jnp.float32)
        + flat_dot(grad_pre, weights[1].T)
        + arrived.astype(jnp.float32)
    )
    return (grad_in.astype(jnp.bfloat16), terms)


def keep_slot(holding_rows, micro_index, in_range, value):
    former = lax.dynamic_slice_in_dim(holding_rows, micro_index, 1, 0)
    return lax.dynamic_update_slice_in_dim(
        holding_rows, jnp.where(in_range, value, former), micro_index, 0
    )


def run_layers(signal, skip_cot, res_cot, w_tap, w_now, w_res, w_skip, section_index, sections):
    number, seq_rows, channels = signal.shape
    weights = (w_tap[0], w_now[0], w_res[0], w_skip[0])
    total_steps = number + sections - 1
    saved_in = jnp.zeros((number, seq_rows, channels), jnp.bfloat16)
    saved_tap = jnp.zeros((number, seq_rows, channels), jnp.bfloat16)
    skip_running_sum = jnp.zeros((number, seq_rows, w_skip.shape[2]), jnp.float32)
    received = jnp.zeros((1, seq_rows, channels), jnp.bfloat16)
    for moment in range(total_steps):
        chosen = [
            (layer_number, section_index == layer_number)
            for layer_number in range(sections)
            if 0 <= moment - layer_number < number
        ]
        position = moment - section_index
        in_range = (position >= 0) & (position < number)
        micro_index = jnp.clip(position, 0, number - 1)
        incoming = signal[min(moment, number - 1)][None]
        layer_in = jnp.where(section_index == 0, incoming, received)
        tapped, stream_out, skip_term = layer_forward(layer_in, weights, chosen)
        saved_in = keep_slot(saved_in, micro_index, in_range, layer_in)
        saved_tap = keep_slot(saved_tap, micro_index, in_range, tapped)
        skip_running_sum = keep_slot(skip_running_sum, micro_index, in_range, skip_term)
        if moment + 1 < total_steps:
            received = passed_along(stream_out, "section", 1)
    skip_total = lax.psum(skip_running_sum, "section").astype(jnp.bfloat16)
    partial_sums = [
        jnp.zeros(weights[0].shape, jnp.float32),
        jnp.zeros(weights[1].shape, jnp.float32),
        jnp.zeros(weights[2].shape, jnp.float32),
        jnp.zeros(weights[3].shape, jnp.float32),
    ]
    input_grads = jnp.zeros((number, seq_rows, channels), jnp.bfloat16)
    received = jnp.zeros((1, seq_rows, channels), jnp.bfloat16)
    for moment in range(total_steps):
        chosen = [
            (layer_number, section_index == layer_number)
            for layer_number in range(sections)
            if 0 <= moment - (sections - 1 - layer_number) < number
        ]
        position = moment - (sections - 1 - section_index)
        in_range = (position >= 0) & (position < number)
        micro_index = jnp.clip(position, 0, number - 1)
        top_grad = lax.dynamic_slice_in_dim(res_cot, micro_index, 1, 0)
        grad_out = jnp.where(section_index == sections - 1, top_grad, received)
        layer_in = lax.dynamic_slice_in_dim(saved_in, micro_index, 1, 0)
        tapped = lax.dynamic_slice_in_dim(saved_tap, micro_index, 1, 0)
        skip_grad = lax.dynamic_slice_in_dim(skip_cot, micro_index, 1, 0)
        grad_in, terms = layer_backward(layer_in, tapped, grad_out, skip_grad, weights, chosen)
        factor = in_range.astype(jnp.float32)
        partial_sums = [partial_sums[spot] + factor * terms[spot] for spot in range(4)]
        input_grads = keep_slot(input_grads, micro_index, in_range, grad_in)
        if moment + 1 < total_steps:
            received = passed_along(grad_in, "section", -1)
    return (skip_total, input_grads, tuple((part[None] for part in partial_sums)))


def pipelined_body(signal, skip_cot, res_cot, w_tap, w_now, w_res, w_skip):
    sections = lax.axis_size("section")
    shards = lax.axis_size("tm")
    section_index = lax.axis_index("section")
    number, seq_rows, channels = signal.shape
    skip_total, input_grads, partial_sums = run_layers(
        signal, skip_cot, res_cot, w_tap, w_now, w_res, w_skip, section_index, sections
    )
    summed = lax.psum((partial_sums[0], partial_sums[1], partial_sums[2], partial_sums[3]), "tm")
    grad_scale = 1.0 / math.sqrt(number * seq_rows * shards)
    return (
        skip_total,
        input_grads[None],
        summed[0] * grad_scale,
        summed[1] * grad_scale,
        summed[2] * grad_scale,
        summed[3] * grad_scale,
    )


def narrow_dot(left, right):
    return lax.dot_general(left, right, (((1,), (0,)), ((), ())), preferred_element_type=jnp.float32)


def rows_dot(left, right):
    return lax.dot_general(left, right, (((0,), (0,)), ((), ())), preferred_element_type=jnp.float32)


def turned_dot(left, right):
    return lax.dot_general(left, right, (((1,), (1,)), ((), ())), preferred_element_type=jnp.float32)


def skip_sum(gated, weights, columns):
    total = narrow_dot(gated[0], weights[0, :, columns])
    for k in range(1, len(gated)):
        total = total + narrow_dot(gated[k], weights[k, :, columns])
    return total.astype(jnp.bfloat16)


def finish_kernel(own_skip, gated_all, dz_all, g_all, weights, skip_out, base_out):
    section = lax.axis_index("section")
    layers, seqs, _, channels = gated_all.shape
    skip_out[section] = own_skip[...]
    above = jnp.maximum(section, 1)
    lowest = section == 0
    for i in range(seqs):
        at = jnp.bitwise_xor(section, i + 1)
        skip_out[at] = skip_sum([gated_all[k, i] for k in range(layers)], weights, slice(3 * channels, 4 * channels))
        below = turned_dot(dz_all[0, i], weights[0, :, : 2 * channels])
        base_out[i] = g_all[above, i].astype(jnp.float32) + jnp.where(lowest, below, 0.0)


def finish(own_skip, gated_all, dz_all, g_all, weights):
    layers, seqs, seq_rows, channels = gated_all.shape
    out_shape = [
        jax.ShapeDtypeStruct((layers, seq_rows, channels), jnp.bfloat16),
        jax.ShapeDtypeStruct((seqs, seq_rows, channels), jnp.float32),
    ]
    return local_call(finish_kernel, "finish", [own_skip, gated_all, dz_all, g_all, weights], out_shape)


def add_products(section, sums, sums_in, tapped, h_all, gated_all, dz_all, g_all, cot):
    channels = tapped.shape[-1]
    for i in range(tapped.shape[0]):
        products = (
            rows_dot(tapped[i], dz_all[section, i]),
            rows_dot(h_all[section, i], dz_all[section, i]),
            rows_dot(gated_all[section, i], g_all[section + 1, i]),
            rows_dot(gated_all[section, i], cot[i]),
        )
        column = 0
        for product in products:
            spot = slice(column, column + product.shape[1])
            column += product.shape[1]
            if i:
                sums[:, spot] += product
            else:
                sums[:, spot] = sums_in[:, spot] + product if sums_in is not None else product


def ahead_kernel(tapped, cot, h_all, gated_all, dz_all, g_all, weights, next_signal, next_cot, next_res, sums, ahead_pre, ahead_du):
    layers, _, _, channels = gated_all.shape
    half = channels
    early = layers - ahead_du.shape[0]
    section = lax.axis_index("section")
    add_products(section, sums, None, tapped, h_all, gated_all, dz_all, g_all, cot)
    for i in range(layers - 1):
        ahead_pre[i] = narrow_dot(next_signal[i], weights[0, :, : 2 * half])
        for k in range(early, layers):
            du = turned_dot(next_cot[i], weights[k, :, 3 * half : 4 * half])
            if k == layers - 1:
                du = du + turned_dot(next_res[i], weights[k, :, 2 * half : 3 * half])
            ahead_du[k - early, i] = du


def ahead(tap, cot, kept, weights, following):
    layers, channels, width = weights.shape
    _, seq_rows, _ = cot.shape
    shapes = [(channels, width), (layers - 1, seq_rows, 2 * channels), (4, layers - 1, seq_rows, channels)]
    out_shape = [jax.ShapeDtypeStruct(shape, jnp.float32) for shape in shapes]
    return local_call(ahead_kernel, "ahead", [tap[None], cot, *kept, weights, *following], out_shape)


def stack_kernel(layers, last, *refs):
    refs = list(refs)
    take = lambda count: [refs.pop(0) for _ in range(count)]
    signal, cot, res_cot = take(3)
    taps = take(layers - 1 if last else 1)
    if last:
        weights, sums_in, ahead_pre, ahead_du = take(4)
        gated_all, dz_all, g_all, *sent_outs, kept_out = take(6)
    else:
        own = take(4)
        mine = take(layers - 1)
        other = take(layers - 1)
        skip_out, grad_out, back_out, weights, h_all, gated_all, dz_all, g_all = take(8)
    early = layers - ahead_du.shape[0] if last else layers
    if last:
        (h_all,) = take(1)
    tapped, tanh_all, sig_all = take(3)
    stream_here, tap_here = take(2)
    if last:
        (sums,) = take(1)
    else:
        (weights_here,) = take(1)
    section = lax.axis_index("section")
    core = lax.rem(lax.axis_index("tm"), 2)
    _, seqs, seq_rows, channels = h_all.shape
    half = channels
    now = slice(0, 2 * half)
    res = slice(2 * half, 2 * half + channels)
    skip = slice(2 * half + channels, 2 * half + 2 * channels)
    tap = slice(2 * half + 2 * channels, 4 * half + 2 * channels)
    low_rows = channels // 2
    def wait_bytes(target, there):
        pltpu.make_async_copy(target, target, there).wait()

    if not last:
        for ref, cols in zip(own, (now, res, skip, tap)):
            pltpu.make_async_copy(ref.at[0], weights.at[section, :, cols], weights_here.at[section]).start()
        for by in range(1, layers):
            slot = jnp.bitwise_xor(section, by)
            for ref, side in ((mine[by - 1], core), (other[by - 1], 1 - core)):
                rows = pl.ds(pl.multiple_of(side * low_rows, low_rows), low_rows)
                pltpu.make_async_copy(ref, weights.at[slot, rows], weights_here.at[slot]).start()
    pltpu.make_async_copy(signal, h_all.at[0], stream_here.at[0]).start()
    for i, ref in enumerate(taps):
        pltpu.make_async_copy(ref, tapped.at[i], tap_here).start()
    pltpu.make_async_copy(res_cot, g_all.at[layers], stream_here.at[1]).start()

    layer_in = lambda k, i: h_all[k, i] if k else signal[i]
    grad_out_of = lambda k, i: g_all[k + 1, i] if k + 1 < layers else res_cot[i]
    for k in range(layers):
        if not last:
            wait_bytes(weights.at[k], weights_here.at[k])
        for i in range(seqs):
            if k == 0 and last:
                pre = ahead_pre[i] + narrow_dot(taps[i][...], weights[0, :, tap])
            else:
                pre = narrow_dot(layer_in(k, i), weights[k, :, now])
                if k == 0:
                    pre = pre + narrow_dot(taps[i][...], weights[0, :, tap])
            tanh_part = jnp.tanh(pre[:, :half])
            sig_part = 0.5 * jnp.tanh(0.5 * pre[:, half:]) + 0.5
            tanh_all[k, i] = tanh_part
            sig_all[k, i] = sig_part
            gated_all[k, i] = (tanh_part * sig_part).astype(jnp.bfloat16)
        if k + 1 < layers:
            for i in range(seqs):
                stream = narrow_dot(gated_all[k, i], weights[k, :, res])
                h_all[k + 1, i] = (layer_in(k, i).astype(jnp.float32) + stream).astype(jnp.bfloat16)
    if not last:
        skip_out[...] = skip_sum([gated_all[k, 0] for k in range(layers)], weights, skip)
    for k in reversed(range(layers)):
        for i in range(seqs):
            if last and k == layers - 1:
                du = ahead_du[k - early, i]
            else:
                du = turned_dot(grad_out_of(k, i), weights[k, :, res])
                if last and k >= early:
                    du = du + ahead_du[k - early, i]
                else:
                    du = du + turned_dot(cot[i], weights[k, :, skip])
            tanh_part = tanh_all[k, i]
            sig_part = sig_all[k, i]
            scaled = du * sig_part
            dz_all[k, i, :, :half] = (scaled * (1.0 - tanh_part * tanh_part)).astype(jnp.bfloat16)
            dz_all[k, i, :, half:] = (scaled * (tanh_part * (1.0 - sig_part))).astype(jnp.bfloat16)
        for i in range(seqs if k or not last else 0):
            below = turned_dot(dz_all[k, i], weights[k, :, now])
            g_all[k, i] = (grad_out_of(k, i).astype(jnp.float32) + below).astype(jnp.bfloat16)
    wait_bytes(h_all.at[0], stream_here.at[0])
    wait_bytes(tapped, tap_here)
    wait_bytes(g_all.at[layers], stream_here.at[1])
    if not last:
        grad_out[...] = g_all[section, 0]
        back_out[...] = turned_dot(dz_all[0, 0], weights[0, :, tap]).astype(jnp.bfloat16)
    if last:
        add_products(section, sums, sums_in, tapped, h_all, gated_all, dz_all, g_all, cot)
    if last:
        kept_out[...] = sums[pl.ds(pl.multiple_of(core * low_rows, low_rows), low_rows)]
        sent_rows = low_rows // len(sent_outs)
        for i, sent_out in enumerate(sent_outs):
            start = pl.multiple_of((1 - core) * low_rows + i * sent_rows, sent_rows)
            sent_out[...] = sums[pl.ds(start, sent_rows)].astype(jnp.bfloat16)


def layer_stack(streams, taps, number, weights, earlier=None):
    seqs, seq_rows, channels = streams[0].shape
    layers = number
    last = earlier is not None
    width = 6 * channels
    anywhere = pl.BlockSpec(memory_space=pl.ANY)
    near = pl.BlockSpec(memory_space=pltpu.VMEM)
    rows = lambda count, wide=1: ((count, seqs, seq_rows, wide * channels), jnp.bfloat16)
    kept = [rows(layers), rows(layers, 2), rows(layers + 1)]
    scratch = [pltpu.VMEM(*rows(layers))] if last else []
    scratch += [
        pltpu.VMEM((seqs, seq_rows, channels), jnp.bfloat16),
        pltpu.VMEM((layers, seqs, seq_rows, channels), jnp.float32),
        pltpu.VMEM((layers, seqs, seq_rows, channels), jnp.float32),
        pltpu.SemaphoreType.DMA((2,)),
        pltpu.SemaphoreType.DMA,
    ]
    operands = [*streams, *taps, *weights]
    in_specs = [near] * (3 + len(taps)) + [near if last else anywhere] * len(weights)
    if last:
        operands += [*earlier]
        in_specs += [near] * len(earlier)
        shapes = kept + [((channels // 4, width), jnp.bfloat16)] * 2 + [((channels // 2, width), jnp.float32)]
        scratch += [pltpu.VMEM((channels, width), jnp.float32)]
    else:
        shapes = [((seq_rows, channels), jnp.bfloat16)] * 3 + [((layers, channels, width), jnp.bfloat16), rows(layers)] + kept
        scratch += [pltpu.SemaphoreType.DMA((layers,))]
    flops = 2 * 22 * layers * seqs * seq_rows * channels * channels
    return pl.pallas_call(
        functools.partial(stack_kernel, layers, last),
        in_specs=in_specs,
        out_specs=[near] * len(shapes),
        out_shape=[jax.ShapeDtypeStruct(*shape) for shape in shapes],
        scratch_shapes=scratch,
        compiler_params=pltpu.CompilerParams(vmem_limit_bytes=(21 if last else 18) * 2**20),
        cost_estimate=pl.CostEstimate(flops=flops, bytes_accessed=16 * seqs * seq_rows * channels, transcendentals=0),
        name="layer_stack",
    )(*operands)


def order_kernel(*refs):
    count = (len(refs) - 1) // 3
    sources, owns, others, sems = refs[:count], refs[count : 2 * count], refs[2 * count : 3 * count], refs[-1]
    section = lax.axis_index("section")
    copies = []
    for i, source in enumerate(sources):
        for by in range(source.shape[0]):
            target = owns[i].at[0] if by == 0 else others[i].at[by - 1]
            copies.append(pltpu.make_async_copy(source.at[jnp.bitwise_xor(section, by)], target, sems.at[i, by]))
    for copy in copies:
        copy.start()
    for copy in copies:
        copy.wait()


def order_streams(*streams):
    number, seq_rows, channels = streams[0].shape
    count = len(streams)
    anywhere = pl.BlockSpec(memory_space=pl.ANY)
    near = pl.BlockSpec(memory_space=pltpu.VMEM)
    shape = lambda seqs: jax.ShapeDtypeStruct((seqs, seq_rows, channels), jnp.bfloat16)
    ordered = pl.pallas_call(
        order_kernel,
        in_specs=[anywhere] * count,
        out_specs=[near] * 2 * count,
        out_shape=[shape(1)] * count + [shape(number - 1)] * count,
        scratch_shapes=[pltpu.SemaphoreType.DMA((count, number))],
        compiler_params=pltpu.CompilerParams(vmem_limit_bytes=8 * 2**20),
        cost_estimate=pl.CostEstimate(flops=0, bytes_accessed=2**24, transcendentals=0),
        name="order_streams",
    )(*streams)
    return ordered[:count], ordered[count:]


def spread_kernel(places, kept, got_low, got_high, own_out, *outs):
    place = lax.axis_index("tm") // 2
    piece_rows = own_out.shape[0]
    for by in range(places):
        rows = pl.ds(pl.multiple_of(jnp.bitwise_xor(place, by) * piece_rows, piece_rows), piece_rows)
        here = pl.ds(pl.multiple_of(lax.rem(jnp.bitwise_xor(place, by) * piece_rows, got_low.shape[0]), piece_rows), piece_rows)
        got = jnp.where(jnp.bitwise_xor(place, by) * piece_rows < got_low.shape[0], got_low[here], got_high[here])
        total = kept[rows] + got.astype(jnp.float32)
        if by == 0:
            own_out[...] = total
        else:
            outs[by - 1][...] = total.astype(jnp.bfloat16)


def final_kernel(places, scale, *refs):
    shard = lax.axis_index("tm")
    place, core = shard // 2, lax.rem(shard, 2)
    pieces, other, outs = refs[:places], refs[places], refs[places + 1 :]
    piece_rows = pieces[0].shape[0]
    live = jnp.where(lax.axis_index("section") == 0, scale, 0.0)
    for side, values in ((core, [ref[...] for ref in pieces]), (1 - core, [other[i] for i in range(places)])):
        for by, value in enumerate(values):
            at = (side * places + jnp.bitwise_xor(place, by)) * piece_rows
            rows = pl.ds(pl.multiple_of(at, piece_rows), piece_rows)
            value = value.astype(jnp.float32)
            column = 0
            for i, out in enumerate(outs):
                width = out.shape[2]
                out[0, rows, :] = value[:, column : column + width] * (live if i == 0 else scale)
                column += width


def add_kernel(own_base, base, *refs):
    *backs, out = refs
    section = lax.axis_index("section")
    own = jnp.where(section == 0, 1.0, 0.0)
    for i, back in enumerate(backs):
        term = back[...].astype(jnp.float32)
        total = base[i - 1] + term if i else own_base[...].astype(jnp.float32) + term * own
        out[0, jnp.bitwise_xor(section, i)] = total.astype(jnp.bfloat16)


def add_back(own_base, base, backs):
    shape = (1, len(backs), *own_base.shape)
    return local_call(add_kernel, "add_back", [own_base, base, *backs], [jax.ShapeDtypeStruct(shape, jnp.bfloat16)], 2**24)[0]


def local_call(kernel, name, operands, out_shape, weight=0):
    near = pl.BlockSpec(memory_space=pltpu.VMEM)
    return pl.pallas_call(
        kernel,
        in_specs=[near] * len(operands),
        out_specs=[near] * len(out_shape),
        out_shape=[jax.ShapeDtypeStruct(value.shape, value.dtype) for value in out_shape],
        compiler_params=pltpu.CompilerParams(vmem_limit_bytes=12 * 2**20),
        cost_estimate=pl.CostEstimate(flops=0, bytes_accessed=weight, transcendentals=0) if weight else None,
        name=name,
    )(*operands)


def swapped(x, axis, by):
    return lax.ppermute(x, axis, [(i, i ^ by) for i in range(lax.axis_size(axis))])


def between(x, shards, pairs, reached):
    return lax.ppermute(x, ("section", "tm"), [(i * shards + t, j * shards + t) for i, j in pairs for t in reached])


def spread(got, kept, places):
    rows, width = kept.shape
    piece = (rows // places, width)
    narrow = jax.ShapeDtypeStruct(piece, jnp.bfloat16)
    own, *pieces = local_call(
        functools.partial(spread_kernel, places), "spread", [kept, *got],
        [jax.ShapeDtypeStruct(piece, jnp.float32)] + [narrow] * (places - 1),
    )
    return own, pieces


def sum_over_chips(own, pieces, scale, beside):
    rows, width = own.shape
    places = len(pieces) + 1
    arrived = [swapped(value, "tm", 2 * (by + 1)) for by, value in reversed(list(enumerate(pieces)))]
    total = sum([value.astype(jnp.float32) for value in arrived], own).astype(jnp.bfloat16)
    by_distance = [total] + [swapped(total, "tm", 2 * by) for by in range(1, places)]
    by_distance, beside = lax.optimization_barrier((by_distance, beside))
    other = swapped(jnp.stack(by_distance), "tm", 1)
    channels = width // 6
    out_shape = [jax.ShapeDtypeStruct((1, 2 * places * rows, cols), jnp.float32) for cols in (2 * channels, 2 * channels, channels, channels)]
    return local_call(functools.partial(final_kernel, places, scale), "place_sums", by_distance + [other], out_shape), beside


def stacked_body(signal, skip_cot, res_cot, w_tap, w_now, w_res, w_skip):
    sections = lax.axis_size("section")
    shards = lax.axis_size("tm")
    section = lax.axis_index("section")
    core = lax.axis_index("tm") % 2
    number, seq_rows, channels = signal.shape
    span = FIRST_DILATION // seq_rows

    tap = passed_along(lax.dynamic_index_in_dim(signal, section, 0, False), "tm", span)
    packed = jnp.concatenate([w_now[0], w_res[0], w_skip[0], w_tap[0]], axis=1)
    half_rows = packed.shape[0] // 2
    own_half = lax.dynamic_slice_in_dim(packed, core * half_rows, half_rows, 0)
    mine = [swapped(own_half, "section", by) for by in range(1, sections)]
    own_streams, other_streams = order_streams(signal, skip_cot, res_cot)
    tap, mine, own_streams, other_streams = lax.optimization_barrier((tap, mine, own_streams, other_streams))
    other = [swapped(piece, "tm", 1) for piece in mine]
    taps = [tap] + [swapped(tap, "section", by) for by in reversed(range(1, sections))][::-1]

    pieces = [w_now, w_res, w_skip, w_tap, *mine, *other]
    own_skip, own_base, back, weights, *kept_own = layer_stack(own_streams, taps[:1], number, pieces)
    ahead_terms = ahead(taps[0], own_streams[1], kept_own, weights, other_streams)
    back = passed_along(back, "tm", -span)
    gated, dz, g, *sent, kept = layer_stack(other_streams, taps[1:], number, [weights], earlier=ahead_terms)
    got = [swapped(value, "tm", 1) for value in sent]
    own_piece, pieces = spread(got, kept, shards // 2)
    pieces, back = lax.optimization_barrier((pieces, back))
    reached = range(shards - span)
    arrived = [between(back, shards, [(by, 0)], reached) for by in reversed(range(1, sections))][::-1]
    grad_scale = 1.0 / math.sqrt(number * seq_rows * shards)
    skip_total, base = finish(own_skip, gated, dz, g, weights)
    input_grads = add_back(own_base, base, [back, *arrived])
    summed, input_grads = sum_over_chips(own_piece, pieces, grad_scale, input_grads)
    return (skip_total, input_grads, *summed)


def body(signal, skip_cot, res_cot, w_tap, w_now, w_res, w_skip):
    sections = lax.axis_size("section")
    shards = lax.axis_size("tm")
    number, seq_rows, channels = signal.shape
    span, beyond = divmod(FIRST_DILATION, seq_rows)
    one_live_tap = beyond == 0 and span < shards <= 2 * span
    square = w_res.shape[1:] == (channels, channels) and w_skip.shape[1:] == (channels, channels)
    pairs = sections == number == 4 and shards % 2 == 0 and shards & (shards - 1) == 0
    if one_live_tap and square and pairs:
        return stacked_body(signal, skip_cot, res_cot, w_tap, w_now, w_res, w_skip)
    return pipelined_body(signal, skip_cot, res_cot, w_tap, w_now, w_res, w_skip)


def solution(mesh):
    in_specs = (
        P(None, "tm", None),
        P(None, "tm", None),
        P(None, "tm", None),
        P("section", None, None),
        P("section", None, None),
        P("section", None, None),
        P("section", None, None),
    )
    out_specs = (
        P(None, "tm", None),
        P("section", None, "tm", None),
        P("section", None, None),
        P("section", None, None),
        P("section", None, None),
        P("section", None, None),
    )
    return jax.shard_map(body, mesh=mesh, in_specs=in_specs, out_specs=out_specs, check_vma=False)
```
